256 devices in a mesh: engine: 16 (over y, x), seq: 16 (over z, core).
Axes of the slice: x: 4, y: 4, z: 8, core: 2. Of those that a mesh axis runs over, the one named last changes fastest.
Arguments:
- queries: bfloat16 [512, 4, 4096], P(('engine', 'seq')), may hold values from -16 to 16
- new_keys: bfloat16 [512, 4, 512], P(('engine', 'seq')), may hold values from -6 to 6
- new_values: bfloat16 [512, 4, 512], P(('engine', 'seq')), may hold values from -12 to 12
- suffix_keys: bfloat16 [512, 512, 512], P(('engine', 'seq')), may hold values from -6 to 6
- suffix_values: bfloat16 [512, 512, 512], P(('engine', 'seq')), may hold values from -12 to 12
- suffix_len: int32 [512], P(('engine', 'seq')), may hold values from 1 to 512, as said below
- sample_prompt: int32 [512, 1], P(('engine', 'seq')), may hold values from 0 to 15; in each aligned block of 32 rows (0 to 31, 32 to 63, ...) at most 3 rows name the same one
- prefix_keys: bfloat16 [16, 16384, 512], P('engine', 'seq'), may hold values from -6 to 6
- prefix_values: bfloat16 [16, 16384, 512], P('engine', 'seq'), may hold values from -12 to 12
Outputs:
- attended: bfloat16 [512, 4, 4096], P(('engine', 'seq'))
The draws below stay inside these ranges and needn't reach their ends.
Inputs may be any that keep to these rules, and one draw needn't show every extreme that they name: `suffix_len`: every draw has a sample whose length is 512. `sample_prompt`: within the samples of one index of engine (aligned blocks of 32 samples) no prompt is named by more than 3 samples, a bound that some block reaches.
All inputs are finite; a program needn't handle non-finite values.
Results may differ from the reference program's by a relative error of at most 0.0022.
Values may be sent and summed in bfloat16 or wider, within the bound.
No kernel may reach another device: no remote copies, remote signals or barrier semaphores. Data moves between devices by JAX's collectives and lax.ppermute only.
A program may use at most 64 MiB of HBM per device.

```python
import math
import jax
import jax.numpy as jnp
import numpy as np
from jax import lax

HQ = 32
KVH = 4
HD = 128
GROUP = 8
STEPS = 4
SAMP_DEV = 2
PRE_DEV = 1024
SUF = 512
SAMPLES = 512
PREFIX = 16384
PROMPTS = 16
CAPE = 3
N_SEQ = 16


def shaped_keys(key, shape):
    noise_part = jax.random.normal(key, shape, jnp.float32)
    return jnp.clip(noise_part, -6.0, 6.0)


def draw_queries(key, part):
    key = jax.random.fold_in(key, 7)
    shape = (SAMPLES, STEPS, HQ * HD)
    noise_part = jax.random.normal(key, shape, jnp.float32)
    values = 2.5 * noise_part
    return jnp.clip(values, -16.0, 16.0).astype(jnp.bfloat16)


def draw_new_keys(key, part):
    key = jax.random.fold_in(key, 13)
    return shaped_keys(key, (SAMPLES, STEPS, KVH * HD)).astype(jnp.bfloat16)


def draw_suffix_keys(key, part):
    key = jax.random.fold_in(key, 17)
    return shaped_keys(key, (SAMPLES, SUF, KVH * HD)).astype(jnp.bfloat16)


def draw_prefix_keys(key, part):
    key = jax.random.fold_in(key, 19)
    return shaped_keys(key, (PROMPTS, PREFIX, KVH * HD)).astype(jnp.bfloat16)


def draw_suffix_len(key, part):
    key = jax.random.fold_in(key, 23)
    lengths = jax.random.randint(key, (SAMPLES,), 1, SUF + 1)
    chosen = jax.random.randint(jax.random.fold_in(key, 1), (), 0, SAMPLES)
    return jnp.where(jnp.arange(SAMPLES) == chosen, SUF, lengths).astype(jnp.int32)


def level_of(rng, shape, cuts, low, top_value):
    loudness = 1.0
    for position, shards_of in cuts:
        heights = jax.random.uniform(jax.random.fold_in(jax.random.fold_in(rng, 6), position), (shards_of,), jnp.float32, low / len(cuts), top_value / len(cuts))
        loudness = loudness * jnp.repeat(jnp.exp(heights), shape[position] // shards_of).reshape((-1,) + (1,) * (len(shape) - 1 - position))
    return loudness


def routed_block(stream_key, own, number, rows, count, top, limit, skew):
    order = jax.random.permutation(stream_key, count)
    crowded, common = load_shares(count, rows * top, limit, skew, True), load_shares(count, rows * top, limit, skew, False)
    places = jnp.arange(count)

    def named(sizes, rotation):
        used = int((sizes > 0).sum())
        fixed = max(1, used // 4)
        passed = fixed + (places - fixed + rotation * (used - fixed)) % max(1, count - fixed)
        return jnp.zeros((count,), jnp.int32).at[order[jnp.where(places < fixed, places, passed)]].set(jnp.asarray(sizes, jnp.int32))

    sizes = jnp.where(number % 4 == 0, named(crowded, number // 4), named(common, number - number // 4 - 1))
    mixed = jax.random.permutation(jax.random.fold_in(own, 3), count)
    donor, receiver = mixed[0:count // 2 * 2:2], mixed[1:count // 2 * 2:2]
    slack = jnp.minimum(sizes[donor] - 1, limit - sizes[receiver]) // 2
    slack = jnp.where((donor == order[0]) | (receiver == order[0]) | (sizes[receiver] == 0), 0, jnp.maximum(slack, 0))
    passed = jax.random.randint(jax.random.fold_in(own, 4), (count // 2,), 0, 1 << 20) % (slack + 1)
    sizes = sizes.at[donor].add(-passed).at[receiver].add(passed)
    members = jnp.searchsorted(jnp.cumsum(sizes), jnp.arange(rows * top), side="right").astype(jnp.int32)
    listing = members.reshape(top, rows).T
    listing = listing[jax.random.permutation(jax.random.fold_in(own, 1), rows)]
    rotation = jax.random.randint(jax.random.fold_in(own, 2), (rows, 1), 0, top)
    return jnp.take_along_axis(listing, (jnp.arange(top)[None, :] + rotation) % top, axis=1)


def load_shares(count, total, reach, lean, full):
    loads = [(1 << 20) // math.isqrt(standing ** lean) + 1 for standing in range(1, count + 1)]
    largest = reach if full else min(reach, max(-(-total // count), total * loads[0] // sum(loads)))
    least = 1 if total - largest >= count - 1 else 0
    given, surplus = [largest] + [least] * (count - 1), total - largest - least * (count - 1)
    while surplus > 0:
        free = [i for i in range(1, count) if given[i] < largest] or [i for i in range(1, count) if given[i] < reach]
        mass, remaining = sum([loads[i] for i in free]), surplus
        for i in free:
            more = min(reach - given[i], max(1, remaining * loads[i] // mass), surplus)
            given[i] = given[i] + more
            surplus = surplus - more
    return np.array(given)


def scatter_about(own_key, extent, deviation, limit, split=(), kind=jnp.bfloat16):
    values = jax.random.normal(own_key, extent, jnp.float32) * deviation
    if len(split) > 0:
        values = level_of(own_key, extent, split, -0.22, 0.18) * values
    return jnp.clip(values, min=-limit, max=limit).astype(kind)


def setup_inputs(seed: int = 0) -> dict:
    key_of = jax.random.split(jax.random.key(seed), 10)
    queries = draw_queries(jax.random.fold_in(key_of[9], 71), 0)
    new_keys = draw_new_keys(jax.random.fold_in(key_of[9], 71), 0)
    new_values = scatter_about(key_of[2], (SAMPLES, STEPS, KVH * HD), 2.0, 12.0, ((0, 256),))
    suffix_keys = draw_suffix_keys(jax.random.fold_in(key_of[9], 71), 0)
    suffix_values = scatter_about(key_of[4], (SAMPLES, SUF, KVH * HD), 2.0, 12.0, ((0, 256),))
    suffix_len = draw_suffix_len(jax.random.fold_in(key_of[9], 71), 0)
    sample_prompt_keys = jax.random.split(jax.random.fold_in(key_of[6], 1), SAMPLES // (SAMP_DEV * N_SEQ))
    sample_prompt_turns = jax.random.permutation(jax.random.fold_in(key_of[6], 3), SAMPLES // (SAMP_DEV * N_SEQ))
    sample_prompt = jax.vmap(lambda own, number: routed_block(jax.random.fold_in(key_of[6], 2), own, number, SAMP_DEV * N_SEQ, PROMPTS, 1, CAPE, 2))(sample_prompt_keys, sample_prompt_turns).reshape((SAMPLES, 1))
    prefix_keys = draw_prefix_keys(jax.random.fold_in(key_of[9], 71), 0)
    prefix_values = scatter_about(key_of[8], (PROMPTS, PREFIX, KVH * HD), 2.0, 12.0, ((0, 16), (1, 16)))
    return dict(queries=queries, new_keys=new_keys, new_values=new_values, suffix_keys=suffix_keys, suffix_values=suffix_values, suffix_len=suffix_len, sample_prompt=sample_prompt, prefix_keys=prefix_keys, prefix_values=prefix_values)


def rounded(values):
    narrow = lax.optimization_barrier(values.astype(jnp.bfloat16))
    return narrow.astype(jnp.float32)


def reference(queries, new_keys, new_values, suffix_keys, suffix_values, suffix_len, sample_prompt, prefix_keys, prefix_values):
    scaling = HD ** -0.5
    prompt_ids = sample_prompt[:, 0].astype(jnp.int32)

    def single_sample(record):
        query, fresh_keys, fresh_values, cache_keys, cache_values, length, prompt = record
        query_rows = query.astype(jnp.float32).reshape(STEPS, KVH, GROUP, HD)
        prompt_keys = lax.dynamic_index_in_dim(prefix_keys, prompt, 0, keepdims=False)
        prompt_keys = prompt_keys.astype(jnp.float32).reshape(N_SEQ, PRE_DEV, KVH, HD)
        prompt_values = lax.dynamic_index_in_dim(prefix_values, prompt, 0, keepdims=False)
        prompt_values = prompt_values.astype(jnp.float32).reshape(N_SEQ, PRE_DEV, KVH, HD)
        scores = jnp.einsum("tgid,bkgd->tgibk", query_rows, prompt_keys) * scaling
        block_max = jnp.max(scores, axis=-1)
        probs = jnp.exp(scores - block_max[..., None])
        block_sum = jnp.sum(probs, axis=-1)
        block_out = jnp.einsum("tgibk,bkgd->tgibd", rounded(probs), prompt_values) / block_sum[..., None]
        block_lse = block_max + jnp.log(block_sum)
        highest = jnp.max(block_lse, axis=3)
        weight = jnp.exp(block_lse - highest[..., None])
        weight_sum = jnp.sum(weight, axis=3)
        prefix_out = jnp.sum(weight[..., None] * block_out, axis=3) / weight_sum[..., None]
        prefix_lse = highest + jnp.log(weight_sum)

        cache_k = cache_keys.astype(jnp.float32).reshape(SUF, KVH, HD)
        cache_v = cache_values.astype(jnp.float32).reshape(SUF, KVH, HD)
        fresh_k = fresh_keys.astype(jnp.float32).reshape(STEPS, KVH, HD)
        fresh_v = fresh_values.astype(jnp.float32).reshape(STEPS, KVH, HD)
        cache_scores = jnp.einsum("tgid,jgd->tgij", query_rows, cache_k) * scaling
        fresh_scores = jnp.einsum("tgid,ugd->tgiu", query_rows, fresh_k) * scaling
        live_mask = jnp.arange(SUF, dtype=jnp.int32) < length
        causal = jnp.arange(STEPS)[None, :] <= jnp.arange(STEPS)[:, None]
        cache_scores = jnp.where(live_mask, cache_scores, -jnp.inf)
        fresh_scores = jnp.where(causal[:, None, None, :], fresh_scores, -jnp.inf)
        row_max = jnp.maximum(jnp.max(cache_scores, axis=-1), jnp.max(fresh_scores, axis=-1))
        cache_probs = jnp.exp(cache_scores - row_max[..., None])
        fresh_probs = jnp.exp(fresh_scores - row_max[..., None])
        row_sum = jnp.sum(cache_probs, axis=-1) + jnp.sum(fresh_probs, axis=-1)
        suffix_out = (jnp.einsum("tgij,jgd->tgid", rounded(cache_probs), cache_v)
                      + jnp.einsum("tgiu,ugd->tgid", rounded(fresh_probs), fresh_v)) / row_sum[..., None]
        suffix_lse = row_max + jnp.log(row_sum)

        summit = jnp.maximum(prefix_lse, suffix_lse)
        prefix_weight = jnp.exp(prefix_lse - summit)
        suffix_weight = jnp.exp(suffix_lse - summit)
        combined = (prefix_weight[..., None] * prefix_out + suffix_weight[..., None] * suffix_out) / (prefix_weight + suffix_weight)[..., None]
        return combined.reshape(STEPS, HQ * HD).astype(jnp.bfloat16)

    return lax.map(single_sample, (queries, new_keys, new_values, suffix_keys, suffix_values, suffix_len, prompt_ids))
```

```python
import functools
import math

import jax
import jax.numpy as jnp
from jax import lax
from jax.experimental import pallas as pl
from jax.experimental.pallas import tpu as pltpu
from jax.sharding import PartitionSpec as P

KVH = 4
GROUP = 8
HD = 128
CAPE = 3
SCALING = HD ** (-0.5)
LOG2E = math.log2(math.e)
LN2 = math.log(2.0)
LSE_ONE = float(2**20)
VMEM = pl.BlockSpec(memory_space=pltpu.VMEM)
SMEM = pl.BlockSpec(memory_space=pltpu.SMEM)


def params(mib):
    return pltpu.CompilerParams(vmem_limit_bytes=mib * 1024 * 1024)


def shape(dims, dtype):
    return jax.ShapeDtypeStruct(dims, dtype)


def prepare_kernel(prompt_ref, queries_ref, rows_ref, payload_ref):
    samples, steps, features = queries_ref.shape
    heads = features // HD
    part = heads * steps // KVH
    extra = payload_ref.shape[1] - samples * part
    lanes = lax.broadcasted_iota(jnp.int32, (extra, HD), 1)
    note = jnp.zeros((extra, HD), jnp.int32)
    for sample in range(samples):
        note = jnp.where(lanes == sample, prompt_ref[sample], note)
    note = note.astype(jnp.float32).astype(jnp.bfloat16)
    for sample in range(samples):
        for first in range(0, heads, 4):
            tile = jnp.concatenate(
                [
                    queries_ref[sample, :, (first + i) * HD : (first + i + 1) * HD].astype(jnp.float32)
                    for i in range(4)
                ],
                axis=0,
            ).astype(jnp.bfloat16)
            row = first * steps
            rows_ref[sample, row : row + 4 * steps] = tile
            group, row = row // part, row % part
            for place in range(group, payload_ref.shape[0], KVH):
                payload_ref[place, sample * part + row : sample * part + row + 4 * steps] = tile
    for place in range(payload_ref.shape[0]):
        payload_ref[place, samples * part :] = note


def split_kernel(head_ref, k_ref, v_ref, *refs):
    outs, sems = refs[:-1], refs[-1]
    copies = []
    for place, out in enumerate(outs):
        head = jnp.bitwise_xor(head_ref[0], place)
        cols = pl.ds(pl.multiple_of(head * HD, HD), HD)
        for which, array in enumerate((k_ref, v_ref)):
            copies.append(
                pltpu.make_async_copy(array.at[0, :, cols], out.at[which], sems.at[place, which])
            )
    for copy in copies:
        copy.start()
    for copy in copies:
        copy.wait()


def pack_kernel(samples, pick_ref, received_ref, packed_ref):
    part = packed_ref.shape[1] // CAPE
    for slot in range(packed_ref.shape[0] * CAPE):
        sample = pick_ref[slot]
        packed_ref[slot // CAPE, (slot % CAPE) * part : (slot % CAPE + 1) * part] = received_ref[
            sample // samples, pl.ds(pl.multiple_of((sample % samples) * part, part), part)
        ]


def block_attention(rows, keys, values):
    raw = lax.dot_general(rows, keys, (((1,), (1,)), ((), ())), preferred_element_type=jnp.float32)
    top = jnp.max(raw, axis=1, keepdims=True)
    probs = jnp.exp2((raw - top) * (SCALING * LOG2E))
    total = jnp.sum(probs, axis=1, keepdims=True)
    acc = jnp.dot(probs.astype(jnp.bfloat16), values, preferred_element_type=jnp.float32)
    return acc, top, total


def encode(out):
    largest = jnp.max(jnp.abs(out), axis=1, keepdims=True)
    power = jnp.floor(jnp.log2(jnp.maximum(largest, 2.0**-112) * 1.0001)) + 1.0
    code = jnp.clip(jnp.round(out * jnp.exp2(15.0 - power)), -32767.0, 32767.0)
    return code.astype(jnp.int32), power.astype(jnp.int32)


def prefix_kernel(chunk, q_ref, *refs):
    blocks, reply_ref = refs[:-1], refs[-1]
    slots, per = q_ref.shape[0], q_ref.shape[1]
    rows_of = per // 2
    body = CAPE * rows_of

    def step(index, _):
        rows = q_ref[pl.ds(index * chunk, chunk)].reshape(chunk * per, HD)
        parts = [block_attention(rows, block[0], block[1]) for block in blocks]
        top = functools.reduce(jnp.maximum, [part[1] for part in parts])
        weights = [jnp.exp2((part[1] - top) * (SCALING * LOG2E)) for part in parts]
        total = functools.reduce(jnp.add, [w * part[2] for w, part in zip(weights, parts)])
        out = functools.reduce(jnp.add, [w * part[0] for w, part in zip(weights, parts)]) / total
        log = top * SCALING + jnp.log(total)
        code, power = encode(out)
        code = code.reshape(chunk, per, HD)
        packed = jnp.bitwise_or(
            jnp.left_shift(code[:, :rows_of], 16), jnp.bitwise_and(code[:, rows_of:], 0xFFFF)
        )
        row = lax.broadcasted_iota(jnp.int32, (chunk, per, HD), 1)
        lane = lax.broadcasted_iota(jnp.int32, (chunk, per, HD), 2)
        log = jnp.round(log * LSE_ONE).astype(jnp.int32).reshape(chunk, per, 1)
        note = jnp.where(lane == row, log, 0)
        note = jnp.where(lane == row + per, power.reshape(chunk, per, 1), note)
        note = jnp.sum(note, axis=1)
        for part in range(chunk // CAPE):
            dest = index * (chunk // CAPE) + part
            here = slice(part * CAPE, (part + 1) * CAPE)
            reply_ref[dest, 0:body] = packed[here].reshape(body, HD)
            reply_ref[dest, body : body + CAPE] = note[here]
        return 0

    lax.fori_loop(0, slots // chunk, step, 0)


def select_kernel(samples, slot_ref, reply_ref, chosen_ref):
    body = (chosen_ref.shape[1] - 8) // samples
    for sample in range(chosen_ref.shape[0] * samples):
        slot = slot_ref[sample]
        place, which = slot // CAPE, slot % CAPE
        start = (sample % samples) * body
        chosen_ref[sample // samples, start : start + body] = reply_ref[
            place, pl.ds(pl.multiple_of(which * body, body), body)
        ]
        note = samples * body + sample % samples
        chosen_ref[sample // samples, note : note + 1] = reply_ref[
            place, pl.ds(CAPE * body + which, 1)
        ]


def suffix_kernel(length_ref, rows_ref, fresh_k_ref, fresh_v_ref, k_ref, v_ref, out_ref, log_ref):
    samples, positions = k_ref.shape[0], k_ref.shape[1]
    fresh = fresh_k_ref.shape[1]
    per = rows_ref.shape[1] // KVH
    steps = per // GROUP
    column = lax.broadcasted_iota(jnp.int32, (per, positions), 1)
    step = lax.rem(lax.broadcasted_iota(jnp.int32, (per, fresh), 0), steps)
    causal = lax.broadcasted_iota(jnp.int32, (per, fresh), 1) <= step
    for sample in range(samples):
        live = column < length_ref[sample]
        for group in range(KVH):
            cols = slice(group * HD, (group + 1) * HD)
            rows = rows_ref[sample, group * per : (group + 1) * per]
            dims = (((1,), (1,)), ((), ()))
            cache_raw = lax.dot_general(
                rows, k_ref[sample, :, cols], dims, preferred_element_type=jnp.float32
            )
            fresh_raw = lax.dot_general(
                rows, fresh_k_ref[sample, :, cols], dims, preferred_element_type=jnp.float32
            )
            cache_raw = jnp.where(live, cache_raw, -jnp.inf)
            fresh_raw = jnp.where(causal, fresh_raw, -jnp.inf)
            top = jnp.maximum(
                jnp.max(cache_raw, axis=1, keepdims=True), jnp.max(fresh_raw, axis=1, keepdims=True)
            )
            cache_probs = jnp.exp2((cache_raw - top) * (SCALING * LOG2E))
            fresh_probs = jnp.exp2((fresh_raw - top) * (SCALING * LOG2E))
            total = jnp.sum(cache_probs, axis=1, keepdims=True) + jnp.sum(
                fresh_probs, axis=1, keepdims=True
            )
            acc = jnp.dot(
                cache_probs.astype(jnp.bfloat16),
                v_ref[sample, :, cols],
                preferred_element_type=jnp.float32,
            ) + jnp.dot(
                fresh_probs.astype(jnp.bfloat16),
                fresh_v_ref[sample, :, cols],
                preferred_element_type=jnp.float32,
            )
            here = slice(group * per, (group + 1) * per)
            out_ref[sample, here] = acc / total
            log_ref[sample, here] = jnp.broadcast_to(top * SCALING + jnp.log(total), (per, HD))


def combine_kernel(chosen_ref, suffix_out_ref, suffix_log_ref, out_ref):
    places, samples = chosen_ref.shape[0], suffix_out_ref.shape[0]
    steps = out_ref.shape[1]
    body = (chosen_ref.shape[1] - 8) // samples
    per = 2 * body
    row = lax.broadcasted_iota(jnp.int32, (per, HD), 0)
    lane = lax.broadcasted_iota(jnp.int32, (per, HD), 1)

    def turn(note, offset):
        spread = jnp.broadcast_to(note, (per, HD))
        return jnp.sum(jnp.where(lane == row + offset, spread, 0.0), axis=1, keepdims=True)

    for sample in range(samples):
        for group in range(KVH):
            logs, scales, codes = [], [], []
            for place in range(group, places, KVH):
                packed = chosen_ref[place, sample * body : (sample + 1) * body]
                high = jnp.right_shift(packed, 16)
                low = jnp.right_shift(jnp.left_shift(packed, 16), 16)
                codes.append(jnp.concatenate([high, low], axis=0).astype(jnp.float32))
                at = samples * body + sample
                note = chosen_ref[place, at : at + 1].astype(jnp.float32)
                logs.append(turn(note, 0) * (1.0 / LSE_ONE))
                scales.append(jnp.exp2(turn(note, per) - 15.0))
            peak = functools.reduce(jnp.maximum, logs)
            weights = [jnp.exp(log - peak) for log in logs]
            weight_sum = functools.reduce(jnp.add, weights)
            prefix = functools.reduce(
                jnp.add, [(w * s) * c for w, s, c in zip(weights, scales, codes)]
            )
            prefix_log = peak + jnp.log(weight_sum)
            first = group * per
            suffix_log = suffix_log_ref[sample, first : first + per][:, 0:1]
            suffix = suffix_out_ref[sample, first : first + per]
            top = jnp.maximum(prefix_log, suffix_log)
            prefix_weight = jnp.exp(prefix_log - top)
            suffix_weight = jnp.exp(suffix_log - top)
            whole = prefix_weight + suffix_weight
            result = (prefix_weight / (weight_sum * whole)) * prefix + (
                suffix_weight / whole
            ) * suffix
            for i in range(per // steps):
                head = first // steps + i
                out_ref[sample, :, head * HD : (head + 1) * HD] = result[
                    i * steps : (i + 1) * steps
                ].astype(jnp.bfloat16)


def local(
    queries,
    new_keys,
    new_values,
    suffix_keys,
    suffix_values,
    suffix_len,
    sample_prompt,
    prefix_keys,
    prefix_values,
):
    samples, steps, features = queries.shape
    heads = features // HD
    per = GROUP * steps
    seq_count = lax.axis_size("seq")
    engine_count = lax.axis_size("engine")
    positions = prefix_keys.shape[1]

    head_id = lax.rem(lax.axis_index("seq"), KVH).reshape(1)
    heads_of_block = pl.pallas_call(
        split_kernel,
        out_shape=[shape((2, positions, HD), jnp.bfloat16)] * KVH,
        in_specs=[SMEM] + [pl.BlockSpec(memory_space=pl.ANY)] * 2,
        out_specs=[VMEM] * KVH,
        scratch_shapes=[pltpu.SemaphoreType.DMA((KVH, 2))],
        name="split",
    )(head_id, prefix_keys, prefix_values)

    def swap(array, near, swapped):
        pairs = []
        for place in range(seq_count):
            chip, core = place // 2, place % 2
            chip = (chip + near * (2 * core - 1)) % (seq_count // 2)
            pairs.append((place, 2 * chip + (1 - core if swapped else core)))
        return lax.ppermute(array, "seq", pairs)

    blocks = [
        heads_of_block[0],
        swap(heads_of_block[1], 0, True),
        swap(heads_of_block[2], 1, False),
        swap(heads_of_block[3], 1, True),
    ]

    rows, payload = pl.pallas_call(
        prepare_kernel,
        out_shape=(
            shape((samples, heads * steps, HD), jnp.bfloat16),
            shape((seq_count, samples * per + 8, HD), jnp.bfloat16),
        ),
        in_specs=[SMEM, VMEM],
        out_specs=(VMEM, VMEM),
        name="prepare",
    )(sample_prompt.reshape(samples), queries)
    received = lax.all_to_all(payload, "seq", split_axis=0, concat_axis=0, tiled=True)

    ids = received[:, samples * per, 0:samples].astype(jnp.int32).reshape(seq_count * samples)
    order = jnp.arange(seq_count * samples, dtype=jnp.int32)
    same = (ids[:, None] == ids[None, :]) & (order[None, :] < order[:, None])
    slot = ids * CAPE + jnp.sum(same.astype(jnp.int32), axis=1)
    places = jnp.arange(engine_count * CAPE, dtype=jnp.int32)
    pick = jnp.sum(jnp.where(slot[None, :] == places[:, None], order[None, :], 0), axis=1)

    packed = pl.pallas_call(
        functools.partial(pack_kernel, samples),
        out_shape=shape((engine_count, CAPE * per, HD), jnp.bfloat16),
        in_specs=[SMEM, VMEM],
        out_specs=VMEM,
        name="pack",
    )(pick, received)
    dispatched = lax.all_to_all(packed, "engine", split_axis=0, concat_axis=0, tiled=True)

    fresh_pad = ((0, 0), (0, 16 - steps), (0, 0))
    suffix_out, suffix_log = pl.pallas_call(
        suffix_kernel,
        out_shape=(
            shape((samples, heads * steps, HD), jnp.float32),
            shape((samples, heads * steps, HD), jnp.float32),
        ),
        in_specs=[SMEM] + [VMEM] * 5,
        out_specs=(VMEM, VMEM),
        compiler_params=params(24),
        name="suffix",
    )(
        suffix_len,
        rows,
        jnp.pad(new_keys, fresh_pad),
        jnp.pad(new_values, fresh_pad),
        suffix_keys,
        suffix_values,
    )

    reply = pl.pallas_call(
        functools.partial(prefix_kernel, 4 * CAPE),
        out_shape=shape((engine_count, CAPE * per // 2 + 8, HD), jnp.int32),
        in_specs=[VMEM] * (1 + KVH),
        out_specs=VMEM,
        compiler_params=params(48),
        name="prefix",
    )(dispatched.reshape(engine_count * CAPE, per, HD), *blocks)
    returned = lax.all_to_all(reply, "engine", split_axis=0, concat_axis=0, tiled=True)

    chosen = pl.pallas_call(
        functools.partial(select_kernel, samples),
        out_shape=shape((seq_count, samples * per // 2 + 8, HD), jnp.int32),
        in_specs=[SMEM, VMEM],
        out_specs=VMEM,
        name="select",
    )(slot, returned)
    gathered = lax.all_to_all(chosen, "seq", split_axis=0, concat_axis=0, tiled=True)

    return pl.pallas_call(
        combine_kernel,
        out_shape=shape((samples, steps, features), jnp.bfloat16),
        in_specs=[VMEM] * 3,
        out_specs=VMEM,
        compiler_params=params(24),
        name="combine",
    )(gathered, suffix_out, suffix_log)


def solution(mesh):
    return jax.shard_map(
        local,
        mesh=mesh,
        in_specs=(
            P(("engine", "seq"), None, None),
            P(("engine", "seq"), None, None),
            P(("engine", "seq"), None, None),
            P(("engine", "seq"), None, None),
            P(("engine", "seq"), None, None),
            P(("engine", "seq")),
            P(("engine", "seq"), None),
            P("engine", "seq", None),
            P("engine", "seq", None),
        ),
        out_specs=P(("engine", "seq"), None, None),
        check_vma=False,
    )
```

```python
import functools
import math

import jax
import jax.numpy as jnp
from jax import lax
from jax.experimental import pallas as pl
from jax.experimental.pallas import tpu as pltpu
from jax.sharding import PartitionSpec as P

KVH = 4
GROUP = 8
HD = 128
CAPE = 3
SCALING = HD ** (-0.5)
LOG2E = math.log2(math.e)
LN2 = math.log(2.0)
LSE_ONE = float(2**20)
VMEM = pl.BlockSpec(memory_space=pltpu.VMEM)
SMEM = pl.BlockSpec(memory_space=pltpu.SMEM)


def params(mib):
    return pltpu.CompilerParams(vmem_limit_bytes=mib * 1024 * 1024)


def shape(dims, dtype):
    return jax.ShapeDtypeStruct(dims, dtype)


def prepare_kernel(prompt_ref, queries_ref, rows_ref, payload_ref):
    samples, steps, features = queries_ref.shape
    heads = features // HD
    part = heads * steps // KVH
    extra = payload_ref.shape[1] - samples * part
    lanes = lax.broadcasted_iota(jnp.int32, (extra, HD), 1)
    note = jnp.zeros((extra, HD), jnp.int32)
    for sample in range(samples):
        note = jnp.where(lanes == sample, prompt_ref[sample], note)
    note = note.astype(jnp.float32).astype(jnp.bfloat16)
    for sample in range(samples):
        for first in range(0, heads, 4):
            tile = jnp.concatenate(
                [
                    queries_ref[sample, :, (first + i) * HD : (first + i + 1) * HD].astype(jnp.float32)
                    for i in range(4)
                ],
                axis=0,
            ).astype(jnp.bfloat16)
            row = first * steps
            rows_ref[sample, row : row + 4 * steps] = tile
            group, row = row // part, row % part
            for place in range(group, payload_ref.shape[0], KVH):
                payload_ref[place, sample * part + row : sample * part + row + 4 * steps] = tile
    for place in range(payload_ref.shape[0]):
        payload_ref[place, samples * part :] = note


def split_kernel(head_ref, k_ref, v_ref, *refs):
    outs, sems = refs[:-1], refs[-1]
    copies = []
    for place, out in enumerate(outs):
        head = jnp.bitwise_xor(head_ref[0], place)
        cols = pl.ds(pl.multiple_of(head * HD, HD), HD)
        for which, array in enumerate((k_ref, v_ref)):
            copies.append(
                pltpu.make_async_copy(array.at[0, :, cols], out.at[which], sems.at[place, which])
            )
    for copy in copies:
        copy.start()
    for copy in copies:
        copy.wait()


def pack_kernel(samples, received_ref, packed_ref, slots_ref, counts_ref):
    prompts, part = packed_ref.shape[0], packed_ref.shape[1] // CAPE
    packed_ref[...] = jnp.zeros(packed_ref.shape, packed_ref.dtype)
    for prompt in range(prompts):
        counts_ref[prompt] = 0
    for place in range(received_ref.shape[0]):
        note = received_ref[place, samples * part :].astype(jnp.float32).astype(jnp.int32)
        for sample in range(samples):
            prompt = note[0, sample]
            rank = counts_ref[prompt]
            counts_ref[prompt] = rank + 1
            slots_ref[place * samples + sample] = prompt * 4 + rank
            packed_ref[prompt, pl.ds(pl.multiple_of(rank * part, part), part)] = received_ref[
                place, sample * part : (sample + 1) * part
            ]


def block_scores(rows, keys):
    return lax.dot_general(rows, keys, (((1,), (1,)), ((), ())), preferred_element_type=jnp.float32)


def block_attention(raw, values):
    top = jnp.max(raw, axis=1, keepdims=True)
    probs = jnp.exp2((raw - top) * (SCALING * LOG2E))
    total = jnp.sum(probs, axis=1, keepdims=True)
    acc = jnp.dot(probs.astype(jnp.bfloat16), values, preferred_element_type=jnp.float32)
    return acc, top, total


def encode(out):
    largest = jnp.max(jnp.abs(out), axis=1, keepdims=True)
    power = jnp.floor(jnp.log2(jnp.maximum(largest, 2.0**-112) * 1.0001)) + 1.0
    code = jnp.clip(jnp.round(out * jnp.exp2(15.0 - power)), -32767.0, 32767.0)
    return code.astype(jnp.int32), power.astype(jnp.int32)


def prefix_kernel(chunk, q_ref, *refs):
    blocks, reply_ref = refs[:-1], refs[-1]
    slots, per = q_ref.shape[0], q_ref.shape[1]
    rows_of = per // 2
    body = CAPE * rows_of

    def step(index, _):
        rows = q_ref[pl.ds(index * chunk, chunk)].reshape(chunk * per, HD)
        parts, raw = [], block_scores(rows, blocks[0][0])
        for place, block in enumerate(blocks):
            ready = raw
            if place + 1 < len(blocks):
                raw = block_scores(rows, blocks[place + 1][0])
            parts.append(block_attention(ready, block[1]))
        top = functools.reduce(jnp.maximum, [part[1] for part in parts])
        weights = [jnp.exp2((part[1] - top) * (SCALING * LOG2E)) for part in parts]
        total = functools.reduce(jnp.add, [w * part[2] for w, part in zip(weights, parts)])
        share = 1.0 / total
        out = functools.reduce(jnp.add, [(w * share) * part[0] for w, part in zip(weights, parts)])
        log = top * SCALING + jnp.log(total)
        code, power = encode(out)
        code = code.reshape(chunk, per, HD)
        packed = jnp.bitwise_or(
            jnp.left_shift(code[:, :rows_of], 16), jnp.bitwise_and(code[:, rows_of:], 0xFFFF)
        )
        row = lax.broadcasted_iota(jnp.int32, (chunk, per, HD), 1)
        lane = lax.broadcasted_iota(jnp.int32, (chunk, per, HD), 2)
        log = jnp.round(log * LSE_ONE).astype(jnp.int32).reshape(chunk, per, 1)
        note = jnp.where(lane == row, log, 0)
        note = jnp.where(lane == row + per, power.reshape(chunk, per, 1), note)
        note = jnp.sum(note, axis=1)
        for part in range(chunk // CAPE):
            dest = index * (chunk // CAPE) + part
            here = slice(part * CAPE, (part + 1) * CAPE)
            reply_ref[dest, 0:body] = packed[here].reshape(body, HD)
            reply_ref[dest, body : body + CAPE] = note[here]
        return 0

    lax.fori_loop(0, slots // chunk, step, 0)


def select_kernel(samples, slots_ref, reply_ref, chosen_ref):
    body = (chosen_ref.shape[1] - 8) // samples
    for sample in range(chosen_ref.shape[0] * samples):
        slot = slots_ref[sample]
        prompt, rank = lax.shift_right_logical(slot, 2), lax.bitwise_and(slot, 3)
        place, start = sample // samples, (sample % samples) * body
        chosen_ref[place, start : start + body] = reply_ref[
            prompt, pl.ds(pl.multiple_of(rank * body, body), body)
        ]
        note = samples * body + sample % samples
        chosen_ref[place, note : note + 1] = reply_ref[prompt, pl.ds(CAPE * body + rank, 1)]


def suffix_kernel(length_ref, rows_ref, fresh_k_ref, fresh_v_ref, k_ref, v_ref, out_ref, log_ref):
    samples, positions = k_ref.shape[0], k_ref.shape[1]
    fresh = fresh_k_ref.shape[1]
    per = rows_ref.shape[1] // KVH
    steps = per // GROUP
    column = lax.broadcasted_iota(jnp.int32, (per, positions), 1)
    step = lax.rem(lax.broadcasted_iota(jnp.int32, (per, fresh), 0), steps)
    causal = lax.broadcasted_iota(jnp.int32, (per, fresh), 1) <= step
    for sample in range(samples):
        live = column < length_ref[sample]
        for group in range(KVH):
            cols = slice(group * HD, (group + 1) * HD)
            rows = rows_ref[sample, group * per : (group + 1) * per]
            dims = (((1,), (1,)), ((), ()))
            cache_raw = lax.dot_general(
                rows, k_ref[sample, :, cols], dims, preferred_element_type=jnp.float32
            )
            fresh_raw = lax.dot_general(
                rows, fresh_k_ref[sample, :, cols], dims, preferred_element_type=jnp.float32
            )
            cache_raw = jnp.where(live, cache_raw, -jnp.inf)
            fresh_raw = jnp.where(causal, fresh_raw, -jnp.inf)
            top = jnp.maximum(
                jnp.max(cache_raw, axis=1, keepdims=True), jnp.max(fresh_raw, axis=1, keepdims=True)
            )
            cache_probs = jnp.exp2((cache_raw - top) * (SCALING * LOG2E))
            fresh_probs = jnp.exp2((fresh_raw - top) * (SCALING * LOG2E))
            total = jnp.sum(cache_probs, axis=1, keepdims=True) + jnp.sum(
                fresh_probs, axis=1, keepdims=True
            )
            acc = jnp.dot(
                cache_probs.astype(jnp.bfloat16),
                v_ref[sample, :, cols],
                preferred_element_type=jnp.float32,
            ) + jnp.dot(
                fresh_probs.astype(jnp.bfloat16),
                fresh_v_ref[sample, :, cols],
                preferred_element_type=jnp.float32,
            )
            here = slice(group * per, (group + 1) * per)
            out_ref[sample, here] = acc / total
            log_ref[sample, here] = jnp.broadcast_to(top * SCALING + jnp.log(total), (per, HD))


def combine_kernel(chosen_ref, suffix_out_ref, suffix_log_ref, out_ref):
    places, samples = chosen_ref.shape[0], suffix_out_ref.shape[0]
    steps = out_ref.shape[1]
    body = (chosen_ref.shape[1] - 8) // samples
    per = 2 * body
    row = lax.broadcasted_iota(jnp.int32, (per, HD), 0)
    lane = lax.broadcasted_iota(jnp.int32, (per, HD), 1)

    def turn(note, offset):
        spread = jnp.broadcast_to(note, (per, HD))
        return jnp.sum(jnp.where(lane == row + offset, spread, 0.0), axis=1, keepdims=True)

    for sample in range(samples):
        for group in range(KVH):
            logs, scales, codes = [], [], []
            for place in range(group, places, KVH):
                packed = chosen_ref[place, sample * body : (sample + 1) * body]
                high = jnp.right_shift(packed, 16)
                low = jnp.right_shift(jnp.left_shift(packed, 16), 16)
                codes.append(jnp.concatenate([high, low], axis=0).astype(jnp.float32))
                at = samples * body + sample
                note = chosen_ref[place, at : at + 1].astype(jnp.float32)
                logs.append(turn(note, 0) * (1.0 / LSE_ONE))
                scales.append(jnp.exp2(turn(note, per) - 15.0))
            peak = functools.reduce(jnp.maximum, logs)
            weights = [jnp.exp(log - peak) for log in logs]
            weight_sum = functools.reduce(jnp.add, weights)
            prefix = functools.reduce(
                jnp.add, [(w * s) * c for w, s, c in zip(weights, scales, codes)]
            )
            prefix_log = peak + jnp.log(weight_sum)
            first = group * per
            suffix_log = suffix_log_ref[sample, first : first + per][:, 0:1]
            suffix = suffix_out_ref[sample, first : first + per]
            top = jnp.maximum(prefix_log, suffix_log)
            prefix_weight = jnp.exp(prefix_log - top)
            suffix_weight = jnp.exp(suffix_log - top)
            whole = prefix_weight + suffix_weight
            result = (prefix_weight / (weight_sum * whole)) * prefix + (
                suffix_weight / whole
            ) * suffix
            for i in range(per // steps):
                head = first // steps + i
                out_ref[sample, :, head * HD : (head + 1) * HD] = result[
                    i * steps : (i + 1) * steps
                ].astype(jnp.bfloat16)


def local(
    queries,
    new_keys,
    new_values,
    suffix_keys,
    suffix_values,
    suffix_len,
    sample_prompt,
    prefix_keys,
    prefix_values,
):
    samples, steps, features = queries.shape
    heads = features // HD
    per = GROUP * steps
    seq_count = lax.axis_size("seq")
    engine_count = lax.axis_size("engine")
    positions = prefix_keys.shape[1]

    head_id = lax.rem(lax.axis_index("seq"), KVH).reshape(1)
    heads_of_block = pl.pallas_call(
        split_kernel,
        out_shape=[shape((2, positions, HD), jnp.bfloat16)] * KVH,
        in_specs=[SMEM] + [pl.BlockSpec(memory_space=pltpu.HBM)] * 2,
        out_specs=[VMEM] * KVH,
        scratch_shapes=[pltpu.SemaphoreType.DMA((KVH, 2))],
        compiler_params=params(4),
        name="split",
    )(head_id, prefix_keys, prefix_values)

    def swap(array, near, swapped):
        pairs = []
        for place in range(seq_count):
            chip, core = place // 2, place % 2
            chip = (chip + near * (2 * core - 1)) % (seq_count // 2)
            pairs.append((place, 2 * chip + (1 - core if swapped else core)))
        return lax.ppermute(array, "seq", pairs)

    blocks = [
        heads_of_block[0],
        swap(heads_of_block[1], 0, True),
        swap(heads_of_block[2], 1, False),
        swap(heads_of_block[3], 1, True),
    ]

    rows, payload = pl.pallas_call(
        prepare_kernel,
        out_shape=(
            shape((samples, heads * steps, HD), jnp.bfloat16),
            shape((seq_count, samples * per + 8, HD), jnp.bfloat16),
        ),
        in_specs=[SMEM, VMEM],
        out_specs=(VMEM, VMEM),
        name="prepare",
    )(sample_prompt.reshape(samples), queries)
    received = lax.all_to_all(payload, "seq", split_axis=0, concat_axis=0, tiled=True)

    fresh_pad = ((0, 0), (0, 16 - steps), (0, 0))
    suffix_out, suffix_log = pl.pallas_call(
        suffix_kernel,
        out_shape=(
            shape((samples, heads * steps, HD), jnp.float32),
            shape((samples, heads * steps, HD), jnp.float32),
        ),
        in_specs=[SMEM] + [VMEM] * 5,
        out_specs=(VMEM, VMEM),
        compiler_params=params(12),
        name="suffix",
    )(
        suffix_len,
        rows,
        jnp.pad(new_keys, fresh_pad),
        jnp.pad(new_values, fresh_pad),
        suffix_keys,
        suffix_values,
    )

    received, suffix_out, suffix_log = lax.optimization_barrier(
        (received, suffix_out, suffix_log)
    )

    packed, slots = pl.pallas_call(
        functools.partial(pack_kernel, samples),
        out_shape=(
            shape((engine_count, CAPE * per, HD), jnp.bfloat16),
            shape((seq_count * samples,), jnp.int32),
        ),
        in_specs=[VMEM],
        out_specs=(VMEM, SMEM),
        scratch_shapes=[pltpu.SMEM((engine_count,), jnp.int32)],
        compiler_params=params(4),
        name="pack",
    )(received)
    dispatched = lax.all_to_all(packed, "engine", split_axis=0, concat_axis=0, tiled=True)

    reply = pl.pallas_call(
        functools.partial(prefix_kernel, 8 * CAPE),
        out_shape=shape((engine_count, CAPE * per // 2 + 8, HD), jnp.int32),
        in_specs=[VMEM] * (1 + KVH),
        out_specs=VMEM,
        compiler_params=params(32),
        name="prefix",
    )(dispatched.reshape(engine_count * CAPE, per, HD), *blocks)
    returned = lax.all_to_all(reply, "engine", split_axis=0, concat_axis=0, tiled=True)

    chosen = pl.pallas_call(
        functools.partial(select_kernel, samples),
        out_shape=shape((seq_count, samples * per // 2 + 8, HD), jnp.int32),
        in_specs=[SMEM, VMEM],
        out_specs=VMEM,
        compiler_params=params(4),
        name="select",
    )(slots, returned)
    gathered = lax.all_to_all(chosen, "seq", split_axis=0, concat_axis=0, tiled=True)

    return pl.pallas_call(
        combine_kernel,
        out_shape=shape((samples, steps, features), jnp.bfloat16),
        in_specs=[VMEM] * 3,
        out_specs=VMEM,
        compiler_params=params(6),
        name="combine",
    )(gathered, suffix_out, suffix_log)


def solution(mesh):
    return jax.shard_map(
        local,
        mesh=mesh,
        in_specs=(
            P(("engine", "seq"), None, None),
            P(("engine", "seq"), None, None),
            P(("engine", "seq"), None, None),
            P(("engine", "seq"), None, None),
            P(("engine", "seq"), None, None),
            P(("engine", "seq")),
            P(("engine", "seq"), None),
            P("engine", "seq", None),
            P("engine", "seq", None),
        ),
        out_specs=P(("engine", "seq"), None, None),
        check_vma=False,
    )
```

```python
import functools
import math

import jax
import jax.numpy as jnp
from jax import lax
from jax.experimental import pallas as pl
from jax.experimental.pallas import tpu as pltpu
from jax.sharding import PartitionSpec as P

KVH = 4
GROUP = 8
HD = 128
CAPE = 3
SCALING = HD ** (-0.5)
LOG2E = math.log2(math.e)
LN2 = math.log(2.0)
LSE_ONE = float(2**20)
VMEM = pl.BlockSpec(memory_space=pltpu.VMEM)
SMEM = pl.BlockSpec(memory_space=pltpu.SMEM)


def params(mib):
    return pltpu.CompilerParams(vmem_limit_bytes=mib * 1024 * 1024)


def shape(dims, dtype):
    return jax.ShapeDtypeStruct(dims, dtype)


def prepare_kernel(prompt_ref, queries_ref, rows_ref, payload_ref):
    samples, steps, features = queries_ref.shape
    heads = features // HD
    part = heads * steps // KVH
    extra = payload_ref.shape[1] - samples * part
    lanes = lax.broadcasted_iota(jnp.int32, (extra, HD), 1)
    note = jnp.zeros((extra, HD), jnp.int32)
    for sample in range(samples):
        note = jnp.where(lanes == sample, prompt_ref[sample], note)
    note = note.astype(jnp.float32).astype(jnp.bfloat16)
    for sample in range(samples):
        for first in range(0, heads, 4):
            tile = jnp.concatenate(
                [
                    queries_ref[sample, :, (first + i) * HD : (first + i + 1) * HD].astype(jnp.float32)
                    for i in range(4)
                ],
                axis=0,
            ).astype(jnp.bfloat16)
            row = first * steps
            rows_ref[sample, row : row + 4 * steps] = tile
            group, row = row // part, row % part
            for place in range(group, payload_ref.shape[0], KVH):
                payload_ref[place, sample * part + row : sample * part + row + 4 * steps] = tile
    for place in range(payload_ref.shape[0]):
        payload_ref[place, samples * part :] = note


def split_kernel(head_ref, k_ref, v_ref, *refs):
    outs, sems = refs[:-1], refs[-1]
    copies = []
    for place, out in enumerate(outs):
        head = jnp.bitwise_xor(head_ref[0], place)
        cols = pl.ds(pl.multiple_of(head * HD, HD), HD)
        for which, array in enumerate((k_ref, v_ref)):
            copies.append(
                pltpu.make_async_copy(array.at[0, :, cols], out.at[which], sems.at[place, which])
            )
    for copy in copies:
        copy.start()
    for copy in copies:
        copy.wait()


def pack_kernel(samples, received_ref, packed_ref, slots_ref, counts_ref):
    prompts, part = packed_ref.shape[0], packed_ref.shape[1] // CAPE
    packed_ref[...] = jnp.zeros(packed_ref.shape, packed_ref.dtype)
    for prompt in range(prompts):
        counts_ref[prompt] = 0
    for place in range(received_ref.shape[0]):
        note = received_ref[place, samples * part :].astype(jnp.float32).astype(jnp.int32)
        for sample in range(samples):
            prompt = note[0, sample]
            rank = counts_ref[prompt]
            counts_ref[prompt] = rank + 1
            slots_ref[place * samples + sample] = prompt * 4 + rank
            packed_ref[prompt, pl.ds(pl.multiple_of(rank * part, part), part)] = received_ref[
                place, sample * part : (sample + 1) * part
            ]


def block_scores(rows, keys):
    return lax.dot_general(rows, keys, (((1,), (1,)), ((), ())), preferred_element_type=jnp.float32)


def block_attention(raw, values):
    top = jnp.max(raw, axis=1, keepdims=True)
    probs = jnp.exp2(raw * (SCALING * LOG2E) - top * (SCALING * LOG2E))
    total = jnp.sum(probs, axis=1, keepdims=True)
    acc = jnp.dot(probs.astype(jnp.bfloat16), values, preferred_element_type=jnp.float32)
    return acc, top, total


def encode(out):
    largest = jnp.max(jnp.abs(out), axis=1, keepdims=True)
    power = jnp.floor(jnp.log2(jnp.maximum(largest, 2.0**-112) * 1.0001)) + 1.0
    code = jnp.clip(jnp.round(out * jnp.exp2(15.0 - power)), -32767.0, 32767.0)
    return code.astype(jnp.int32), power.astype(jnp.int32)


def prefix_kernel(chunk, q_ref, *refs):
    blocks, reply_ref = refs[:-1], refs[-1]
    slots, per = q_ref.shape[0], q_ref.shape[1]
    rows_of = per // 2
    body = CAPE * rows_of

    def step(index, _):
        rows = q_ref[pl.ds(index * chunk, chunk)].reshape(chunk * per, HD)
        parts, raw = [], block_scores(rows, blocks[0][0])
        for place, block in enumerate(blocks):
            ready = raw
            if place + 1 < len(blocks):
                raw = block_scores(rows, blocks[place + 1][0])
            parts.append(block_attention(ready, block[1]))
        top = functools.reduce(jnp.maximum, [part[1] for part in parts])
        weights = [jnp.exp2((part[1] - top) * (SCALING * LOG2E)) for part in parts]
        total = functools.reduce(jnp.add, [w * part[2] for w, part in zip(weights, parts)])
        share = 1.0 / total
        out = functools.reduce(jnp.add, [(w * share) * part[0] for w, part in zip(weights, parts)])
        log = top * SCALING + jnp.log(total)
        code, power = encode(out)
        code = code.reshape(chunk, per, HD)
        packed = jnp.bitwise_or(
            jnp.left_shift(code[:, :rows_of], 16), jnp.bitwise_and(code[:, rows_of:], 0xFFFF)
        )
        row = lax.broadcasted_iota(jnp.int32, (chunk, per, HD), 1)
        lane = lax.broadcasted_iota(jnp.int32, (chunk, per, HD), 2)
        log = jnp.round(log * LSE_ONE).astype(jnp.int32).reshape(chunk, per, 1)
        note = jnp.where(lane == row, log, 0)
        note = jnp.where(lane == row + per, power.reshape(chunk, per, 1), note)
        note = jnp.sum(note, axis=1)
        for part in range(chunk // CAPE):
            dest = index * (chunk // CAPE) + part
            here = slice(part * CAPE, (part + 1) * CAPE)
            reply_ref[dest, 0:body] = packed[here].reshape(body, HD)
            reply_ref[dest, body : body + CAPE] = note[here]
        return 0

    lax.fori_loop(0, slots // chunk, step, 0)


def select_kernel(samples, slots_ref, reply_ref, chosen_ref):
    body = (chosen_ref.shape[1] - 8) // samples
    for sample in range(chosen_ref.shape[0] * samples):
        slot = slots_ref[sample]
        prompt, rank = lax.shift_right_logical(slot, 2), lax.bitwise_and(slot, 3)
        place, start = sample // samples, (sample % samples) * body
        chosen_ref[place, start : start + body] = reply_ref[
            prompt, pl.ds(pl.multiple_of(rank * body, body), body)
        ]
        note = samples * body + sample % samples
        chosen_ref[place, note : note + 1] = reply_ref[prompt, pl.ds(CAPE * body + rank, 1)]


def suffix_kernel(length_ref, rows_ref, fresh_k_ref, fresh_v_ref, k_ref, v_ref, out_ref, log_ref):
    samples, positions = k_ref.shape[0], k_ref.shape[1]
    fresh = fresh_k_ref.shape[1]
    per = rows_ref.shape[1] // KVH
    steps = per // GROUP
    column = lax.broadcasted_iota(jnp.int32, (per, positions), 1)
    step = lax.rem(lax.broadcasted_iota(jnp.int32, (per, fresh), 0), steps)
    causal = lax.broadcasted_iota(jnp.int32, (per, fresh), 1) <= step
    for sample in range(samples):
        live = column < length_ref[sample]
        for group in range(KVH):
            cols = slice(group * HD, (group + 1) * HD)
            rows = rows_ref[sample, group * per : (group + 1) * per]
            dims = (((1,), (1,)), ((), ()))
            cache_raw = lax.dot_general(
                rows, k_ref[sample, :, cols], dims, preferred_element_type=jnp.float32
            )
            fresh_raw = lax.dot_general(
                rows, fresh_k_ref[sample, :, cols], dims, preferred_element_type=jnp.float32
            )
            cache_raw = jnp.where(live, cache_raw, -jnp.inf)
            fresh_raw = jnp.where(causal, fresh_raw, -jnp.inf)
            top = jnp.maximum(
                jnp.max(cache_raw, axis=1, keepdims=True), jnp.max(fresh_raw, axis=1, keepdims=True)
            )
            cache_probs = jnp.exp2((cache_raw - top) * (SCALING * LOG2E))
            fresh_probs = jnp.exp2((fresh_raw - top) * (SCALING * LOG2E))
            total = jnp.sum(cache_probs, axis=1, keepdims=True) + jnp.sum(
                fresh_probs, axis=1, keepdims=True
            )
            acc = jnp.dot(
                cache_probs.astype(jnp.bfloat16),
                v_ref[sample, :, cols],
                preferred_element_type=jnp.float32,
            ) + jnp.dot(
                fresh_probs.astype(jnp.bfloat16),
                fresh_v_ref[sample, :, cols],
                preferred_element_type=jnp.float32,
            )
            here = slice(group * per, (group + 1) * per)
            out_ref[sample, here] = acc / total
            log_ref[sample, here] = jnp.broadcast_to(top * SCALING + jnp.log(total), (per, HD))


def combine_kernel(chosen_ref, suffix_out_ref, suffix_log_ref, out_ref):
    places, samples = chosen_ref.shape[0], suffix_out_ref.shape[0]
    steps = out_ref.shape[1]
    body = (chosen_ref.shape[1] - 8) // samples
    per = 2 * body
    row = lax.broadcasted_iota(jnp.int32, (per, HD), 0)
    lane = lax.broadcasted_iota(jnp.int32, (per, HD), 1)

    def turn(note, offset):
        spread = jnp.broadcast_to(note, (per, HD))
        return jnp.sum(jnp.where(lane == row + offset, spread, 0.0), axis=1, keepdims=True)

    for sample in range(samples):
        for group in range(KVH):
            logs, scales, codes = [], [], []
            for place in range(group, places, KVH):
                packed = chosen_ref[place, sample * body : (sample + 1) * body]
                high = jnp.right_shift(packed, 16)
                low = jnp.right_shift(jnp.left_shift(packed, 16), 16)
                codes.append(jnp.concatenate([high, low], axis=0).astype(jnp.float32))
                at = samples * body + sample
                note = chosen_ref[place, at : at + 1].astype(jnp.float32)
                logs.append(turn(note, 0) * (1.0 / LSE_ONE))
                scales.append(jnp.exp2(turn(note, per) - 15.0))
            peak = functools.reduce(jnp.maximum, logs)
            weights = [jnp.exp(log - peak) for log in logs]
            weight_sum = functools.reduce(jnp.add, weights)
            prefix = functools.reduce(
                jnp.add, [(w * s) * c for w, s, c in zip(weights, scales, codes)]
            )
            prefix_log = peak + jnp.log(weight_sum)
            first = group * per
            suffix_log = suffix_log_ref[sample, first : first + per][:, 0:1]
            suffix = suffix_out_ref[sample, first : first + per]
            top = jnp.maximum(prefix_log, suffix_log)
            prefix_weight = jnp.exp(prefix_log - top)
            suffix_weight = jnp.exp(suffix_log - top)
            whole = prefix_weight + suffix_weight
            result = (prefix_weight / (weight_sum * whole)) * prefix + (
                suffix_weight / whole
            ) * suffix
            for i in range(per // steps):
                head = first // steps + i
                out_ref[sample, :, head * HD : (head + 1) * HD] = result[
                    i * steps : (i + 1) * steps
                ].astype(jnp.bfloat16)


def local(
    queries,
    new_keys,
    new_values,
    suffix_keys,
    suffix_values,
    suffix_len,
    sample_prompt,
    prefix_keys,
    prefix_values,
):
    samples, steps, features = queries.shape
    heads = features // HD
    per = GROUP * steps
    seq_count = lax.axis_size("seq")
    engine_count = lax.axis_size("engine")
    positions = prefix_keys.shape[1]

    head_id = lax.rem(lax.axis_index("seq"), KVH).reshape(1)
    heads_of_block = pl.pallas_call(
        split_kernel,
        out_shape=[shape((2, positions, HD), jnp.bfloat16)] * KVH,
        in_specs=[SMEM] + [pl.BlockSpec(memory_space=pltpu.HBM)] * 2,
        out_specs=[VMEM] * KVH,
        scratch_shapes=[pltpu.SemaphoreType.DMA((KVH, 2))],
        compiler_params=params(4),
        name="split",
    )(head_id, prefix_keys, prefix_values)

    def swap(array, near, swapped):
        pairs = []
        for place in range(seq_count):
            chip, core = place // 2, place % 2
            chip = (chip + near * (2 * core - 1)) % (seq_count // 2)
            pairs.append((place, 2 * chip + (1 - core if swapped else core)))
        return lax.ppermute(array, "seq", pairs)

    blocks = [
        heads_of_block[0],
        swap(heads_of_block[1], 0, True),
        swap(heads_of_block[2], 1, False),
        swap(heads_of_block[3], 1, True),
    ]

    rows, payload = pl.pallas_call(
        prepare_kernel,
        out_shape=(
            shape((samples, heads * steps, HD), jnp.bfloat16),
            shape((seq_count, samples * per + 8, HD), jnp.bfloat16),
        ),
        in_specs=[SMEM, VMEM],
        out_specs=(VMEM, VMEM),
        name="prepare",
    )(sample_prompt.reshape(samples), queries)
    received = lax.all_to_all(payload, "seq", split_axis=0, concat_axis=0, tiled=True)

    fresh_pad = ((0, 0), (0, 16 - steps), (0, 0))
    suffix_out, suffix_log = pl.pallas_call(
        suffix_kernel,
        out_shape=(
            shape((samples, heads * steps, HD), jnp.float32),
            shape((samples, heads * steps, HD), jnp.float32),
        ),
        in_specs=[SMEM] + [VMEM] * 5,
        out_specs=(VMEM, VMEM),
        compiler_params=params(12),
        name="suffix",
    )(
        suffix_len,
        rows,
        jnp.pad(new_keys, fresh_pad),
        jnp.pad(new_values, fresh_pad),
        suffix_keys,
        suffix_values,
    )

    packed, slots = pl.pallas_call(
        functools.partial(pack_kernel, samples),
        out_shape=(
            shape((engine_count, CAPE * per, HD), jnp.bfloat16),
            shape((seq_count * samples,), jnp.int32),
        ),
        in_specs=[VMEM],
        out_specs=(VMEM, SMEM),
        scratch_shapes=[pltpu.SMEM((engine_count,), jnp.int32)],
        compiler_params=params(4),
        name="pack",
    )(received)
    dispatched = lax.all_to_all(packed, "engine", split_axis=0, concat_axis=0, tiled=True)

    dispatched, suffix_out, suffix_log = lax.optimization_barrier(
        (dispatched, suffix_out, suffix_log)
    )

    reply = pl.pallas_call(
        functools.partial(prefix_kernel, 16 * CAPE),
        out_shape=shape((engine_count, CAPE * per // 2 + 8, HD), jnp.int32),
        in_specs=[VMEM] * (1 + KVH),
        out_specs=VMEM,
        compiler_params=params(32),
        name="prefix",
    )(dispatched.reshape(engine_count * CAPE, per, HD), *blocks)
    returned = lax.all_to_all(reply, "engine", split_axis=0, concat_axis=0, tiled=True)

    chosen = pl.pallas_call(
        functools.partial(select_kernel, samples),
        out_shape=shape((seq_count, samples * per // 2 + 8, HD), jnp.int32),
        in_specs=[SMEM, VMEM],
        out_specs=VMEM,
        compiler_params=params(4),
        name="select",
    )(slots, returned)
    gathered = lax.all_to_all(chosen, "seq", split_axis=0, concat_axis=0, tiled=True)

    return pl.pallas_call(
        combine_kernel,
        out_shape=shape((samples, steps, features), jnp.bfloat16),
        in_specs=[VMEM] * 3,
        out_specs=VMEM,
        compiler_params=params(6),
        name="combine",
    )(gathered, suffix_out, suffix_log)


def solution(mesh):
    return jax.shard_map(
        local,
        mesh=mesh,
        in_specs=(
            P(("engine", "seq"), None, None),
            P(("engine", "seq"), None, None),
            P(("engine", "seq"), None, None),
            P(("engine", "seq"), None, None),
            P(("engine", "seq"), None, None),
            P(("engine", "seq")),
            P(("engine", "seq"), None),
            P("engine", "seq", None),
            P("engine", "seq", None),
        ),
        out_specs=P(("engine", "seq"), None, None),
        check_vma=False,
    )
```

```python
import functools
import math

import jax
import jax.numpy as jnp
from jax import lax
from jax.experimental import pallas as pl
from jax.experimental.pallas import tpu as pltpu
from jax.sharding import PartitionSpec as P

KVH = 4
GROUP = 8
HD = 128
CAPE = 3
SCALING = HD ** (-0.5)
LOG2E = math.log2(math.e)
LN2 = math.log(2.0)
LSE_ONE = float(2**20)
VMEM = pl.BlockSpec(memory_space=pltpu.VMEM)
SMEM = pl.BlockSpec(memory_space=pltpu.SMEM)


def params(mib):
    return pltpu.CompilerParams(vmem_limit_bytes=mib * 1024 * 1024)


def shape(dims, dtype):
    return jax.ShapeDtypeStruct(dims, dtype)


def prepare_kernel(prompt_ref, queries_ref, rows_ref, payload_ref):
    samples, steps, features = queries_ref.shape
    heads = features // HD
    part = heads * steps // KVH
    extra = payload_ref.shape[1] - samples * part
    lanes = lax.broadcasted_iota(jnp.int32, (extra, HD), 1)
    note = jnp.zeros((extra, HD), jnp.int32)
    for sample in range(samples):
        note = jnp.where(lanes == sample, prompt_ref[sample], note)
    note = note.astype(jnp.float32).astype(jnp.bfloat16)
    for sample in range(samples):
        for first in range(0, heads, 4):
            tile = jnp.concatenate(
                [
                    queries_ref[sample, :, (first + i) * HD : (first + i + 1) * HD].astype(jnp.float32)
                    for i in range(4)
                ],
                axis=0,
            ).astype(jnp.bfloat16)
            row = first * steps
            rows_ref[sample, row : row + 4 * steps] = tile
            group, row = row // part, row % part
            for place in range(group, payload_ref.shape[0], KVH):
                payload_ref[place, sample * part + row : sample * part + row + 4 * steps] = tile
    for place in range(payload_ref.shape[0]):
        payload_ref[place, samples * part :] = note


def split_kernel(head_ref, k_ref, v_ref, *refs):
    outs, sems = refs[:-1], refs[-1]
    copies = []
    for place, out in enumerate(outs):
        head = jnp.bitwise_xor(head_ref[0], place)
        cols = pl.ds(pl.multiple_of(head * HD, HD), HD)
        for which, array in enumerate((k_ref, v_ref)):
            copies.append(
                pltpu.make_async_copy(array.at[0, :, cols], out.at[which], sems.at[place, which])
            )
    for copy in copies:
        copy.start()
    for copy in copies:
        copy.wait()


def pack_kernel(samples, received_ref, packed_ref, slots_ref, counts_ref):
    prompts, part = packed_ref.shape[0], packed_ref.shape[1] // CAPE
    packed_ref[...] = jnp.zeros(packed_ref.shape, packed_ref.dtype)
    for prompt in range(prompts):
        counts_ref[prompt] = 0
    for place in range(received_ref.shape[0]):
        note = received_ref[place, samples * part :].astype(jnp.float32).astype(jnp.int32)
        for sample in range(samples):
            prompt = note[0, sample]
            rank = counts_ref[prompt]
            counts_ref[prompt] = rank + 1
            slots_ref[place * samples + sample] = prompt * 4 + rank
            packed_ref[prompt, pl.ds(pl.multiple_of(rank * part, part), part)] = received_ref[
                place, sample * part : (sample + 1) * part
            ]


def scores(rows, keys):
    return lax.dot_general(rows, keys, (((1,), (1,)), ((), ())), preferred_element_type=jnp.float32)


def encode(out):
    largest = jnp.max(jnp.abs(out), axis=1, keepdims=True)
    power = jnp.floor(jnp.log2(jnp.maximum(largest, 2.0**-112) * 1.0001)) + 1.0
    code = jnp.clip(jnp.round(out * jnp.exp2(15.0 - power)), -32767.0, 32767.0)
    return code.astype(jnp.int32), power.astype(jnp.int32)


def prefix_kernel(chunk, q_ref, *refs):
    blocks, (reply_ref, raw_ref, probs_ref, acc_ref) = refs[:-4], refs[-4:]
    slots, per = q_ref.shape[0], q_ref.shape[1]
    rows_of = per // 2
    row = lax.broadcasted_iota(jnp.int32, (per, HD), 0)
    lane = lax.broadcasted_iota(jnp.int32, (per, HD), 1)

    def step(index, _):
        rows = q_ref[pl.ds(index * chunk, chunk)].reshape(chunk * per, HD)
        raw_ref[0] = scores(rows, blocks[0][0])
        tops, sums = [], []
        for place, block in enumerate(blocks):
            turn = place % 2
            if place + 1 < len(blocks):
                raw_ref[1 - turn] = scores(rows, blocks[place + 1][0])
            for slot in range(chunk):
                here = slice(slot * per, (slot + 1) * per)
                raw = raw_ref[turn, here]
                top = jnp.max(raw, axis=1, keepdims=True)
                probs = jnp.exp2((raw - top) * (SCALING * LOG2E))
                probs_ref[turn, here] = probs.astype(jnp.bfloat16)
                tops.append(top)
                sums.append(jnp.sum(probs, axis=1, keepdims=True))
            acc_ref[place] = jnp.dot(
                probs_ref[turn], block[1], preferred_element_type=jnp.float32
            )
        for slot in range(chunk):
            here = slice(slot * per, (slot + 1) * per)
            top = functools.reduce(jnp.maximum, tops[slot::chunk])
            weights = [jnp.exp2((one - top) * (SCALING * LOG2E)) for one in tops[slot::chunk]]
            total = functools.reduce(
                jnp.add, [w * one for w, one in zip(weights, sums[slot::chunk])]
            )
            share = 1.0 / total
            out = functools.reduce(
                jnp.add, [(w * share) * acc_ref[place, here] for place, w in enumerate(weights)]
            )
            log = jnp.round((top * SCALING + jnp.log(total)) * LSE_ONE).astype(jnp.int32)
            code, power = encode(out)
            packed = jnp.bitwise_or(
                jnp.left_shift(code[:rows_of], 16), jnp.bitwise_and(code[rows_of:], 0xFFFF)
            )
            note = jnp.where(lane == row, log, 0)
            note = jnp.where(lane == row + per, power, note)
            note = jnp.sum(note, axis=0, keepdims=True)
            dest, rank = index * (chunk // CAPE) + slot // CAPE, slot % CAPE
            for part in range(rows_of // 4):
                reply_ref[dest, rank * (rows_of // 4) + part] = packed[part * 4 : part * 4 + 4]
            reply_ref[dest, CAPE * (rows_of // 4), rank : rank + 1] = note
        return 0

    lax.fori_loop(0, slots // chunk, step, 0)


def select_kernel(samples, slots_ref, reply_ref, chosen_ref):
    body = (chosen_ref.shape[1] - 1) // samples
    for sample in range(chosen_ref.shape[0] * samples):
        slot = slots_ref[sample]
        prompt, rank = lax.shift_right_logical(slot, 2), lax.bitwise_and(slot, 3)
        place, which = sample // samples, sample % samples
        chosen_ref[place, which * body : (which + 1) * body] = reply_ref[
            prompt, pl.ds(rank * body, body)
        ]
        chosen_ref[place, samples * body, which : which + 1] = reply_ref[
            prompt, CAPE * body, pl.ds(rank, 1)
        ]


def suffix_kernel(length_ref, rows_ref, fresh_k_ref, fresh_v_ref, k_ref, v_ref, out_ref, log_ref):
    samples, positions = k_ref.shape[0], k_ref.shape[1]
    fresh = fresh_k_ref.shape[1]
    per = rows_ref.shape[1] // KVH
    steps = per // GROUP
    column = lax.broadcasted_iota(jnp.int32, (per, positions), 1)
    step = lax.rem(lax.broadcasted_iota(jnp.int32, (per, fresh), 0), steps)
    causal = lax.broadcasted_iota(jnp.int32, (per, fresh), 1) <= step
    for sample in range(samples):
        live = column < length_ref[sample]
        for group in range(KVH):
            cols = slice(group * HD, (group + 1) * HD)
            rows = rows_ref[sample, group * per : (group + 1) * per]
            dims = (((1,), (1,)), ((), ()))
            cache_raw = lax.dot_general(
                rows, k_ref[sample, :, cols], dims, preferred_element_type=jnp.float32
            )
            fresh_raw = lax.dot_general(
                rows, fresh_k_ref[sample, :, cols], dims, preferred_element_type=jnp.float32
            )
            cache_raw = jnp.where(live, cache_raw, -jnp.inf)
            fresh_raw = jnp.where(causal, fresh_raw, -jnp.inf)
            top = jnp.maximum(
                jnp.max(cache_raw, axis=1, keepdims=True), jnp.max(fresh_raw, axis=1, keepdims=True)
            )
            cache_probs = jnp.exp2((cache_raw - top) * (SCALING * LOG2E))
            fresh_probs = jnp.exp2((fresh_raw - top) * (SCALING * LOG2E))
            total = jnp.sum(cache_probs, axis=1, keepdims=True) + jnp.sum(
                fresh_probs, axis=1, keepdims=True
            )
            acc = jnp.dot(
                cache_probs.astype(jnp.bfloat16),
                v_ref[sample, :, cols],
                preferred_element_type=jnp.float32,
            ) + jnp.dot(
                fresh_probs.astype(jnp.bfloat16),
                fresh_v_ref[sample, :, cols],
                preferred_element_type=jnp.float32,
            )
            here = slice(group * per, (group + 1) * per)
            out_ref[sample, here] = acc / total
            log_ref[sample, here] = jnp.broadcast_to(top * SCALING + jnp.log(total), (per, HD))


def combine_kernel(chosen_ref, suffix_out_ref, suffix_log_ref, out_ref):
    places, samples = chosen_ref.shape[0], suffix_out_ref.shape[0]
    steps = out_ref.shape[1]
    body = (chosen_ref.shape[1] - 1) // samples
    per = 8 * body
    row = lax.broadcasted_iota(jnp.int32, (per, HD), 0)
    lane = lax.broadcasted_iota(jnp.int32, (per, HD), 1)

    def turn(note, offset):
        spread = jnp.broadcast_to(note, (per, HD))
        return jnp.sum(jnp.where(lane == row + offset, spread, 0.0), axis=1, keepdims=True)

    for sample in range(samples):
        for group in range(KVH):
            logs, scales, codes = [], [], []
            for place in range(group, places, KVH):
                packed = jnp.concatenate(
                    [chosen_ref[place, sample * body + part] for part in range(body)], axis=0
                )
                high = jnp.right_shift(packed, 16)
                low = jnp.right_shift(jnp.left_shift(packed, 16), 16)
                codes.append(jnp.concatenate([high, low], axis=0).astype(jnp.float32))
                note = chosen_ref[place, samples * body, sample : sample + 1].astype(jnp.float32)
                logs.append(turn(note, 0) * (1.0 / LSE_ONE))
                scales.append(jnp.exp2(turn(note, per) - 15.0))
            peak = functools.reduce(jnp.maximum, logs)
            weights = [jnp.exp(log - peak) for log in logs]
            weight_sum = functools.reduce(jnp.add, weights)
            prefix = functools.reduce(
                jnp.add, [(w * s) * c for w, s, c in zip(weights, scales, codes)]
            )
            prefix_log = peak + jnp.log(weight_sum)
            first = group * per
            suffix_log = suffix_log_ref[sample, first : first + per][:, 0:1]
            suffix = suffix_out_ref[sample, first : first + per]
            top = jnp.maximum(prefix_log, suffix_log)
            prefix_weight = jnp.exp(prefix_log - top)
            suffix_weight = jnp.exp(suffix_log - top)
            whole = prefix_weight + suffix_weight
            result = (prefix_weight / (weight_sum * whole)) * prefix + (
                suffix_weight / whole
            ) * suffix
            for i in range(per // steps):
                head = first // steps + i
                out_ref[sample, :, head * HD : (head + 1) * HD] = result[
                    i * steps : (i + 1) * steps
                ].astype(jnp.bfloat16)


def local(
    queries,
    new_keys,
    new_values,
    suffix_keys,
    suffix_values,
    suffix_len,
    sample_prompt,
    prefix_keys,
    prefix_values,
):
    samples, steps, features = queries.shape
    heads = features // HD
    per = GROUP * steps
    seq_count = lax.axis_size("seq")
    engine_count = lax.axis_size("engine")
    positions = prefix_keys.shape[1]

    head_id = lax.rem(lax.axis_index("seq"), KVH).reshape(1)
    heads_of_block = pl.pallas_call(
        split_kernel,
        out_shape=[shape((2, positions, HD), jnp.bfloat16)] * KVH,
        in_specs=[SMEM] + [pl.BlockSpec(memory_space=pltpu.HBM)] * 2,
        out_specs=[VMEM] * KVH,
        scratch_shapes=[pltpu.SemaphoreType.DMA((KVH, 2))],
        compiler_params=params(4),
        name="split",
    )(head_id, prefix_keys, prefix_values)

    def swap(array, near, swapped):
        pairs = []
        for place in range(seq_count):
            chip, core = place // 2, place % 2
            chip = (chip + near * (2 * core - 1)) % (seq_count // 2)
            pairs.append((place, 2 * chip + (1 - core if swapped else core)))
        return lax.ppermute(array, "seq", pairs)

    blocks = [
        heads_of_block[0],
        swap(heads_of_block[1], 0, True),
        swap(heads_of_block[2], 1, False),
        swap(heads_of_block[3], 1, True),
    ]

    rows, payload = pl.pallas_call(
        prepare_kernel,
        out_shape=(
            shape((samples, heads * steps, HD), jnp.bfloat16),
            shape((seq_count, samples * per + 8, HD), jnp.bfloat16),
        ),
        in_specs=[SMEM, VMEM],
        out_specs=(VMEM, VMEM),
        name="prepare",
    )(sample_prompt.reshape(samples), queries)
    received = lax.all_to_all(payload, "seq", split_axis=0, concat_axis=0, tiled=True)

    fresh_pad = ((0, 0), (0, 16 - steps), (0, 0))
    suffix_out, suffix_log = pl.pallas_call(
        suffix_kernel,
        out_shape=(
            shape((samples, heads * steps, HD), jnp.float32),
            shape((samples, heads * steps, HD), jnp.float32),
        ),
        in_specs=[SMEM] + [VMEM] * 5,
        out_specs=(VMEM, VMEM),
        compiler_params=params(12),
        name="suffix",
    )(
        suffix_len,
        rows,
        jnp.pad(new_keys, fresh_pad),
        jnp.pad(new_values, fresh_pad),
        suffix_keys,
        suffix_values,
    )

    packed, slots = pl.pallas_call(
        functools.partial(pack_kernel, samples),
        out_shape=(
            shape((engine_count, CAPE * per, HD), jnp.bfloat16),
            shape((seq_count * samples,), jnp.int32),
        ),
        in_specs=[VMEM],
        out_specs=(VMEM, SMEM),
        scratch_shapes=[pltpu.SMEM((engine_count,), jnp.int32)],
        compiler_params=params(4),
        name="pack",
    )(received)
    dispatched = lax.all_to_all(packed, "engine", split_axis=0, concat_axis=0, tiled=True)

    dispatched, suffix_out, suffix_log = lax.optimization_barrier(
        (dispatched, suffix_out, suffix_log)
    )

    chunk = 8 * CAPE
    reply = pl.pallas_call(
        functools.partial(prefix_kernel, chunk),
        out_shape=shape((engine_count, CAPE * per // 8 + 1, 4, HD), jnp.int32),
        in_specs=[VMEM] * (1 + KVH),
        out_specs=VMEM,
        scratch_shapes=[
            pltpu.VMEM((2, chunk * per, positions), jnp.float32),
            pltpu.VMEM((2, chunk * per, positions), jnp.bfloat16),
            pltpu.VMEM((KVH, chunk * per, HD), jnp.float32),
        ],
        compiler_params=params(28),
        name="prefix",
    )(dispatched.reshape(engine_count * CAPE, per, HD), *blocks)
    returned = lax.all_to_all(reply, "engine", split_axis=0, concat_axis=0, tiled=True)

    chosen = pl.pallas_call(
        functools.partial(select_kernel, samples),
        out_shape=shape((seq_count, samples * per // 8 + 1, 4, HD), jnp.int32),
        in_specs=[SMEM, VMEM],
        out_specs=VMEM,
        compiler_params=params(4),
        name="select",
    )(slots, returned)
    gathered = lax.all_to_all(chosen, "seq", split_axis=0, concat_axis=0, tiled=True)

    return pl.pallas_call(
        combine_kernel,
        out_shape=shape((samples, steps, features), jnp.bfloat16),
        in_specs=[VMEM] * 3,
        out_specs=VMEM,
        compiler_params=params(6),
        name="combine",
    )(gathered, suffix_out, suffix_log)


def solution(mesh):
    return jax.shard_map(
        local,
        mesh=mesh,
        in_specs=(
            P(("engine", "seq"), None, None),
            P(("engine", "seq"), None, None),
            P(("engine", "seq"), None, None),
            P(("engine", "seq"), None, None),
            P(("engine", "seq"), None, None),
            P(("engine", "seq")),
            P(("engine", "seq"), None),
            P("engine", "seq", None),
            P("engine", "seq", None),
        ),
        out_specs=P(("engine", "seq"), None, None),
        check_vma=False,
    )
```

```python
import functools
import math

import jax
import jax.numpy as jnp
from jax import lax
from jax.experimental import pallas as pl
from jax.experimental.pallas import tpu as pltpu
from jax.sharding import PartitionSpec as P

KVH = 4
GROUP = 8
HD = 128
CAPE = 3
SCALING = HD ** (-0.5)
LOG2E = math.log2(math.e)
LN2 = math.log(2.0)
LSE_ONE = float(2**20)
VMEM = pl.BlockSpec(memory_space=pltpu.VMEM)
SMEM = pl.BlockSpec(memory_space=pltpu.SMEM)


def params(mib):
    return pltpu.CompilerParams(vmem_limit_bytes=mib * 1024 * 1024)


def shape(dims, dtype):
    return jax.ShapeDtypeStruct(dims, dtype)


def prepare_kernel(prompt_ref, queries_ref, rows_ref, payload_ref):
    samples, steps, features = queries_ref.shape
    heads = features // HD
    part = heads * steps // KVH
    extra = payload_ref.shape[1] - samples * part
    lanes = lax.broadcasted_iota(jnp.int32, (extra, HD), 1)
    note = jnp.zeros((extra, HD), jnp.int32)
    for sample in range(samples):
        note = jnp.where(lanes == sample, prompt_ref[sample], note)
    note = note.astype(jnp.float32).astype(jnp.bfloat16)
    for sample in range(samples):
        for first in range(0, heads, 4):
            tile = jnp.concatenate(
                [
                    queries_ref[sample, :, (first + i) * HD : (first + i + 1) * HD].astype(jnp.float32)
                    for i in range(4)
                ],
                axis=0,
            ).astype(jnp.bfloat16)
            row = first * steps
            rows_ref[sample, row : row + 4 * steps] = tile
            group, row = row // part, row % part
            for place in range(group, payload_ref.shape[0], KVH):
                payload_ref[place, sample * part + row : sample * part + row + 4 * steps] = tile
    for place in range(payload_ref.shape[0]):
        payload_ref[place, samples * part :] = note


def split_kernel(head_ref, k_ref, v_ref, *refs):
    outs, sems = refs[:-1], refs[-1]
    copies = []
    for place, out in enumerate(outs):
        head = jnp.bitwise_xor(head_ref[0], place)
        cols = pl.ds(pl.multiple_of(head * HD, HD), HD)
        for which, array in enumerate((k_ref, v_ref)):
            copies.append(
                pltpu.make_async_copy(array.at[0, :, cols], out.at[which], sems.at[place, which])
            )
    for copy in copies:
        copy.start()
    for copy in copies:
        copy.wait()


def pack_kernel(samples, received_ref, packed_ref, slots_ref, counts_ref):
    prompts, part = packed_ref.shape[0], packed_ref.shape[1] // CAPE
    packed_ref[...] = jnp.zeros(packed_ref.shape, packed_ref.dtype)
    for prompt in range(prompts):
        counts_ref[prompt] = 0
    for place in range(received_ref.shape[0]):
        note = received_ref[place, samples * part :].astype(jnp.float32).astype(jnp.int32)
        for sample in range(samples):
            prompt = note[0, sample]
            rank = counts_ref[prompt]
            counts_ref[prompt] = rank + 1
            slots_ref[place * samples + sample] = prompt * 4 + rank
            packed_ref[prompt, pl.ds(pl.multiple_of(rank * part, part), part)] = received_ref[
                place, sample * part : (sample + 1) * part
            ]


def scores(rows, keys):
    return lax.dot_general(rows, keys, (((1,), (1,)), ((), ())), preferred_element_type=jnp.float32)


def encode(out):
    largest = jnp.max(jnp.abs(out), axis=1, keepdims=True)
    power = jnp.floor(jnp.log2(jnp.maximum(largest, 2.0**-112) * 1.0001)) + 1.0
    code = jnp.clip(jnp.round(out * jnp.exp2(15.0 - power)), -32767.0, 32767.0)
    return code.astype(jnp.int32), power.astype(jnp.int32)


def prefix_kernel(chunk, q_ref, *refs):
    blocks, reply_ref = refs[:-1], refs[-1]
    slots, per = q_ref.shape[0], q_ref.shape[1]
    rows_of = per // 2
    row = lax.broadcasted_iota(jnp.int32, (chunk, per, HD), 1)
    lane = lax.broadcasted_iota(jnp.int32, (chunk, per, HD), 2)

    def attention(raw, values):
        top = jnp.max(raw, axis=1, keepdims=True)
        probs = jnp.exp2((raw - top) * (SCALING * LOG2E))
        total = jnp.sum(probs, axis=1, keepdims=True)
        acc = jnp.dot(probs.astype(jnp.bfloat16), values, preferred_element_type=jnp.float32)
        return acc, top, total

    def finish(first, parts):
        top = functools.reduce(jnp.maximum, [part[1] for part in parts])
        weights = [jnp.exp2((part[1] - top) * (SCALING * LOG2E)) for part in parts]
        total = functools.reduce(jnp.add, [w * part[2] for w, part in zip(weights, parts)])
        share = 1.0 / total
        out = functools.reduce(jnp.add, [(w * share) * part[0] for w, part in zip(weights, parts)])
        log = jnp.round((top * SCALING + jnp.log(total)) * LSE_ONE).astype(jnp.int32)
        code, power = encode(out)
        code = code.reshape(chunk, per, HD)
        packed = jnp.bitwise_or(
            jnp.left_shift(code[:, :rows_of], 16), jnp.bitwise_and(code[:, rows_of:], 0xFFFF)
        )
        note = jnp.where(lane == row, log.reshape(chunk, per, 1), 0)
        note = jnp.where(lane == row + per, power.reshape(chunk, per, 1), note)
        note = jnp.sum(note, axis=1)
        for slot in range(chunk):
            dest, rank = (first + slot) // CAPE, (first + slot) % CAPE
            for part in range(rows_of // 4):
                reply_ref[dest, rank * (rows_of // 4) + part] = packed[
                    slot, part * 4 : part * 4 + 4
                ]
            reply_ref[dest, CAPE * (rows_of // 4), rank : rank + 1] = note[slot : slot + 1]

    stages = [(first, place) for first in range(0, slots, chunk) for place in range(len(blocks))]
    rows = {
        first: q_ref[first : first + chunk].reshape(chunk * per, HD)
        for first in range(0, slots, chunk)
    }
    raw, parts = scores(rows[0], blocks[0][0]), []
    for number, (first, place) in enumerate(stages):
        ready = raw
        if number + 1 < len(stages):
            later, block = stages[number + 1]
            raw = scores(rows[later], blocks[block][0])
        parts.append(attention(ready, blocks[place][1]))
        if place + 1 == len(blocks):
            finish(first, parts)
            parts = []


def select_kernel(samples, slots_ref, reply_ref, chosen_ref):
    body = (chosen_ref.shape[1] - 1) // samples
    for sample in range(chosen_ref.shape[0] * samples):
        slot = slots_ref[sample]
        prompt, rank = lax.shift_right_logical(slot, 2), lax.bitwise_and(slot, 3)
        place, which = sample // samples, sample % samples
        chosen_ref[place, which * body : (which + 1) * body] = reply_ref[
            prompt, pl.ds(rank * body, body)
        ]
        chosen_ref[place, samples * body, which : which + 1] = reply_ref[
            prompt, CAPE * body, pl.ds(rank, 1)
        ]


def suffix_kernel(length_ref, rows_ref, fresh_k_ref, fresh_v_ref, k_ref, v_ref, out_ref, log_ref):
    samples, positions = k_ref.shape[0], k_ref.shape[1]
    fresh = fresh_k_ref.shape[1]
    per = rows_ref.shape[1] // KVH
    steps = per // GROUP
    column = lax.broadcasted_iota(jnp.int32, (per, positions), 1)
    step = lax.rem(lax.broadcasted_iota(jnp.int32, (per, fresh), 0), steps)
    causal = lax.broadcasted_iota(jnp.int32, (per, fresh), 1) <= step
    for sample in range(samples):
        live = column < length_ref[sample]
        for group in range(KVH):
            cols = slice(group * HD, (group + 1) * HD)
            rows = rows_ref[sample, group * per : (group + 1) * per]
            dims = (((1,), (1,)), ((), ()))
            cache_raw = lax.dot_general(
                rows, k_ref[sample, :, cols], dims, preferred_element_type=jnp.float32
            )
            fresh_raw = lax.dot_general(
                rows, fresh_k_ref[sample, :, cols], dims, preferred_element_type=jnp.float32
            )
            cache_raw = jnp.where(live, cache_raw, -jnp.inf)
            fresh_raw = jnp.where(causal, fresh_raw, -jnp.inf)
            top = jnp.maximum(
                jnp.max(cache_raw, axis=1, keepdims=True), jnp.max(fresh_raw, axis=1, keepdims=True)
            )
            cache_probs = jnp.exp2((cache_raw - top) * (SCALING * LOG2E))
            fresh_probs = jnp.exp2((fresh_raw - top) * (SCALING * LOG2E))
            total = jnp.sum(cache_probs, axis=1, keepdims=True) + jnp.sum(
                fresh_probs, axis=1, keepdims=True
            )
            acc = jnp.dot(
                cache_probs.astype(jnp.bfloat16),
                v_ref[sample, :, cols],
                preferred_element_type=jnp.float32,
            ) + jnp.dot(
                fresh_probs.astype(jnp.bfloat16),
                fresh_v_ref[sample, :, cols],
                preferred_element_type=jnp.float32,
            )
            here = slice(group * per, (group + 1) * per)
            out_ref[sample, here] = acc / total
            log_ref[sample, here] = jnp.broadcast_to(top * SCALING + jnp.log(total), (per, HD))


def combine_kernel(chosen_ref, suffix_out_ref, suffix_log_ref, out_ref):
    places, samples = chosen_ref.shape[0], suffix_out_ref.shape[0]
    steps = out_ref.shape[1]
    body = (chosen_ref.shape[1] - 1) // samples
    per = 8 * body
    row = lax.broadcasted_iota(jnp.int32, (per, HD), 0)
    lane = lax.broadcasted_iota(jnp.int32, (per, HD), 1)

    def turn(note, offset):
        spread = jnp.broadcast_to(note, (per, HD))
        return jnp.sum(jnp.where(lane == row + offset, spread, 0.0), axis=1, keepdims=True)

    for sample in range(samples):
        for group in range(KVH):
            logs, scales, codes = [], [], []
            for place in range(group, places, KVH):
                packed = jnp.concatenate(
                    [chosen_ref[place, sample * body + part] for part in range(body)], axis=0
                )
                high = jnp.right_shift(packed, 16)
                low = jnp.right_shift(jnp.left_shift(packed, 16), 16)
                codes.append(jnp.concatenate([high, low], axis=0).astype(jnp.float32))
                note = chosen_ref[place, samples * body, sample : sample + 1].astype(jnp.float32)
                logs.append(turn(note, 0) * (1.0 / LSE_ONE))
                scales.append(jnp.exp2(turn(note, per) - 15.0))
            peak = functools.reduce(jnp.maximum, logs)
            weights = [jnp.exp(log - peak) for log in logs]
            weight_sum = functools.reduce(jnp.add, weights)
            prefix = functools.reduce(
                jnp.add, [(w * s) * c for w, s, c in zip(weights, scales, codes)]
            )
            prefix_log = peak + jnp.log(weight_sum)
            first = group * per
            suffix_log = suffix_log_ref[sample, first : first + per][:, 0:1]
            suffix = suffix_out_ref[sample, first : first + per]
            top = jnp.maximum(prefix_log, suffix_log)
            prefix_weight = jnp.exp(prefix_log - top)
            suffix_weight = jnp.exp(suffix_log - top)
            whole = prefix_weight + suffix_weight
            result = (prefix_weight / (weight_sum * whole)) * prefix + (
                suffix_weight / whole
            ) * suffix
            for i in range(per // steps):
                head = first // steps + i
                out_ref[sample, :, head * HD : (head + 1) * HD] = result[
                    i * steps : (i + 1) * steps
                ].astype(jnp.bfloat16)


def local(
    queries,
    new_keys,
    new_values,
    suffix_keys,
    suffix_values,
    suffix_len,
    sample_prompt,
    prefix_keys,
    prefix_values,
):
    samples, steps, features = queries.shape
    heads = features // HD
    per = GROUP * steps
    seq_count = lax.axis_size("seq")
    engine_count = lax.axis_size("engine")
    positions = prefix_keys.shape[1]

    head_id = lax.rem(lax.axis_index("seq"), KVH).reshape(1)
    heads_of_block = pl.pallas_call(
        split_kernel,
        out_shape=[shape((2, positions, HD), jnp.bfloat16)] * KVH,
        in_specs=[SMEM] + [pl.BlockSpec(memory_space=pltpu.HBM)] * 2,
        out_specs=[VMEM] * KVH,
        scratch_shapes=[pltpu.SemaphoreType.DMA((KVH, 2))],
        compiler_params=params(4),
        name="split",
    )(
        head_id,
        pltpu.with_memory_space_constraint(prefix_keys, pltpu.HBM),
        pltpu.with_memory_space_constraint(prefix_values, pltpu.HBM),
    )

    def swap(array, near, swapped):
        pairs = []
        for place in range(seq_count):
            chip, core = place // 2, place % 2
            chip = (chip + near * (2 * core - 1)) % (seq_count // 2)
            pairs.append((place, 2 * chip + (1 - core if swapped else core)))
        return lax.ppermute(array, "seq", pairs)

    blocks = [
        heads_of_block[0],
        swap(heads_of_block[1], 0, True),
        swap(heads_of_block[2], 1, False),
        swap(heads_of_block[3], 1, True),
    ]

    rows, payload = pl.pallas_call(
        prepare_kernel,
        out_shape=(
            shape((samples, heads * steps, HD), jnp.bfloat16),
            shape((seq_count, samples * per + 8, HD), jnp.bfloat16),
        ),
        in_specs=[SMEM, VMEM],
        out_specs=(VMEM, VMEM),
        name="prepare",
    )(sample_prompt.reshape(samples), queries)
    received = lax.all_to_all(payload, "seq", split_axis=0, concat_axis=0, tiled=True)

    fresh_pad = ((0, 0), (0, 16 - steps), (0, 0))
    suffix_out, suffix_log = pl.pallas_call(
        suffix_kernel,
        out_shape=(
            shape((samples, heads * steps, HD), jnp.float32),
            shape((samples, heads * steps, HD), jnp.float32),
        ),
        in_specs=[SMEM] + [VMEM] * 5,
        out_specs=(VMEM, VMEM),
        compiler_params=params(12),
        name="suffix",
    )(
        suffix_len,
        rows,
        jnp.pad(new_keys, fresh_pad),
        jnp.pad(new_values, fresh_pad),
        suffix_keys,
        suffix_values,
    )

    packed, slots = pl.pallas_call(
        functools.partial(pack_kernel, samples),
        out_shape=(
            pltpu.HBM((engine_count, CAPE * per, HD), jnp.bfloat16),
            shape((seq_count * samples,), jnp.int32),
        ),
        in_specs=[VMEM],
        out_specs=(VMEM, SMEM),
        scratch_shapes=[pltpu.SMEM((engine_count,), jnp.int32)],
        compiler_params=params(4),
        name="pack",
    )(received)
    dispatched = lax.all_to_all(packed, "engine", split_axis=0, concat_axis=0, tiled=True)

    dispatched, suffix_out, suffix_log = lax.optimization_barrier(
        (dispatched, suffix_out, suffix_log)
    )

    chunk = 4 * CAPE
    reply = pl.pallas_call(
        functools.partial(prefix_kernel, chunk),
        out_shape=shape((engine_count, CAPE * per // 8 + 1, 4, HD), jnp.int32),
        in_specs=[VMEM] * (1 + KVH),
        out_specs=VMEM,
        compiler_params=params(28),
        name="prefix",
    )(dispatched.reshape(engine_count * CAPE, per, HD), *blocks)
    returned = lax.all_to_all(reply, "engine", split_axis=0, concat_axis=0, tiled=True)

    chosen = pl.pallas_call(
        functools.partial(select_kernel, samples),
        out_shape=shape((seq_count, samples * per // 8 + 1, 4, HD), jnp.int32),
        in_specs=[SMEM, VMEM],
        out_specs=VMEM,
        compiler_params=params(4),
        name="select",
    )(slots, returned)
    gathered = lax.all_to_all(chosen, "seq", split_axis=0, concat_axis=0, tiled=True)

    return pl.pallas_call(
        combine_kernel,
        out_shape=shape((samples, steps, features), jnp.bfloat16),
        in_specs=[VMEM] * 3,
        out_specs=VMEM,
        compiler_params=params(6),
        name="combine",
    )(gathered, suffix_out, suffix_log)


def solution(mesh):
    return jax.shard_map(
        local,
        mesh=mesh,
        in_specs=(
            P(("engine", "seq"), None, None),
            P(("engine", "seq"), None, None),
            P(("engine", "seq"), None, None),
            P(("engine", "seq"), None, None),
            P(("engine", "seq"), None, None),
            P(("engine", "seq")),
            P(("engine", "seq"), None),
            P("engine", "seq", None),
            P("engine", "seq", None),
        ),
        out_specs=P(("engine", "seq"), None, None),
        check_vma=False,
    )
```

```python
import functools
import math

import jax
import jax.numpy as jnp
from jax import lax
from jax.experimental import pallas as pl
from jax.experimental.pallas import tpu as pltpu
from jax.sharding import PartitionSpec as P

KVH = 4
GROUP = 8
HD = 128
CAPE = 3
SCALING = HD ** (-0.5)
LOG2E = math.log2(math.e)
LN2 = math.log(2.0)
LSE_ONE = float(2**20)
VMEM = pl.BlockSpec(memory_space=pltpu.VMEM)
SMEM = pl.BlockSpec(memory_space=pltpu.SMEM)


def params(mib):
    return pltpu.CompilerParams(vmem_limit_bytes=mib * 1024 * 1024)


def shape(dims, dtype):
    return jax.ShapeDtypeStruct(dims, dtype)


def prepare_kernel(prompt_ref, queries_ref, rows_ref, payload_ref):
    samples, steps, features = queries_ref.shape
    heads = features // HD
    part = heads * steps // KVH
    extra = payload_ref.shape[1] - samples * part
    lanes = lax.broadcasted_iota(jnp.int32, (extra, HD), 1)
    note = jnp.zeros((extra, HD), jnp.int32)
    for sample in range(samples):
        note = jnp.where(lanes == sample, prompt_ref[sample], note)
    note = note.astype(jnp.float32).astype(jnp.bfloat16)
    for sample in range(samples):
        for first in range(0, heads, 4):
            tile = jnp.concatenate(
                [
                    queries_ref[sample, :, (first + i) * HD : (first + i + 1) * HD].astype(jnp.float32)
                    for i in range(4)
                ],
                axis=0,
            ).astype(jnp.bfloat16)
            row = first * steps
            rows_ref[sample, row : row + 4 * steps] = tile
            group, row = row // part, row % part
            for place in range(group, payload_ref.shape[0], KVH):
                payload_ref[place, sample * part + row : sample * part + row + 4 * steps] = tile
    for place in range(payload_ref.shape[0]):
        payload_ref[place, samples * part :] = note


def split_kernel(head_ref, k_ref, v_ref, *refs):
    outs, sems = refs[:-1], refs[-1]
    copies = []
    for place, out in enumerate(outs):
        head = jnp.bitwise_xor(head_ref[0], place)
        cols = pl.ds(pl.multiple_of(head * HD, HD), HD)
        for which, array in enumerate((k_ref, v_ref)):
            copies.append(
                pltpu.make_async_copy(array.at[0, :, cols], out.at[which], sems.at[place, which])
            )
    for copy in copies:
        copy.start()
    for copy in copies:
        copy.wait()


def pack_kernel(samples, received_ref, packed_ref, slots_ref, counts_ref):
    prompts, part = packed_ref.shape[0], packed_ref.shape[1] // CAPE
    packed_ref[...] = jnp.zeros(packed_ref.shape, packed_ref.dtype)
    for prompt in range(prompts):
        counts_ref[prompt] = 0
    for place in range(received_ref.shape[0]):
        note = received_ref[place, samples * part :].astype(jnp.float32).astype(jnp.int32)
        for sample in range(samples):
            prompt = note[0, sample]
            rank = counts_ref[prompt]
            counts_ref[prompt] = rank + 1
            slots_ref[place * samples + sample] = prompt * 4 + rank
            packed_ref[prompt, pl.ds(pl.multiple_of(rank * part, part), part)] = received_ref[
                place, sample * part : (sample + 1) * part
            ]


def block_scores(rows, keys):
    return lax.dot_general(rows, keys, (((1,), (1,)), ((), ())), preferred_element_type=jnp.float32)


def block_attention(raw, values):
    top = jnp.max(raw, axis=1, keepdims=True)
    probs = jnp.exp2((raw - top) * (SCALING * LOG2E))
    total = jnp.sum(probs, axis=1, keepdims=True)
    acc = jnp.dot(probs.astype(jnp.bfloat16), values, preferred_element_type=jnp.float32)
    return acc, top, total


def encode(out):
    largest = jnp.max(jnp.abs(out), axis=1, keepdims=True)
    power = jnp.floor(jnp.log2(jnp.maximum(largest, 2.0**-112) * 1.0001)) + 1.0
    code = jnp.round(out * jnp.exp2(15.0 - power))
    return code.astype(jnp.int32), power.astype(jnp.int32)


def prefix_kernel(chunk, q_ref, *refs):
    blocks, reply_ref = refs[:-1], refs[-1]
    slots, per = q_ref.shape[0], q_ref.shape[1]
    rows_of = per // 2
    body = CAPE * rows_of

    def step(index, _):
        rows = q_ref[pl.ds(index * chunk, chunk)].reshape(chunk * per, HD)
        parts, raw = [], block_scores(rows, blocks[0][0])
        for place, block in enumerate(blocks):
            ready = raw
            if place + 1 < len(blocks):
                raw = block_scores(rows, blocks[place + 1][0])
            parts.append(block_attention(ready, block[1]))
        top = functools.reduce(jnp.maximum, [part[1] for part in parts])
        weights = [jnp.exp2((part[1] - top) * (SCALING * LOG2E)) for part in parts]
        total = functools.reduce(jnp.add, [w * part[2] for w, part in zip(weights, parts)])
        share = 1.0 / total
        out = functools.reduce(jnp.add, [(w * share) * part[0] for w, part in zip(weights, parts)])
        log = top * SCALING + jnp.log(total)
        code, power = encode(out)
        code = code.reshape(chunk, per, HD)
        packed = jnp.bitwise_or(
            jnp.left_shift(code[:, :rows_of], 16), jnp.bitwise_and(code[:, rows_of:], 0xFFFF)
        )
        row = lax.broadcasted_iota(jnp.int32, (chunk, per, HD), 1)
        lane = lax.broadcasted_iota(jnp.int32, (chunk, per, HD), 2)
        log = jnp.round(log * LSE_ONE).astype(jnp.int32).reshape(chunk, per, 1)
        note = jnp.where(lane == row, log, 0)
        note = jnp.where(lane == row + per, power.reshape(chunk, per, 1), note)
        note = jnp.sum(note, axis=1)
        for part in range(chunk // CAPE):
            dest = index * (chunk // CAPE) + part
            here = slice(part * CAPE, (part + 1) * CAPE)
            reply_ref[dest, 0:body] = packed[here].reshape(body, HD)
            reply_ref[dest, body : body + CAPE] = note[here]
        return 0

    lax.fori_loop(0, slots // chunk, step, 0)


def select_kernel(samples, slots_ref, reply_ref, chosen_ref):
    body = (chosen_ref.shape[1] - 8) // samples
    for sample in range(chosen_ref.shape[0] * samples):
        slot = slots_ref[sample]
        prompt, rank = lax.shift_right_logical(slot, 2), lax.bitwise_and(slot, 3)
        place, start = sample // samples, (sample % samples) * body
        chosen_ref[place, start : start + body] = reply_ref[
            prompt, pl.ds(pl.multiple_of(rank * body, body), body)
        ]
        note = samples * body + sample % samples
        chosen_ref[place, note : note + 1] = reply_ref[prompt, pl.ds(CAPE * body + rank, 1)]


def suffix_kernel(length_ref, rows_ref, fresh_k_ref, fresh_v_ref, k_ref, v_ref, out_ref, log_ref):
    samples, positions = k_ref.shape[0], k_ref.shape[1]
    fresh = 16

    def padded(array):
        rest = jnp.zeros((fresh - array.shape[0], HD), jnp.float32)
        return jnp.concatenate([array.astype(jnp.float32), rest], axis=0).astype(jnp.bfloat16)

    per = rows_ref.shape[1] // KVH
    steps = per // GROUP
    column = lax.broadcasted_iota(jnp.int32, (per, positions), 1)
    step = lax.rem(lax.broadcasted_iota(jnp.int32, (per, fresh), 0), steps)
    causal = lax.broadcasted_iota(jnp.int32, (per, fresh), 1) <= step
    for sample in range(samples):
        live = column < length_ref[sample]
        for group in range(KVH):
            cols = slice(group * HD, (group + 1) * HD)
            rows = rows_ref[sample, group * per : (group + 1) * per]
            dims = (((1,), (1,)), ((), ()))
            cache_raw = lax.dot_general(
                rows, k_ref[sample, :, cols], dims, preferred_element_type=jnp.float32
            )
            fresh_raw = lax.dot_general(
                rows, padded(fresh_k_ref[sample, :, cols]), dims, preferred_element_type=jnp.float32
            )
            cache_raw = jnp.where(live, cache_raw, -jnp.inf)
            fresh_raw = jnp.where(causal, fresh_raw, -jnp.inf)
            top = jnp.maximum(
                jnp.max(cache_raw, axis=1, keepdims=True), jnp.max(fresh_raw, axis=1, keepdims=True)
            )
            cache_probs = jnp.exp2((cache_raw - top) * (SCALING * LOG2E))
            fresh_probs = jnp.exp2((fresh_raw - top) * (SCALING * LOG2E))
            total = jnp.sum(cache_probs, axis=1, keepdims=True) + jnp.sum(
                fresh_probs, axis=1, keepdims=True
            )
            acc = jnp.dot(
                cache_probs.astype(jnp.bfloat16),
                v_ref[sample, :, cols],
                preferred_element_type=jnp.float32,
            ) + jnp.dot(
                fresh_probs.astype(jnp.bfloat16),
                padded(fresh_v_ref[sample, :, cols]),
                preferred_element_type=jnp.float32,
            )
            here = slice(group * per, (group + 1) * per)
            out_ref[sample, here] = acc / total
            log_ref[sample, here] = jnp.broadcast_to(top * SCALING + jnp.log(total), (per, HD))


def combine_kernel(chosen_ref, suffix_out_ref, suffix_log_ref, out_ref):
    places, samples = chosen_ref.shape[0], suffix_out_ref.shape[0]
    steps = out_ref.shape[1]
    body = (chosen_ref.shape[1] - 8) // samples
    per = 2 * body
    row = lax.broadcasted_iota(jnp.int32, (per, HD), 0)
    lane = lax.broadcasted_iota(jnp.int32, (per, HD), 1)

    def turn(note, offset):
        spread = jnp.broadcast_to(note, (per, HD))
        return jnp.sum(jnp.where(lane == row + offset, spread, 0.0), axis=1, keepdims=True)

    for sample in range(samples):
        for group in range(KVH):
            logs, scales, codes = [], [], []
            for place in range(group, places, KVH):
                packed = chosen_ref[place, sample * body : (sample + 1) * body]
                high = jnp.right_shift(packed, 16)
                low = jnp.right_shift(jnp.left_shift(packed, 16), 16)
                codes.append(jnp.concatenate([high, low], axis=0).astype(jnp.float32))
                at = samples * body + sample
                note = chosen_ref[place, at : at + 1].astype(jnp.float32)
                logs.append(turn(note, 0) * (1.0 / LSE_ONE))
                scales.append(jnp.exp2(turn(note, per) - 15.0))
            peak = functools.reduce(jnp.maximum, logs)
            weights = [jnp.exp(log - peak) for log in logs]
            weight_sum = functools.reduce(jnp.add, weights)
            prefix = functools.reduce(
                jnp.add, [(w * s) * c for w, s, c in zip(weights, scales, codes)]
            )
            prefix_log = peak + jnp.log(weight_sum)
            first = group * per
            suffix_log = suffix_log_ref[sample, first : first + per][:, 0:1]
            suffix = suffix_out_ref[sample, first : first + per]
            top = jnp.maximum(prefix_log, suffix_log)
            prefix_weight = jnp.exp(prefix_log - top)
            suffix_weight = jnp.exp(suffix_log - top)
            whole = prefix_weight + suffix_weight
            result = (prefix_weight / (weight_sum * whole)) * prefix + (
                suffix_weight / whole
            ) * suffix
            for i in range(per // steps):
                head = first // steps + i
                out_ref[sample, :, head * HD : (head + 1) * HD] = result[
                    i * steps : (i + 1) * steps
                ].astype(jnp.bfloat16)


def local(
    queries,
    new_keys,
    new_values,
    suffix_keys,
    suffix_values,
    suffix_len,
    sample_prompt,
    prefix_keys,
    prefix_values,
):
    samples, steps, features = queries.shape
    heads = features // HD
    per = GROUP * steps
    seq_count = lax.axis_size("seq")
    engine_count = lax.axis_size("engine")
    positions = prefix_keys.shape[1]

    head_id = lax.rem(lax.axis_index("seq"), KVH).reshape(1)
    heads_of_block = pl.pallas_call(
        split_kernel,
        out_shape=[shape((2, positions, HD), jnp.bfloat16)] * KVH,
        in_specs=[SMEM] + [pl.BlockSpec(memory_space=pltpu.HBM)] * 2,
        out_specs=[VMEM] * KVH,
        scratch_shapes=[pltpu.SemaphoreType.DMA((KVH, 2))],
        compiler_params=params(4),
        name="split",
    )(
        head_id,
        pltpu.with_memory_space_constraint(prefix_keys, pltpu.HBM),
        pltpu.with_memory_space_constraint(prefix_values, pltpu.HBM),
    )

    def swap(array, near, swapped):
        pairs = []
        for place in range(seq_count):
            chip, core = place // 2, place % 2
            chip = (chip + near * (2 * core - 1)) % (seq_count // 2)
            pairs.append((place, 2 * chip + (1 - core if swapped else core)))
        return lax.ppermute(array, "seq", pairs)

    blocks = [
        heads_of_block[0],
        swap(heads_of_block[1], 0, True),
        swap(heads_of_block[2], 1, False),
        swap(heads_of_block[3], 1, True),
    ]

    rows, payload = pl.pallas_call(
        prepare_kernel,
        out_shape=(
            shape((samples, heads * steps, HD), jnp.bfloat16),
            shape((seq_count, samples * per + 8, HD), jnp.bfloat16),
        ),
        in_specs=[SMEM, VMEM],
        out_specs=(VMEM, VMEM),
        name="prepare",
    )(sample_prompt.reshape(samples), queries)
    received = lax.all_to_all(payload, "seq", split_axis=0, concat_axis=0, tiled=True)

    suffix_out, suffix_log = pl.pallas_call(
        suffix_kernel,
        out_shape=(
            shape((samples, heads * steps, HD), jnp.float32),
            shape((samples, heads * steps, HD), jnp.float32),
        ),
        in_specs=[SMEM] + [VMEM] * 5,
        out_specs=(VMEM, VMEM),
        compiler_params=params(12),
        name="suffix",
    )(
        suffix_len,
        rows,
        new_keys,
        new_values,
        suffix_keys,
        suffix_values,
    )

    packed, slots = pl.pallas_call(
        functools.partial(pack_kernel, samples),
        out_shape=(
            pltpu.HBM((engine_count, CAPE * per, HD), jnp.bfloat16),
            shape((seq_count * samples,), jnp.int32),
        ),
        in_specs=[VMEM],
        out_specs=(VMEM, SMEM),
        scratch_shapes=[pltpu.SMEM((engine_count,), jnp.int32)],
        compiler_params=params(4),
        name="pack",
    )(received)
    dispatched = lax.all_to_all(packed, "engine", split_axis=0, concat_axis=0, tiled=True)

    dispatched, suffix_out, suffix_log = lax.optimization_barrier(
        (dispatched, suffix_out, suffix_log)
    )

    reply = pl.pallas_call(
        functools.partial(prefix_kernel, 8 * CAPE),
        out_shape=shape((engine_count, CAPE * per // 2 + 8, HD), jnp.int32),
        in_specs=[VMEM] * (1 + KVH),
        out_specs=VMEM,
        compiler_params=params(28),
        name="prefix",
    )(dispatched.reshape(engine_count * CAPE, per, HD), *blocks)
    returned = lax.all_to_all(reply, "engine", split_axis=0, concat_axis=0, tiled=True)

    chosen = pl.pallas_call(
        functools.partial(select_kernel, samples),
        out_shape=shape((seq_count, samples * per // 2 + 8, HD), jnp.int32),
        in_specs=[SMEM, VMEM],
        out_specs=VMEM,
        compiler_params=params(4),
        name="select",
    )(slots, returned)
    gathered = lax.all_to_all(chosen, "seq", split_axis=0, concat_axis=0, tiled=True)

    return pl.pallas_call(
        combine_kernel,
        out_shape=shape((samples, steps, features), jnp.bfloat16),
        in_specs=[VMEM] * 3,
        out_specs=VMEM,
        compiler_params=params(6),
        name="combine",
    )(gathered, suffix_out, suffix_log)


def solution(mesh):
    return jax.shard_map(
        local,
        mesh=mesh,
        in_specs=(
            P(("engine", "seq"), None, None),
            P(("engine", "seq"), None, None),
            P(("engine", "seq"), None, None),
            P(("engine", "seq"), None, None),
            P(("engine", "seq"), None, None),
            P(("engine", "seq")),
            P(("engine", "seq"), None),
            P("engine", "seq", None),
            P("engine", "seq", None),
        ),
        out_specs=P(("engine", "seq"), None, None),
        check_vma=False,
    )
```

```python
import functools
import math

import jax
import jax.numpy as jnp
from jax import lax
from jax.experimental import pallas as pl
from jax.experimental.pallas import tpu as pltpu
from jax.sharding import PartitionSpec as P

KVH = 4
GROUP = 8
HD = 128
CAPE = 3
SCALING = HD ** (-0.5)
LOG2E = math.log2(math.e)
LSE_ONE = float(2**20)
VMEM = pl.BlockSpec(memory_space=pltpu.VMEM)
SMEM = pl.BlockSpec(memory_space=pltpu.SMEM)


def params(mib):
    return pltpu.CompilerParams(vmem_limit_bytes=mib * 1024 * 1024)


def shape(dims, dtype):
    return jax.ShapeDtypeStruct(dims, dtype)


def prepare_kernel(prompt_ref, queries_ref, rows_ref, payload_ref):
    samples, steps, features = queries_ref.shape
    heads = features // HD
    part = heads * steps // KVH
    extra = payload_ref.shape[1] - samples * part
    lanes = lax.broadcasted_iota(jnp.int32, (extra, HD), 1)
    note = jnp.zeros((extra, HD), jnp.int32)
    for sample in range(samples):
        note = jnp.where(lanes == sample, prompt_ref[sample], note)
    note = note.astype(jnp.float32).astype(jnp.bfloat16)
    for sample in range(samples):
        for first in range(0, heads, 4):
            tile = jnp.concatenate(
                [
                    queries_ref[sample, :, (first + i) * HD : (first + i + 1) * HD].astype(jnp.float32)
                    for i in range(4)
                ],
                axis=0,
            ).astype(jnp.bfloat16)
            row = first * steps
            rows_ref[sample, row : row + 4 * steps] = tile
            group, row = row // part, row % part
            for place in range(group, payload_ref.shape[0], KVH):
                payload_ref[place, sample * part + row : sample * part + row + 4 * steps] = tile
    for place in range(payload_ref.shape[0]):
        payload_ref[place, samples * part :] = note


def split_kernel(head_ref, k_ref, v_ref, *refs):
    outs, sems = refs[:-1], refs[-1]
    copies = []
    for place, out in enumerate(outs):
        head = jnp.bitwise_xor(head_ref[0], place)
        cols = pl.ds(pl.multiple_of(head * HD, HD), HD)
        for which, array in enumerate((k_ref, v_ref)):
            copies.append(
                pltpu.make_async_copy(array.at[0, :, cols], out.at[which], sems.at[place, which])
            )
    for copy in copies:
        copy.start()
    for copy in copies:
        copy.wait()


def pack_kernel(samples, _, received_ref, packed_ref, slots_ref, counts_ref):
    prompts, part = packed_ref.shape[0], packed_ref.shape[1] // CAPE
    packed_ref[...] = jnp.zeros(packed_ref.shape, packed_ref.dtype)
    for prompt in range(prompts):
        counts_ref[prompt] = 0
    for place in range(received_ref.shape[0]):
        note = received_ref[place, samples * part :].astype(jnp.float32).astype(jnp.int32)
        for sample in range(samples):
            prompt = note[0, sample]
            rank = counts_ref[prompt]
            counts_ref[prompt] = rank + 1
            slots_ref[place * samples + sample] = prompt * 4 + rank
            packed_ref[prompt, pl.ds(pl.multiple_of(rank * part, part), part)] = received_ref[
                place, sample * part : (sample + 1) * part
            ]


def block_scores(rows, keys):
    return lax.dot_general(rows, keys, (((1,), (1,)), ((), ())), preferred_element_type=jnp.float32)


def block_attention(raw, values):
    top = jnp.max(raw, axis=1, keepdims=True)
    probs = jnp.exp2((raw - top) * (SCALING * LOG2E))
    total = jnp.sum(probs, axis=1, keepdims=True)
    acc = jnp.dot(probs.astype(jnp.bfloat16), values, preferred_element_type=jnp.float32)
    return acc, top * (SCALING * LOG2E), total


def encode(out):
    largest = jnp.max(jnp.abs(out), axis=1, keepdims=True)
    power = jnp.floor(jnp.log2(jnp.maximum(largest, 2.0**-112) * 1.0001)) + 1.0
    code = jnp.clip(jnp.round(out * jnp.exp2(15.0 - power)), -32767.0, 32767.0)
    return code.astype(jnp.int32), power.astype(jnp.int32)


def prefix_kernel(chunk, q_ref, *refs):
    blocks, reply_ref = refs[:-1], refs[-1]
    slots, per = q_ref.shape[0], q_ref.shape[1]
    rows_of = per // 2

    def step(index, _):
        rows = q_ref[pl.ds(index * chunk, chunk)].reshape(chunk * per, HD)
        parts, raw = [], block_scores(rows, blocks[0][0])
        for place, block in enumerate(blocks):
            ready = raw
            if place + 1 < len(blocks):
                raw = block_scores(rows, blocks[place + 1][0])
            parts.append(block_attention(ready, block[1]))
        top = functools.reduce(jnp.maximum, [part[1] for part in parts])
        weights = [jnp.exp2(part[1] - top) for part in parts]
        total = functools.reduce(jnp.add, [w * part[2] for w, part in zip(weights, parts)])
        share = 1.0 / total
        out = functools.reduce(jnp.add, [(w * share) * part[0] for w, part in zip(weights, parts)])
        log = top + jnp.log2(total)
        code, power = encode(out)
        code = code.reshape(chunk, per, HD)
        packed = jnp.bitwise_or(
            jnp.left_shift(code[:, :rows_of], 16), jnp.bitwise_and(code[:, rows_of:], 0xFFFF)
        )
        row = lax.broadcasted_iota(jnp.int32, (chunk, per, HD), 1)
        lane = lax.broadcasted_iota(jnp.int32, (chunk, per, HD), 2)
        log = jnp.round(log * LSE_ONE).astype(jnp.int32).reshape(chunk, per, 1)
        note = jnp.where(lane == row, log, 0)
        note = jnp.where(lane == row + per, power.reshape(chunk, per, 1), note)
        note = jnp.sum(note, axis=1)
        for slot in range(chunk):
            dest, rank = index * (chunk // CAPE) + slot // CAPE, slot % CAPE
            for part in range(rows_of // 4):
                reply_ref[dest, rank * (rows_of // 4) + part] = packed[
                    slot, part * 4 : part * 4 + 4
                ]
            reply_ref[dest, CAPE * (rows_of // 4), rank : rank + 1] = note[slot : slot + 1]
        return 0

    lax.fori_loop(0, slots // chunk, step, 0)


def select_kernel(samples, slots_ref, reply_ref, chosen_ref):
    body = (chosen_ref.shape[1] - 1) // samples
    for sample in range(chosen_ref.shape[0] * samples):
        slot = slots_ref[sample]
        prompt, rank = lax.shift_right_logical(slot, 2), lax.bitwise_and(slot, 3)
        place, which = sample // samples, sample % samples
        chosen_ref[place, which * body : (which + 1) * body] = reply_ref[
            prompt, pl.ds(rank * body, body)
        ]
        chosen_ref[place, samples * body, which : which + 1] = reply_ref[
            prompt, CAPE * body, pl.ds(rank, 1)
        ]


def suffix_kernel(length_ref, rows_ref, fresh_k_ref, fresh_v_ref, k_ref, v_ref, out_ref, log_ref):
    samples, positions = k_ref.shape[0], k_ref.shape[1]
    fresh = 16

    def padded(array):
        rest = jnp.zeros((fresh - array.shape[0], HD), jnp.float32)
        return jnp.concatenate([array.astype(jnp.float32), rest], axis=0).astype(jnp.bfloat16)

    per = rows_ref.shape[1] // KVH
    steps = per // GROUP
    column = lax.broadcasted_iota(jnp.int32, (per, positions), 1)
    step = lax.rem(lax.broadcasted_iota(jnp.int32, (per, fresh), 0), steps)
    causal = lax.broadcasted_iota(jnp.int32, (per, fresh), 1) <= step
    for sample in range(samples):
        live = column < length_ref[sample]
        for group in range(KVH):
            cols = slice(group * HD, (group + 1) * HD)
            rows = rows_ref[sample, group * per : (group + 1) * per]
            dims = (((1,), (1,)), ((), ()))
            cache_raw = lax.dot_general(
                rows, k_ref[sample, :, cols], dims, preferred_element_type=jnp.float32
            )
            fresh_raw = lax.dot_general(
                rows, padded(fresh_k_ref[sample, :, cols]), dims, preferred_element_type=jnp.float32
            )
            cache_raw = jnp.where(live, cache_raw, -jnp.inf)
            fresh_raw = jnp.where(causal, fresh_raw, -jnp.inf)
            top = jnp.maximum(
                jnp.max(cache_raw, axis=1, keepdims=True), jnp.max(fresh_raw, axis=1, keepdims=True)
            )
            cache_probs = jnp.exp2((cache_raw - top) * (SCALING * LOG2E))
            fresh_probs = jnp.exp2((fresh_raw - top) * (SCALING * LOG2E))
            total = jnp.sum(cache_probs, axis=1, keepdims=True) + jnp.sum(
                fresh_probs, axis=1, keepdims=True
            )
            acc = jnp.dot(
                cache_probs.astype(jnp.bfloat16),
                v_ref[sample, :, cols],
                preferred_element_type=jnp.float32,
            ) + jnp.dot(
                fresh_probs.astype(jnp.bfloat16),
                padded(fresh_v_ref[sample, :, cols]),
                preferred_element_type=jnp.float32,
            )
            here = slice(group * per, (group + 1) * per)
            out_ref[sample, here] = acc / total
            log_ref[sample, here] = jnp.broadcast_to(
                top * (SCALING * LOG2E) + jnp.log2(total), (per, HD)
            )


def combine_kernel(chosen_ref, suffix_out_ref, suffix_log_ref, out_ref):
    places, samples = chosen_ref.shape[0], suffix_out_ref.shape[0]
    steps = out_ref.shape[1]
    body = (chosen_ref.shape[1] - 1) // samples
    per = 8 * body
    row = lax.broadcasted_iota(jnp.int32, (per, HD), 0)
    lane = lax.broadcasted_iota(jnp.int32, (per, HD), 1)

    def turn(note, offset):
        spread = jnp.broadcast_to(note, (per, HD))
        return jnp.sum(jnp.where(lane == row + offset, spread, 0.0), axis=1, keepdims=True)

    for sample in range(samples):
        for group in range(KVH):
            logs, scales, codes = [], [], []
            for place in range(group, places, KVH):
                packed = jnp.concatenate(
                    [chosen_ref[place, sample * body + part] for part in range(body)], axis=0
                )
                high = jnp.right_shift(packed, 16)
                low = jnp.right_shift(jnp.left_shift(packed, 16), 16)
                codes.append(jnp.concatenate([high, low], axis=0).astype(jnp.float32))
                note = chosen_ref[place, samples * body, sample : sample + 1].astype(jnp.float32)
                logs.append(turn(note, 0) * (1.0 / LSE_ONE))
                scales.append(jnp.exp2(turn(note, per) - 15.0))
            peak = functools.reduce(jnp.maximum, logs)
            weights = [jnp.exp2(log - peak) for log in logs]
            weight_sum = functools.reduce(jnp.add, weights)
            prefix = functools.reduce(
                jnp.add, [(w * s) * c for w, s, c in zip(weights, scales, codes)]
            )
            prefix_log = peak + jnp.log2(weight_sum)
            first = group * per
            suffix_log = suffix_log_ref[sample, first : first + per][:, 0:1]
            suffix = suffix_out_ref[sample, first : first + per]
            top = jnp.maximum(prefix_log, suffix_log)
            prefix_weight = jnp.exp2(prefix_log - top)
            suffix_weight = jnp.exp2(suffix_log - top)
            whole = prefix_weight + suffix_weight
            result = (prefix_weight / (weight_sum * whole)) * prefix + (
                suffix_weight / whole
            ) * suffix
            for i in range(per // steps):
                head = first // steps + i
                out_ref[sample, :, head * HD : (head + 1) * HD] = result[
                    i * steps : (i + 1) * steps
                ].astype(jnp.bfloat16)


def local(
    queries,
    new_keys,
    new_values,
    suffix_keys,
    suffix_values,
    suffix_len,
    sample_prompt,
    prefix_keys,
    prefix_values,
):
    samples, steps, features = queries.shape
    heads = features // HD
    per = GROUP * steps
    seq_count = lax.axis_size("seq")
    engine_count = lax.axis_size("engine")
    positions = prefix_keys.shape[1]

    head_id = lax.rem(lax.axis_index("seq"), KVH).reshape(1)
    heads_of_block = pl.pallas_call(
        split_kernel,
        out_shape=[shape((2, positions, HD), jnp.bfloat16)] * KVH,
        in_specs=[SMEM] + [pl.BlockSpec(memory_space=pltpu.HBM)] * 2,
        out_specs=[VMEM] * KVH,
        scratch_shapes=[pltpu.SemaphoreType.DMA((KVH, 2))],
        compiler_params=params(16),
        name="split",
    )(
        head_id,
        pltpu.with_memory_space_constraint(prefix_keys, pltpu.HBM),
        pltpu.with_memory_space_constraint(prefix_values, pltpu.HBM),
    )

    def swap(array, near, swapped):
        pairs = []
        for place in range(seq_count):
            chip, core = place // 2, place % 2
            chip = (chip + near * (2 * core - 1)) % (seq_count // 2)
            pairs.append((place, 2 * chip + (1 - core if swapped else core)))
        return lax.ppermute(array, "seq", pairs)

    blocks = [
        heads_of_block[0],
        swap(heads_of_block[1], 0, True),
        swap(heads_of_block[2], 1, False),
        swap(heads_of_block[3], 1, True),
    ]

    rows, payload = pl.pallas_call(
        prepare_kernel,
        out_shape=(
            shape((samples, heads * steps, HD), jnp.bfloat16),
            shape((seq_count, samples * per + 8, HD), jnp.bfloat16),
        ),
        in_specs=[SMEM, VMEM],
        out_specs=(VMEM, VMEM),
        name="prepare",
    )(sample_prompt.reshape(samples), queries)
    received = lax.all_to_all(payload, "seq", split_axis=0, concat_axis=0, tiled=True)

    suffix_out, suffix_log = pl.pallas_call(
        suffix_kernel,
        out_shape=(
            shape((samples, heads * steps, HD), jnp.float32),
            shape((samples, heads * steps, HD), jnp.float32),
        ),
        in_specs=[SMEM] + [VMEM] * 5,
        out_specs=(VMEM, VMEM),
        compiler_params=params(16),
        name="suffix",
    )(
        suffix_len,
        rows,
        new_keys,
        new_values,
        suffix_keys,
        suffix_values,
    )

    suffix_out, suffix_log = pl.pallas_call(
        suffix_kernel,
        out_shape=(
            shape((samples, heads * steps, HD), jnp.float32),
            shape((samples, heads * steps, HD), jnp.float32),
        ),
        in_specs=[SMEM] + [VMEM] * 5,
        out_specs=(VMEM, VMEM),
        compiler_params=params(16),
        name="suffix",
    )(
        suffix_len,
        rows,
        new_keys,
        new_values,
        suffix_keys,
        suffix_values,
    )

    packed, slots = pl.pallas_call(
        functools.partial(pack_kernel, samples),
        out_shape=(
            pltpu.HBM((engine_count, CAPE * per, HD), jnp.bfloat16),
            shape((seq_count * samples,), jnp.int32),
        ),
        in_specs=[pl.BlockSpec(memory_space=pl.ANY), VMEM],
        out_specs=(VMEM, SMEM),
        scratch_shapes=[pltpu.SMEM((engine_count,), jnp.int32)],
        compiler_params=params(16),
        name="pack",
    )(suffix_log, received)
    dispatched = lax.all_to_all(packed, "engine", split_axis=0, concat_axis=0, tiled=True)

    reply = pl.pallas_call(
        functools.partial(prefix_kernel, 8 * CAPE),
        out_shape=shape((engine_count, CAPE * per // 8 + 1, 4, HD), jnp.int32),
        in_specs=[VMEM] * (1 + KVH),
        out_specs=VMEM,
        compiler_params=params(16),
        name="prefix",
    )(
        dispatched.reshape(engine_count * CAPE, per, HD),
        *[pltpu.with_memory_space_constraint(block, pltpu.VMEM) for block in blocks],
    )
    returned = lax.all_to_all(reply, "engine", split_axis=0, concat_axis=0, tiled=True)

    chosen = pl.pallas_call(
        functools.partial(select_kernel, samples),
        out_shape=shape((seq_count, samples * per // 8 + 1, 4, HD), jnp.int32),
        in_specs=[SMEM, VMEM],
        out_specs=VMEM,
        compiler_params=params(16),
        name="select",
    )(slots, returned)
    gathered = lax.all_to_all(chosen, "seq", split_axis=0, concat_axis=0, tiled=True)

    return pl.pallas_call(
        combine_kernel,
        out_shape=shape((samples, steps, features), jnp.bfloat16),
        in_specs=[VMEM] * 3,
        out_specs=VMEM,
        compiler_params=params(16),
        name="combine",
    )(gathered, suffix_out, suffix_log)


def solution(mesh):
    return jax.shard_map(
        local,
        mesh=mesh,
        in_specs=(
            P(("engine", "seq"), None, None),
            P(("engine", "seq"), None, None),
            P(("engine", "seq"), None, None),
            P(("engine", "seq"), None, None),
            P(("engine", "seq"), None, None),
            P(("engine", "seq")),
            P(("engine", "seq"), None),
            P("engine", "seq", None),
            P("engine", "seq", None),
        ),
        out_specs=P(("engine", "seq"), None, None),
        check_vma=False,
    )
```

```python
import functools
import math

import jax
import jax.numpy as jnp
from jax import lax
from jax.experimental import pallas as pl
from jax.experimental.pallas import tpu as pltpu
from jax.sharding import PartitionSpec as P

KVH = 4
GROUP = 8
HD = 128
CAPE = 3
SCALING = HD ** (-0.5)
LOG2E = math.log2(math.e)
LSE_ONE = float(2**20)
VMEM = pl.BlockSpec(memory_space=pltpu.VMEM)
SMEM = pl.BlockSpec(memory_space=pltpu.SMEM)


def params(mib):
    return pltpu.CompilerParams(vmem_limit_bytes=mib * 1024 * 1024)


def shape(dims, dtype):
    return jax.ShapeDtypeStruct(dims, dtype)


def prepare_kernel(prompt_ref, queries_ref, rows_ref, payload_ref):
    samples, steps, features = queries_ref.shape
    heads = features // HD
    part = heads * steps // KVH
    extra = payload_ref.shape[1] - samples * part
    lanes = lax.broadcasted_iota(jnp.int32, (extra, HD), 1)
    note = jnp.zeros((extra, HD), jnp.int32)
    for sample in range(samples):
        note = jnp.where(lanes == sample, prompt_ref[sample], note)
    note = note.astype(jnp.float32).astype(jnp.bfloat16)
    for sample in range(samples):
        for first in range(0, heads, 4):
            tile = jnp.concatenate(
                [
                    queries_ref[sample, :, (first + i) * HD : (first + i + 1) * HD].astype(jnp.float32)
                    for i in range(4)
                ],
                axis=0,
            ).astype(jnp.bfloat16)
            row = first * steps
            rows_ref[sample, row : row + 4 * steps] = tile
            group, row = row // part, row % part
            for place in range(group, payload_ref.shape[0], KVH):
                payload_ref[place, sample * part + row : sample * part + row + 4 * steps] = tile
    for place in range(payload_ref.shape[0]):
        payload_ref[place, samples * part :] = note


def split_kernel(head_ref, k_ref, v_ref, *refs):
    outs, held, sems = refs[:KVH], refs[KVH], refs[KVH + 1]
    copies = []
    for place, out in enumerate(outs):
        head = jnp.bitwise_xor(head_ref[0], place)
        cols = pl.ds(pl.multiple_of(head * HD, HD), HD)
        keys = pltpu.make_async_copy(k_ref.at[0, :, cols], out.at[0], sems.at[place, 0])
        values = pltpu.make_async_copy(v_ref.at[0, :, cols], held.at[place], sems.at[place, 1])
        copies.append((keys, values))
    for keys, values in copies:
        values.start()
    for keys, values in copies:
        keys.start()
    for place, out in enumerate(outs):
        copies[place][1].wait()
        for first in range(0, held.shape[1], HD):
            out[1, first : first + HD] = held[place, first : first + HD].T
    for keys, values in copies:
        keys.wait()


def pack_kernel(samples, _, received_ref, packed_ref, slots_ref, counts_ref):
    prompts, part = packed_ref.shape[0], packed_ref.shape[1] // CAPE
    packed_ref[...] = jnp.zeros(packed_ref.shape, packed_ref.dtype)
    for prompt in range(prompts):
        counts_ref[prompt] = 0
    for place in range(received_ref.shape[0]):
        note = received_ref[place, samples * part :].astype(jnp.float32).astype(jnp.int32)
        for sample in range(samples):
            prompt = note[0, sample]
            rank = counts_ref[prompt]
            counts_ref[prompt] = rank + 1
            slots_ref[place * samples + sample] = prompt * 4 + rank
            packed_ref[prompt, pl.ds(pl.multiple_of(rank * part, part), part)] = received_ref[
                place, sample * part : (sample + 1) * part
            ]


def block_scores(rows, keys):
    return lax.dot_general(keys, rows, (((1,), (1,)), ((), ())), preferred_element_type=jnp.float32)


def block_attention(raw, values):
    values = jnp.concatenate(
        [values[first : first + HD] for first in range(0, values.shape[0], HD)], axis=1
    )
    top = jnp.max(raw, axis=0, keepdims=True)
    probs = jnp.exp2((raw - top) * (SCALING * LOG2E))
    total = jnp.sum(probs, axis=0, keepdims=True)
    acc = jnp.dot(values, probs.astype(jnp.bfloat16), preferred_element_type=jnp.float32)
    return acc, top * (SCALING * LOG2E), total


def encode(out):
    largest = jnp.max(jnp.abs(out), axis=0, keepdims=True)
    power = jnp.floor(jnp.log2(jnp.maximum(largest, 2.0**-112) * 1.0001)) + 1.0
    code = jnp.clip(jnp.round(out * jnp.exp2(15.0 - power)), -32767.0, 32767.0)
    return code.astype(jnp.int32), power.astype(jnp.int32)


def prefix_kernel(chunk, q_ref, *refs):
    blocks, reply_ref = refs[:-1], refs[-1]
    slots, per = q_ref.shape[0], q_ref.shape[1]
    rows_of = per // 2
    wide = chunk * rows_of

    def step(index, _):
        here = pl.ds(index * chunk, chunk)
        rows = jnp.concatenate(
            [
                q_ref[here, 0:rows_of].reshape(wide, HD),
                q_ref[here, rows_of:per].reshape(wide, HD),
            ],
            axis=0,
        )
        parts, raw = [], block_scores(rows, blocks[0][0])
        for place, block in enumerate(blocks):
            ready = raw
            if place + 1 < len(blocks):
                raw = block_scores(rows, blocks[place + 1][0])
            parts.append(block_attention(ready, block[1]))
        top = functools.reduce(jnp.maximum, [part[1] for part in parts])
        weights = [jnp.exp2(part[1] - top) for part in parts]
        total = functools.reduce(jnp.add, [w * part[2] for w, part in zip(weights, parts)])
        share = 1.0 / total
        out = functools.reduce(jnp.add, [(w * share) * part[0] for w, part in zip(weights, parts)])
        log = jnp.round((top + jnp.log2(total)) * LSE_ONE).astype(jnp.int32)
        code, power = encode(out)
        packed = jnp.bitwise_or(
            jnp.left_shift(code[:, :wide], 16), jnp.bitwise_and(code[:, wide:], 0xFFFF)
        ).T
        rest = jnp.zeros((1, HD - 2 * per), jnp.int32)
        for slot in range(chunk):
            dest, rank = index * (chunk // CAPE) + slot // CAPE, slot % CAPE
            first = slot * rows_of
            for part in range(rows_of // 4):
                reply_ref[dest, rank * (rows_of // 4) + part] = packed[
                    first + part * 4 : first + part * 4 + 4
                ]
            pieces = [
                array[:, start : start + rows_of]
                for array in (log, power)
                for start in (first, wide + first)
            ]
            reply_ref[dest, CAPE * (rows_of // 4), rank : rank + 1] = jnp.concatenate(
                pieces + [rest], axis=1
            )
        return 0

    lax.fori_loop(0, slots // chunk, step, 0)


def select_kernel(samples, slots_ref, reply_ref, chosen_ref):
    body = (chosen_ref.shape[1] - 1) // samples
    for sample in range(chosen_ref.shape[0] * samples):
        slot = slots_ref[sample]
        prompt, rank = lax.shift_right_logical(slot, 2), lax.bitwise_and(slot, 3)
        place, which = sample // samples, sample % samples
        chosen_ref[place, which * body : (which + 1) * body] = reply_ref[
            prompt, pl.ds(rank * body, body)
        ]
        chosen_ref[place, samples * body, which : which + 1] = reply_ref[
            prompt, CAPE * body, pl.ds(rank, 1)
        ]


def suffix_kernel(length_ref, rows_ref, fresh_k_ref, fresh_v_ref, k_ref, v_ref, out_ref, log_ref):
    samples, positions = k_ref.shape[0], k_ref.shape[1]
    fresh = 16

    def padded(array):
        rest = jnp.zeros((fresh - array.shape[0], HD), jnp.float32)
        return jnp.concatenate([array.astype(jnp.float32), rest], axis=0).astype(jnp.bfloat16)

    per = rows_ref.shape[1] // KVH
    steps = per // GROUP
    column = lax.broadcasted_iota(jnp.int32, (per, positions), 1)
    step = lax.rem(lax.broadcasted_iota(jnp.int32, (per, fresh), 0), steps)
    causal = lax.broadcasted_iota(jnp.int32, (per, fresh), 1) <= step
    for sample in range(samples):
        live = column < length_ref[sample]
        for group in range(KVH):
            cols = slice(group * HD, (group + 1) * HD)
            rows = rows_ref[sample, group * per : (group + 1) * per]
            dims = (((1,), (1,)), ((), ()))
            cache_raw = lax.dot_general(
                rows, k_ref[sample, :, cols], dims, preferred_element_type=jnp.float32
            )
            fresh_raw = lax.dot_general(
                rows, padded(fresh_k_ref[sample, :, cols]), dims, preferred_element_type=jnp.float32
            )
            cache_raw = jnp.where(live, cache_raw, -jnp.inf)
            fresh_raw = jnp.where(causal, fresh_raw, -jnp.inf)
            top = jnp.maximum(
                jnp.max(cache_raw, axis=1, keepdims=True), jnp.max(fresh_raw, axis=1, keepdims=True)
            )
            cache_probs = jnp.exp2((cache_raw - top) * (SCALING * LOG2E))
            fresh_probs = jnp.exp2((fresh_raw - top) * (SCALING * LOG2E))
            total = jnp.sum(cache_probs, axis=1, keepdims=True) + jnp.sum(
                fresh_probs, axis=1, keepdims=True
            )
            acc = jnp.dot(
                cache_probs.astype(jnp.bfloat16),
                v_ref[sample, :, cols],
                preferred_element_type=jnp.float32,
            ) + jnp.dot(
                fresh_probs.astype(jnp.bfloat16),
                padded(fresh_v_ref[sample, :, cols]),
                preferred_element_type=jnp.float32,
            )
            here = slice(group * per, (group + 1) * per)
            out_ref[sample, here] = acc / total
            log_ref[sample, here] = jnp.broadcast_to(
                top * (SCALING * LOG2E) + jnp.log2(total), (per, HD)
            )


def combine_kernel(chosen_ref, suffix_out_ref, suffix_log_ref, out_ref):
    places, samples = chosen_ref.shape[0], suffix_out_ref.shape[0]
    steps = out_ref.shape[1]
    body = (chosen_ref.shape[1] - 1) // samples
    per = 8 * body
    row = lax.broadcasted_iota(jnp.int32, (per, HD), 0)
    lane = lax.broadcasted_iota(jnp.int32, (per, HD), 1)

    def turn(note, offset):
        spread = jnp.broadcast_to(note, (per, HD))
        return jnp.sum(jnp.where(lane == row + offset, spread, 0.0), axis=1, keepdims=True)

    for sample in range(samples):
        for group in range(KVH):
            logs, scales, codes = [], [], []
            for place in range(group, places, KVH):
                packed = jnp.concatenate(
                    [chosen_ref[place, sample * body + part] for part in range(body)], axis=0
                )
                high = jnp.right_shift(packed, 16)
                low = jnp.right_shift(jnp.left_shift(packed, 16), 16)
                codes.append(jnp.concatenate([high, low], axis=0).astype(jnp.float32))
                note = chosen_ref[place, samples * body, sample : sample + 1].astype(jnp.float32)
                logs.append(turn(note, 0) * (1.0 / LSE_ONE))
                scales.append(jnp.exp2(turn(note, per) - 15.0))
            peak = functools.reduce(jnp.maximum, logs)
            weights = [jnp.exp2(log - peak) for log in logs]
            weight_sum = functools.reduce(jnp.add, weights)
            prefix = functools.reduce(
                jnp.add, [(w * s) * c for w, s, c in zip(weights, scales, codes)]
            )
            prefix_log = peak + jnp.log2(weight_sum)
            first = group * per
            suffix_log = suffix_log_ref[sample, first : first + per][:, 0:1]
            suffix = suffix_out_ref[sample, first : first + per]
            top = jnp.maximum(prefix_log, suffix_log)
            prefix_weight = jnp.exp2(prefix_log - top)
            suffix_weight = jnp.exp2(suffix_log - top)
            whole = prefix_weight + suffix_weight
            result = (prefix_weight / (weight_sum * whole)) * prefix + (
                suffix_weight / whole
            ) * suffix
            for i in range(per // steps):
                head = first // steps + i
                out_ref[sample, :, head * HD : (head + 1) * HD] = result[
                    i * steps : (i + 1) * steps
                ].astype(jnp.bfloat16)


def local(
    queries,
    new_keys,
    new_values,
    suffix_keys,
    suffix_values,
    suffix_len,
    sample_prompt,
    prefix_keys,
    prefix_values,
):
    samples, steps, features = queries.shape
    heads = features // HD
    per = GROUP * steps
    seq_count = lax.axis_size("seq")
    engine_count = lax.axis_size("engine")
    positions = prefix_keys.shape[1]

    head_id = lax.rem(lax.axis_index("seq"), KVH).reshape(1)
    heads_of_block = pl.pallas_call(
        split_kernel,
        out_shape=[shape((2, positions, HD), jnp.bfloat16)] * KVH,
        in_specs=[SMEM] + [pl.BlockSpec(memory_space=pltpu.HBM)] * 2,
        out_specs=[VMEM] * KVH,
        scratch_shapes=[
            pltpu.VMEM((KVH, positions, HD), jnp.bfloat16),
            pltpu.SemaphoreType.DMA((KVH, 2)),
        ],
        compiler_params=params(16),
        name="split",
    )(
        head_id,
        pltpu.with_memory_space_constraint(prefix_keys, pltpu.HBM),
        pltpu.with_memory_space_constraint(prefix_values, pltpu.HBM),
    )

    def swap(array, near, swapped):
        pairs = []
        for place in range(seq_count):
            chip, core = place // 2, place % 2
            chip = (chip + near * (2 * core - 1)) % (seq_count // 2)
            pairs.append((place, 2 * chip + (1 - core if swapped else core)))
        return lax.ppermute(array, "seq", pairs)

    blocks = [
        heads_of_block[0],
        swap(heads_of_block[1], 0, True),
        swap(heads_of_block[2], 1, False),
        swap(heads_of_block[3], 1, True),
    ]

    rows, payload = pl.pallas_call(
        prepare_kernel,
        out_shape=(
            shape((samples, heads * steps, HD), jnp.bfloat16),
            shape((seq_count, samples * per + 8, HD), jnp.bfloat16),
        ),
        in_specs=[SMEM, VMEM],
        out_specs=(VMEM, VMEM),
        name="prepare",
    )(sample_prompt.reshape(samples), queries)
    received = lax.all_to_all(payload, "seq", split_axis=0, concat_axis=0, tiled=True)

    suffix_out, suffix_log = pl.pallas_call(
        suffix_kernel,
        out_shape=(
            shape((samples, heads * steps, HD), jnp.float32),
            shape((samples, heads * steps, HD), jnp.float32),
        ),
        in_specs=[SMEM] + [VMEM] * 5,
        out_specs=(VMEM, VMEM),
        compiler_params=params(16),
        name="suffix",
    )(
        suffix_len,
        rows,
        new_keys,
        new_values,
        suffix_keys,
        suffix_values,
    )

    suffix_out, suffix_log = pl.pallas_call(
        suffix_kernel,
        out_shape=(
            shape((samples, heads * steps, HD), jnp.float32),
            shape((samples, heads * steps, HD), jnp.float32),
        ),
        in_specs=[SMEM] + [VMEM] * 5,
        out_specs=(VMEM, VMEM),
        compiler_params=params(16),
        name="suffix",
    )(
        suffix_len,
        rows,
        new_keys,
        new_values,
        suffix_keys,
        suffix_values,
    )

    packed, slots = pl.pallas_call(
        functools.partial(pack_kernel, samples),
        out_shape=(
            pltpu.HBM((engine_count, CAPE * per, HD), jnp.bfloat16),
            shape((seq_count * samples,), jnp.int32),
        ),
        in_specs=[pl.BlockSpec(memory_space=pl.ANY), VMEM],
        out_specs=(VMEM, SMEM),
        scratch_shapes=[pltpu.SMEM((engine_count,), jnp.int32)],
        compiler_params=params(16),
        name="pack",
    )(suffix_log, received)
    dispatched = lax.all_to_all(packed, "engine", split_axis=0, concat_axis=0, tiled=True)

    reply = pl.pallas_call(
        functools.partial(prefix_kernel, 8 * CAPE),
        out_shape=shape((engine_count, CAPE * per // 8 + 1, 4, HD), jnp.int32),
        in_specs=[VMEM] * (1 + KVH),
        out_specs=VMEM,
        compiler_params=params(16),
        name="prefix",
    )(
        dispatched.reshape(engine_count * CAPE, per, HD),
        *[pltpu.with_memory_space_constraint(block, pltpu.VMEM) for block in blocks],
    )
    returned = lax.all_to_all(reply, "engine", split_axis=0, concat_axis=0, tiled=True)

    chosen = pl.pallas_call(
        functools.partial(select_kernel, samples),
        out_shape=shape((seq_count, samples * per // 8 + 1, 4, HD), jnp.int32),
        in_specs=[SMEM, VMEM],
        out_specs=VMEM,
        compiler_params=params(16),
        name="select",
    )(slots, returned)
    gathered = lax.all_to_all(chosen, "seq", split_axis=0, concat_axis=0, tiled=True)

    return pl.pallas_call(
        combine_kernel,
        out_shape=shape((samples, steps, features), jnp.bfloat16),
        in_specs=[VMEM] * 3,
        out_specs=VMEM,
        compiler_params=params(16),
        name="combine",
    )(gathered, suffix_out, suffix_log)


def solution(mesh):
    return jax.shard_map(
        local,
        mesh=mesh,
        in_specs=(
            P(("engine", "seq"), None, None),
            P(("engine", "seq"), None, None),
            P(("engine", "seq"), None, None),
            P(("engine", "seq"), None, None),
            P(("engine", "seq"), None, None),
            P(("engine", "seq")),
            P(("engine", "seq"), None),
            P("engine", "seq", None),
            P("engine", "seq", None),
        ),
        out_specs=P(("engine", "seq"), None, None),
        check_vma=False,
    )
```

```python
import functools
import math

import jax
import jax.numpy as jnp
from jax import lax
from jax.experimental import pallas as pl
from jax.experimental.pallas import tpu as pltpu
from jax.sharding import PartitionSpec as P

KVH = 4
GROUP = 8
HD = 128
CAPE = 3
SCALING = HD ** (-0.5)
LOG2E = math.log2(math.e)
LSE_ONE = float(2**20)
VMEM = pl.BlockSpec(memory_space=pltpu.VMEM)
SMEM = pl.BlockSpec(memory_space=pltpu.SMEM)


def params(mib):
    return pltpu.CompilerParams(vmem_limit_bytes=mib * 1024 * 1024)


def shape(dims, dtype):
    return jax.ShapeDtypeStruct(dims, dtype)


def prepare_kernel(prompt_ref, queries_ref, rows_ref, payload_ref):
    samples, steps, features = queries_ref.shape
    heads = features // HD
    part = heads * steps // KVH
    extra = payload_ref.shape[1] - samples * part
    lanes = lax.broadcasted_iota(jnp.int32, (extra, HD), 1)
    note = jnp.zeros((extra, HD), jnp.int32)
    for sample in range(samples):
        note = jnp.where(lanes == sample, prompt_ref[sample], note)
    note = note.astype(jnp.float32).astype(jnp.bfloat16)
    for sample in range(samples):
        for first in range(0, heads, 4):
            tile = jnp.concatenate(
                [
                    queries_ref[sample, :, (first + i) * HD : (first + i + 1) * HD].astype(jnp.float32)
                    for i in range(4)
                ],
                axis=0,
            ).astype(jnp.bfloat16)
            row = first * steps
            rows_ref[sample, row : row + 4 * steps] = tile
            group, row = row // part, row % part
            for place in range(group, payload_ref.shape[0], KVH):
                payload_ref[place, sample * part + row : sample * part + row + 4 * steps] = tile
    for place in range(payload_ref.shape[0]):
        payload_ref[place, samples * part :] = note


def split_kernel(head_ref, k_ref, v_ref, *refs):
    outs, held, sems = refs[:KVH], refs[KVH], refs[KVH + 1]
    copies = []
    for place, out in enumerate(outs):
        head = jnp.bitwise_xor(head_ref[0], place)
        cols = pl.ds(pl.multiple_of(head * HD, HD), HD)
        keys = pltpu.make_async_copy(k_ref.at[0, :, cols], out.at[0], sems.at[place, 0])
        values = pltpu.make_async_copy(v_ref.at[0, :, cols], held.at[place], sems.at[place, 1])
        copies.append((keys, values))
    for keys, values in copies:
        values.start()
    for keys, values in copies:
        keys.start()
    for place, out in enumerate(outs):
        copies[place][1].wait()
        for first in range(0, held.shape[1], HD):
            out[1, first : first + HD] = held[place, first : first + HD].T
    for keys, values in copies:
        keys.wait()


def pack_kernel(samples, _, received_ref, packed_ref, slots_ref, counts_ref):
    prompts, part = packed_ref.shape[0], packed_ref.shape[1] // CAPE
    packed_ref[...] = jnp.zeros(packed_ref.shape, packed_ref.dtype)
    for prompt in range(prompts):
        counts_ref[prompt] = 0
    for place in range(received_ref.shape[0]):
        note = received_ref[place, samples * part :].astype(jnp.float32).astype(jnp.int32)
        for sample in range(samples):
            prompt = note[0, sample]
            rank = counts_ref[prompt]
            counts_ref[prompt] = rank + 1
            slots_ref[place * samples + sample] = prompt * 4 + rank
            packed_ref[prompt, pl.ds(pl.multiple_of(rank * part, part), part)] = received_ref[
                place, sample * part : (sample + 1) * part
            ]


def block_scores(rows, keys):
    return lax.dot_general(keys, rows, (((1,), (1,)), ((), ())), preferred_element_type=jnp.float32)


def block_attention(raw, values):
    values = jnp.concatenate(
        [values[first : first + HD] for first in range(0, values.shape[0], HD)], axis=1
    )
    top = jnp.max(raw, axis=0, keepdims=True)
    probs = jnp.exp2((raw - top) * (SCALING * LOG2E))
    total = jnp.sum(probs, axis=0, keepdims=True)
    acc = jnp.dot(values, probs.astype(jnp.bfloat16), preferred_element_type=jnp.float32)
    return acc, top * (SCALING * LOG2E), total


def encode(out):
    largest = jnp.max(jnp.abs(out), axis=0, keepdims=True)
    power = jnp.floor(jnp.log2(jnp.maximum(largest, 2.0**-112) * 1.0001)) + 1.0
    code = jnp.clip(jnp.round(out * jnp.exp2(15.0 - power)), -32767.0, 32767.0)
    return code.astype(jnp.int32), power.astype(jnp.int32)


def prefix_kernel(chunk, q_ref, *refs):
    blocks, reply_ref = refs[:-1], refs[-1]
    slots, per = q_ref.shape[0], q_ref.shape[1]
    rows_of = per // 2
    wide = chunk * rows_of

    def rows_from(start):
        return jnp.concatenate(
            [
                q_ref[start : start + chunk, 0:rows_of].reshape(wide, HD),
                q_ref[start : start + chunk, rows_of:per].reshape(wide, HD),
            ],
            axis=0,
        )

    def finish(start, parts):
        top = functools.reduce(jnp.maximum, [part[1] for part in parts])
        weights = [jnp.exp2(part[1] - top) for part in parts]
        total = functools.reduce(jnp.add, [w * part[2] for w, part in zip(weights, parts)])
        share = 1.0 / total
        out = functools.reduce(jnp.add, [(w * share) * part[0] for w, part in zip(weights, parts)])
        log = jnp.round((top + jnp.log2(total)) * LSE_ONE).astype(jnp.int32)
        code, power = encode(out)
        packed = jnp.bitwise_or(
            jnp.left_shift(code[:, :wide], 16), jnp.bitwise_and(code[:, wide:], 0xFFFF)
        ).T
        rest = jnp.zeros((1, HD - 2 * per), jnp.int32)
        for slot in range(chunk):
            dest, rank = (start + slot) // CAPE, (start + slot) % CAPE
            first = slot * rows_of
            for part in range(rows_of // 4):
                reply_ref[dest, rank * (rows_of // 4) + part] = packed[
                    first + part * 4 : first + part * 4 + 4
                ]
            pieces = [
                array[:, begin : begin + rows_of]
                for array in (log, power)
                for begin in (first, wide + first)
            ]
            reply_ref[dest, CAPE * (rows_of // 4), rank : rank + 1] = jnp.concatenate(
                pieces + [rest], axis=1
            )

    starts = range(0, slots, chunk)
    stages = [(start, place) for start in starts for place in range(len(blocks))]
    rows = {start: rows_from(start) for start in starts}
    raw, parts = block_scores(rows[0], blocks[0][0]), []
    for number, (start, place) in enumerate(stages):
        ready = raw
        if number + 1 < len(stages):
            later, block = stages[number + 1]
            raw = block_scores(rows[later], blocks[block][0])
        parts.append(block_attention(ready, blocks[place][1]))
        if place + 1 == len(blocks):
            finish(start, parts)
            parts = []


def select_kernel(samples, slots_ref, reply_ref, chosen_ref):
    body = (chosen_ref.shape[1] - 1) // samples
    for sample in range(chosen_ref.shape[0] * samples):
        slot = slots_ref[sample]
        prompt, rank = lax.shift_right_logical(slot, 2), lax.bitwise_and(slot, 3)
        place, which = sample // samples, sample % samples
        chosen_ref[place, which * body : (which + 1) * body] = reply_ref[
            prompt, pl.ds(rank * body, body)
        ]
        chosen_ref[place, samples * body, which : which + 1] = reply_ref[
            prompt, CAPE * body, pl.ds(rank, 1)
        ]


def suffix_kernel(length_ref, rows_ref, fresh_k_ref, fresh_v_ref, k_ref, v_ref, out_ref, log_ref):
    samples, positions = k_ref.shape[0], k_ref.shape[1]
    fresh = 16

    def padded(array):
        rest = jnp.zeros((fresh - array.shape[0], HD), jnp.float32)
        return jnp.concatenate([array.astype(jnp.float32), rest], axis=0).astype(jnp.bfloat16)

    per = rows_ref.shape[1] // KVH
    steps = per // GROUP
    column = lax.broadcasted_iota(jnp.int32, (per, positions), 1)
    step = lax.rem(lax.broadcasted_iota(jnp.int32, (per, fresh), 0), steps)
    causal = lax.broadcasted_iota(jnp.int32, (per, fresh), 1) <= step
    for sample in range(samples):
        live = column < length_ref[sample]
        for group in range(KVH):
            cols = slice(group * HD, (group + 1) * HD)
            rows = rows_ref[sample, group * per : (group + 1) * per]
            dims = (((1,), (1,)), ((), ()))
            cache_raw = lax.dot_general(
                rows, k_ref[sample, :, cols], dims, preferred_element_type=jnp.float32
            )
            fresh_raw = lax.dot_general(
                rows, padded(fresh_k_ref[sample, :, cols]), dims, preferred_element_type=jnp.float32
            )
            cache_raw = jnp.where(live, cache_raw, -jnp.inf)
            fresh_raw = jnp.where(causal, fresh_raw, -jnp.inf)
            top = jnp.maximum(
                jnp.max(cache_raw, axis=1, keepdims=True), jnp.max(fresh_raw, axis=1, keepdims=True)
            )
            cache_probs = jnp.exp2((cache_raw - top) * (SCALING * LOG2E))
            fresh_probs = jnp.exp2((fresh_raw - top) * (SCALING * LOG2E))
            total = jnp.sum(cache_probs, axis=1, keepdims=True) + jnp.sum(
                fresh_probs, axis=1, keepdims=True
            )
            acc = jnp.dot(
                cache_probs.astype(jnp.bfloat16),
                v_ref[sample, :, cols],
                preferred_element_type=jnp.float32,
            ) + jnp.dot(
                fresh_probs.astype(jnp.bfloat16),
                padded(fresh_v_ref[sample, :, cols]),
                preferred_element_type=jnp.float32,
            )
            here = slice(group * per, (group + 1) * per)
            out_ref[sample, here] = acc / total
            log_ref[sample, here] = jnp.broadcast_to(
                top * (SCALING * LOG2E) + jnp.log2(total), (per, HD)
            )


def combine_kernel(chosen_ref, suffix_out_ref, suffix_log_ref, out_ref):
    places, samples = chosen_ref.shape[0], suffix_out_ref.shape[0]
    steps = out_ref.shape[1]
    body = (chosen_ref.shape[1] - 1) // samples
    per = 8 * body
    row = lax.broadcasted_iota(jnp.int32, (per, HD), 0)
    lane = lax.broadcasted_iota(jnp.int32, (per, HD), 1)

    def turn(note, offset):
        spread = jnp.broadcast_to(note, (per, HD))
        return jnp.sum(jnp.where(lane == row + offset, spread, 0.0), axis=1, keepdims=True)

    for sample in range(samples):
        for group in range(KVH):
            logs, scales, codes = [], [], []
            for place in range(group, places, KVH):
                packed = jnp.concatenate(
                    [chosen_ref[place, sample * body + part] for part in range(body)], axis=0
                )
                high = jnp.right_shift(packed, 16)
                low = jnp.right_shift(jnp.left_shift(packed, 16), 16)
                codes.append(jnp.concatenate([high, low], axis=0).astype(jnp.float32))
                note = chosen_ref[place, samples * body, sample : sample + 1].astype(jnp.float32)
                logs.append(turn(note, 0) * (1.0 / LSE_ONE))
                scales.append(jnp.exp2(turn(note, per) - 15.0))
            peak = functools.reduce(jnp.maximum, logs)
            weights = [jnp.exp2(log - peak) for log in logs]
            weight_sum = functools.reduce(jnp.add, weights)
            prefix = functools.reduce(
                jnp.add, [(w * s) * c for w, s, c in zip(weights, scales, codes)]
            )
            prefix_log = peak + jnp.log2(weight_sum)
            first = group * per
            suffix_log = suffix_log_ref[sample, first : first + per][:, 0:1]
            suffix = suffix_out_ref[sample, first : first + per]
            top = jnp.maximum(prefix_log, suffix_log)
            prefix_weight = jnp.exp2(prefix_log - top)
            suffix_weight = jnp.exp2(suffix_log - top)
            whole = prefix_weight + suffix_weight
            result = (prefix_weight / (weight_sum * whole)) * prefix + (
                suffix_weight / whole
            ) * suffix
            for i in range(per // steps):
                head = first // steps + i
                out_ref[sample, :, head * HD : (head + 1) * HD] = result[
                    i * steps : (i + 1) * steps
                ].astype(jnp.bfloat16)


def local(
    queries,
    new_keys,
    new_values,
    suffix_keys,
    suffix_values,
    suffix_len,
    sample_prompt,
    prefix_keys,
    prefix_values,
):
    samples, steps, features = queries.shape
    heads = features // HD
    per = GROUP * steps
    seq_count = lax.axis_size("seq")
    engine_count = lax.axis_size("engine")
    positions = prefix_keys.shape[1]

    head_id = lax.rem(lax.axis_index("seq"), KVH).reshape(1)
    heads_of_block = pl.pallas_call(
        split_kernel,
        out_shape=[shape((2, positions, HD), jnp.bfloat16)] * KVH,
        in_specs=[SMEM] + [pl.BlockSpec(memory_space=pltpu.HBM)] * 2,
        out_specs=[VMEM] * KVH,
        scratch_shapes=[
            pltpu.VMEM((KVH, positions, HD), jnp.bfloat16),
            pltpu.SemaphoreType.DMA((KVH, 2)),
        ],
        compiler_params=params(16),
        name="split",
    )(
        head_id,
        pltpu.with_memory_space_constraint(prefix_keys, pltpu.HBM),
        pltpu.with_memory_space_constraint(prefix_values, pltpu.HBM),
    )

    def swap(array, near, swapped):
        pairs = []
        for place in range(seq_count):
            chip, core = place // 2, place % 2
            chip = (chip + near * (2 * core - 1)) % (seq_count // 2)
            pairs.append((place, 2 * chip + (1 - core if swapped else core)))
        return lax.ppermute(array, "seq", pairs)

    blocks = [
        heads_of_block[0],
        swap(heads_of_block[1], 0, True),
        swap(heads_of_block[2], 1, False),
        swap(heads_of_block[3], 1, True),
    ]

    rows, payload = pl.pallas_call(
        prepare_kernel,
        out_shape=(
            shape((samples, heads * steps, HD), jnp.bfloat16),
            shape((seq_count, samples * per + 8, HD), jnp.bfloat16),
        ),
        in_specs=[SMEM, VMEM],
        out_specs=(VMEM, VMEM),
        name="prepare",
    )(sample_prompt.reshape(samples), queries)
    received = lax.all_to_all(payload, "seq", split_axis=0, concat_axis=0, tiled=True)

    suffix_out, suffix_log = pl.pallas_call(
        suffix_kernel,
        out_shape=(
            shape((samples, heads * steps, HD), jnp.float32),
            shape((samples, heads * steps, HD), jnp.float32),
        ),
        in_specs=[SMEM] + [VMEM] * 5,
        out_specs=(VMEM, VMEM),
        compiler_params=params(16),
        name="suffix",
    )(
        suffix_len,
        rows,
        new_keys,
        new_values,
        suffix_keys,
        suffix_values,
    )

    suffix_out, suffix_log = pl.pallas_call(
        suffix_kernel,
        out_shape=(
            shape((samples, heads * steps, HD), jnp.float32),
            shape((samples, heads * steps, HD), jnp.float32),
        ),
        in_specs=[SMEM] + [VMEM] * 5,
        out_specs=(VMEM, VMEM),
        compiler_params=params(16),
        name="suffix",
    )(
        suffix_len,
        rows,
        new_keys,
        new_values,
        suffix_keys,
        suffix_values,
    )

    packed, slots = pl.pallas_call(
        functools.partial(pack_kernel, samples),
        out_shape=(
            pltpu.HBM((engine_count, CAPE * per, HD), jnp.bfloat16),
            shape((seq_count * samples,), jnp.int32),
        ),
        in_specs=[pl.BlockSpec(memory_space=pl.ANY), VMEM],
        out_specs=(VMEM, SMEM),
        scratch_shapes=[pltpu.SMEM((engine_count,), jnp.int32)],
        compiler_params=params(16),
        name="pack",
    )(suffix_log, received)
    dispatched = lax.all_to_all(packed, "engine", split_axis=0, concat_axis=0, tiled=True)

    reply = pl.pallas_call(
        functools.partial(prefix_kernel, 8 * CAPE),
        out_shape=shape((engine_count, CAPE * per // 8 + 1, 4, HD), jnp.int32),
        in_specs=[VMEM] * (1 + KVH),
        out_specs=VMEM,
        compiler_params=params(16),
        name="prefix",
    )(
        dispatched.reshape(engine_count * CAPE, per, HD),
        *[pltpu.with_memory_space_constraint(block, pltpu.VMEM) for block in blocks],
    )
    returned = lax.all_to_all(reply, "engine", split_axis=0, concat_axis=0, tiled=True)

    chosen = pl.pallas_call(
        functools.partial(select_kernel, samples),
        out_shape=shape((seq_count, samples * per // 8 + 1, 4, HD), jnp.int32),
        in_specs=[SMEM, VMEM],
        out_specs=VMEM,
        compiler_params=params(16),
        name="select",
    )(slots, returned)
    gathered = lax.all_to_all(chosen, "seq", split_axis=0, concat_axis=0, tiled=True)

    return pl.pallas_call(
        combine_kernel,
        out_shape=shape((samples, steps, features), jnp.bfloat16),
        in_specs=[VMEM] * 3,
        out_specs=VMEM,
        compiler_params=params(16),
        name="combine",
    )(gathered, suffix_out, suffix_log)


def solution(mesh):
    return jax.shard_map(
        local,
        mesh=mesh,
        in_specs=(
            P(("engine", "seq"), None, None),
            P(("engine", "seq"), None, None),
            P(("engine", "seq"), None, None),
            P(("engine", "seq"), None, None),
            P(("engine", "seq"), None, None),
            P(("engine", "seq")),
            P(("engine", "seq"), None),
            P("engine", "seq", None),
            P("engine", "seq", None),
        ),
        out_specs=P(("engine", "seq"), None, None),
        check_vma=False,
    )
```

```python
import functools
import math

import jax
import jax.numpy as jnp
from jax import lax
from jax.experimental import pallas as pl
from jax.experimental.pallas import tpu as pltpu
from jax.sharding import PartitionSpec as P

KVH = 4
GROUP = 8
HD = 128
CAPE = 3
SCALING = HD ** (-0.5)
LOG2E = math.log2(math.e)
LSE_ONE = float(2**20)
VMEM = pl.BlockSpec(memory_space=pltpu.VMEM)
SMEM = pl.BlockSpec(memory_space=pltpu.SMEM)


def params(mib):
    return pltpu.CompilerParams(vmem_limit_bytes=mib * 1024 * 1024)


def shape(dims, dtype):
    return jax.ShapeDtypeStruct(dims, dtype)


def prepare_kernel(prompt_ref, queries_ref, rows_ref, payload_ref):
    samples, steps, features = queries_ref.shape
    heads = features // HD
    part = heads * steps // KVH
    extra = payload_ref.shape[1] - samples * part
    lanes = lax.broadcasted_iota(jnp.int32, (extra, HD), 1)
    note = jnp.zeros((extra, HD), jnp.int32)
    for sample in range(samples):
        note = jnp.where(lanes == sample, prompt_ref[sample], note)
    note = note.astype(jnp.float32).astype(jnp.bfloat16)
    for sample in range(samples):
        for first in range(0, heads, 4):
            tile = jnp.concatenate(
                [
                    queries_ref[sample, :, (first + i) * HD : (first + i + 1) * HD].astype(jnp.float32)
                    for i in range(4)
                ],
                axis=0,
            ).astype(jnp.bfloat16)
            row = first * steps
            rows_ref[sample, row : row + 4 * steps] = tile
            group, row = row // part, row % part
            for place in range(group, payload_ref.shape[0], KVH):
                payload_ref[place, sample * part + row : sample * part + row + 4 * steps] = tile
    for place in range(payload_ref.shape[0]):
        payload_ref[place, samples * part :] = note


def split_kernel(head_ref, k_ref, v_ref, *refs):
    outs, held, sems = refs[:KVH], refs[KVH], refs[KVH + 1]
    copies = []
    for place, out in enumerate(outs):
        head = jnp.bitwise_xor(head_ref[0], place)
        cols = pl.ds(pl.multiple_of(head * HD, HD), HD)
        keys = pltpu.make_async_copy(k_ref.at[0, :, cols], out.at[0], sems.at[place, 0])
        values = pltpu.make_async_copy(v_ref.at[0, :, cols], held.at[place], sems.at[place, 1])
        copies.append((keys, values))
    for keys, values in copies:
        values.start()
    for keys, values in copies:
        keys.start()
    for place, out in enumerate(outs):
        copies[place][1].wait()
        for first in range(0, held.shape[1], HD):
            out[1, first : first + HD] = held[place, first : first + HD].T
    for keys, values in copies:
        keys.wait()


def pack_kernel(samples, _, received_ref, packed_ref, slots_ref, counts_ref):
    prompts, part = packed_ref.shape[0], packed_ref.shape[1] // CAPE
    packed_ref[...] = jnp.zeros(packed_ref.shape, packed_ref.dtype)
    for prompt in range(prompts):
        counts_ref[prompt] = 0
    for place in range(received_ref.shape[0]):
        note = received_ref[place, samples * part :].astype(jnp.float32).astype(jnp.int32)
        for sample in range(samples):
            prompt = note[0, sample]
            rank = counts_ref[prompt]
            counts_ref[prompt] = rank + 1
            slots_ref[place * samples + sample] = prompt * 4 + rank
            packed_ref[prompt, pl.ds(pl.multiple_of(rank * part, part), part)] = received_ref[
                place, sample * part : (sample + 1) * part
            ]


def block_scores(rows, keys):
    return lax.dot_general(keys, rows, (((1,), (1,)), ((), ())), preferred_element_type=jnp.float32)


def block_attention(raw, values):
    values = jnp.concatenate(
        [values[first : first + HD] for first in range(0, values.shape[0], HD)], axis=1
    )
    top = jnp.max(raw, axis=0, keepdims=True)
    probs = jnp.exp2((raw - top) * (SCALING * LOG2E))
    total = jnp.sum(probs, axis=0, keepdims=True)
    acc = jnp.dot(values, probs.astype(jnp.bfloat16), preferred_element_type=jnp.float32)
    return acc, top * (SCALING * LOG2E), total


def encode(out):
    largest = jnp.max(jnp.abs(out), axis=0, keepdims=True)
    power = jnp.floor(jnp.log2(jnp.maximum(largest, 2.0**-112) * 1.0001)) + 1.0
    code = jnp.clip(jnp.round(out * jnp.exp2(15.0 - power)), -32767.0, 32767.0)
    return code.astype(jnp.int32), power.astype(jnp.int32)


def prefix_kernel(chunk, q_ref, *refs):
    blocks, reply_ref = refs[:-1], refs[-1]
    slots, per = q_ref.shape[0], q_ref.shape[1]
    rows_of = per // 2
    wide = chunk * rows_of

    def rows_from(start):
        return jnp.concatenate(
            [
                q_ref[start : start + chunk, 0:rows_of].reshape(wide, HD),
                q_ref[start : start + chunk, rows_of:per].reshape(wide, HD),
            ],
            axis=0,
        )

    def finish(start, parts):
        top = functools.reduce(jnp.maximum, [part[1] for part in parts])
        weights = [jnp.exp2(part[1] - top) for part in parts]
        total = functools.reduce(jnp.add, [w * part[2] for w, part in zip(weights, parts)])
        share = 1.0 / total
        out = functools.reduce(jnp.add, [(w * share) * part[0] for w, part in zip(weights, parts)])
        log = jnp.round((top + jnp.log2(total)) * LSE_ONE).astype(jnp.int32)
        code, power = encode(out)
        packed = jnp.bitwise_or(
            jnp.left_shift(code[:, :wide], 16), jnp.bitwise_and(code[:, wide:], 0xFFFF)
        ).T
        rest = jnp.zeros((1, HD - 2 * per), jnp.int32)
        for slot in range(chunk):
            dest, rank = (start + slot) // CAPE, (start + slot) % CAPE
            first = slot * rows_of
            for part in range(rows_of // 4):
                reply_ref[dest, rank * (rows_of // 4) + part] = packed[
                    first + part * 4 : first + part * 4 + 4
                ]
            pieces = [
                array[:, begin : begin + rows_of]
                for array in (log, power)
                for begin in (first, wide + first)
            ]
            reply_ref[dest, CAPE * (rows_of // 4), rank : rank + 1] = jnp.concatenate(
                pieces + [rest], axis=1
            )

    starts = range(0, slots, chunk)
    stages = [(start, place) for start in starts for place in range(len(blocks))]
    rows = {start: rows_from(start) for start in starts}
    raw, parts = block_scores(rows[0], blocks[0][0]), []
    for number, (start, place) in enumerate(stages):
        ready = raw
        if number + 1 < len(stages):
            later, block = stages[number + 1]
            raw = block_scores(rows[later], blocks[block][0])
        parts.append(block_attention(ready, blocks[place][1]))
        if place + 1 == len(blocks):
            finish(start, parts)
            parts = []


def select_kernel(samples, slots_ref, reply_ref, chosen_ref):
    body = (chosen_ref.shape[1] - 1) // samples
    for sample in range(chosen_ref.shape[0] * samples):
        slot = slots_ref[sample]
        prompt, rank = lax.shift_right_logical(slot, 2), lax.bitwise_and(slot, 3)
        place, which = sample // samples, sample % samples
        chosen_ref[place, which * body : (which + 1) * body] = reply_ref[
            prompt, pl.ds(rank * body, body)
        ]
        chosen_ref[place, samples * body, which : which + 1] = reply_ref[
            prompt, CAPE * body, pl.ds(rank, 1)
        ]


def suffix_kernel(length_ref, rows_ref, fresh_k_ref, fresh_v_ref, k_ref, v_ref, out_ref, log_ref):
    samples, positions = k_ref.shape[0], k_ref.shape[1]
    fresh = 16

    def padded(array):
        rest = jnp.zeros((fresh - array.shape[0], HD), jnp.float32)
        return jnp.concatenate([array.astype(jnp.float32), rest], axis=0).astype(jnp.bfloat16)

    per = rows_ref.shape[1] // KVH
    steps = per // GROUP
    column = lax.broadcasted_iota(jnp.int32, (per, positions), 1)
    step = lax.rem(lax.broadcasted_iota(jnp.int32, (per, fresh), 0), steps)
    causal = lax.broadcasted_iota(jnp.int32, (per, fresh), 1) <= step
    for sample in range(samples):
        live = column < length_ref[sample]
        for group in range(KVH):
            cols = slice(group * HD, (group + 1) * HD)
            rows = rows_ref[sample, group * per : (group + 1) * per]
            dims = (((1,), (1,)), ((), ()))
            cache_raw = lax.dot_general(
                rows, k_ref[sample, :, cols], dims, preferred_element_type=jnp.float32
            )
            fresh_raw = lax.dot_general(
                rows, padded(fresh_k_ref[sample, :, cols]), dims, preferred_element_type=jnp.float32
            )
            cache_raw = jnp.where(live, cache_raw, -jnp.inf)
            fresh_raw = jnp.where(causal, fresh_raw, -jnp.inf)
            top = jnp.maximum(
                jnp.max(cache_raw, axis=1, keepdims=True), jnp.max(fresh_raw, axis=1, keepdims=True)
            )
            cache_probs = jnp.exp2((cache_raw - top) * (SCALING * LOG2E))
            fresh_probs = jnp.exp2((fresh_raw - top) * (SCALING * LOG2E))
            total = jnp.sum(cache_probs, axis=1, keepdims=True) + jnp.sum(
                fresh_probs, axis=1, keepdims=True
            )
            acc = jnp.dot(
                cache_probs.astype(jnp.bfloat16),
                v_ref[sample, :, cols],
                preferred_element_type=jnp.float32,
            ) + jnp.dot(
                fresh_probs.astype(jnp.bfloat16),
                padded(fresh_v_ref[sample, :, cols]),
                preferred_element_type=jnp.float32,
            )
            here = slice(group * per, (group + 1) * per)
            out_ref[sample, here] = acc / total
            log_ref[sample, here] = jnp.broadcast_to(
                top * (SCALING * LOG2E) + jnp.log2(total), (per, HD)
            )


def combine_kernel(chosen_ref, suffix_out_ref, suffix_log_ref, out_ref):
    places, samples = chosen_ref.shape[0], suffix_out_ref.shape[0]
    steps = out_ref.shape[1]
    body = (chosen_ref.shape[1] - 1) // samples
    per = 8 * body
    row = lax.broadcasted_iota(jnp.int32, (per, HD), 0)
    lane = lax.broadcasted_iota(jnp.int32, (per, HD), 1)

    def turn(note, offset):
        spread = jnp.broadcast_to(note, (per, HD))
        return jnp.sum(jnp.where(lane == row + offset, spread, 0.0), axis=1, keepdims=True)

    for sample in range(samples):
        for group in range(KVH):
            logs, scales, codes = [], [], []
            for place in range(group, places, KVH):
                packed = jnp.concatenate(
                    [chosen_ref[place, sample * body + part] for part in range(body)], axis=0
                )
                high = jnp.right_shift(packed, 16)
                low = jnp.right_shift(jnp.left_shift(packed, 16), 16)
                codes.append(jnp.concatenate([high, low], axis=0).astype(jnp.float32))
                note = chosen_ref[place, samples * body, sample : sample + 1].astype(jnp.float32)
                logs.append(turn(note, 0) * (1.0 / LSE_ONE))
                scales.append(jnp.exp2(turn(note, per) - 15.0))
            peak = functools.reduce(jnp.maximum, logs)
            weights = [jnp.exp2(log - peak) for log in logs]
            weight_sum = functools.reduce(jnp.add, weights)
            prefix = functools.reduce(
                jnp.add, [(w * s) * c for w, s, c in zip(weights, scales, codes)]
            )
            prefix_log = peak + jnp.log2(weight_sum)
            first = group * per
            suffix_log = suffix_log_ref[sample, first : first + per][:, 0:1]
            suffix = suffix_out_ref[sample, first : first + per]
            top = jnp.maximum(prefix_log, suffix_log)
            prefix_weight = jnp.exp2(prefix_log - top)
            suffix_weight = jnp.exp2(suffix_log - top)
            whole = prefix_weight + suffix_weight
            result = (prefix_weight / (weight_sum * whole)) * prefix + (
                suffix_weight / whole
            ) * suffix
            for i in range(per // steps):
                head = first // steps + i
                out_ref[sample, :, head * HD : (head + 1) * HD] = result[
                    i * steps : (i + 1) * steps
                ].astype(jnp.bfloat16)


def local(
    queries,
    new_keys,
    new_values,
    suffix_keys,
    suffix_values,
    suffix_len,
    sample_prompt,
    prefix_keys,
    prefix_values,
):
    samples, steps, features = queries.shape
    heads = features // HD
    per = GROUP * steps
    seq_count = lax.axis_size("seq")
    engine_count = lax.axis_size("engine")
    positions = prefix_keys.shape[1]

    head_id = lax.rem(lax.axis_index("seq"), KVH).reshape(1)
    heads_of_block = pl.pallas_call(
        split_kernel,
        out_shape=[shape((2, positions, HD), jnp.bfloat16)] * KVH,
        in_specs=[SMEM] + [pl.BlockSpec(memory_space=pltpu.HBM)] * 2,
        out_specs=[VMEM] * KVH,
        scratch_shapes=[
            pltpu.VMEM((KVH, positions, HD), jnp.bfloat16),
            pltpu.SemaphoreType.DMA((KVH, 2)),
        ],
        compiler_params=params(16),
        name="split",
    )(
        head_id,
        pltpu.with_memory_space_constraint(prefix_keys, pltpu.HBM),
        pltpu.with_memory_space_constraint(prefix_values, pltpu.HBM),
    )

    def swap(array, near, swapped):
        pairs = []
        for place in range(seq_count):
            chip, core = place // 2, place % 2
            chip = (chip + near * (2 * core - 1)) % (seq_count // 2)
            pairs.append((place, 2 * chip + (1 - core if swapped else core)))
        return lax.ppermute(array, "seq", pairs)

    blocks = [
        heads_of_block[0],
        swap(heads_of_block[1], 0, True),
        swap(heads_of_block[2], 1, False),
        swap(heads_of_block[3], 1, True),
    ]

    rows, payload = pl.pallas_call(
        prepare_kernel,
        out_shape=(
            shape((samples, heads * steps, HD), jnp.bfloat16),
            shape((seq_count, samples * per + 8, HD), jnp.bfloat16),
        ),
        in_specs=[SMEM, VMEM],
        out_specs=(VMEM, VMEM),
        name="prepare",
    )(sample_prompt.reshape(samples), queries)
    received = lax.all_to_all(payload, "seq", split_axis=0, concat_axis=0, tiled=True)

    suffix_out, suffix_log = pl.pallas_call(
        suffix_kernel,
        out_shape=(
            shape((samples, heads * steps, HD), jnp.float32),
            shape((samples, heads * steps, HD), jnp.float32),
        ),
        in_specs=[SMEM] + [VMEM] * 5,
        out_specs=(VMEM, VMEM),
        compiler_params=params(16),
        name="suffix",
    )(
        suffix_len,
        rows,
        new_keys,
        new_values,
        suffix_keys,
        suffix_values,
    )

    suffix_out, suffix_log = pl.pallas_call(
        suffix_kernel,
        out_shape=(
            shape((samples, heads * steps, HD), jnp.float32),
            shape((samples, heads * steps, HD), jnp.float32),
        ),
        in_specs=[SMEM] + [VMEM] * 5,
        out_specs=(VMEM, VMEM),
        compiler_params=params(16),
        name="suffix",
    )(
        suffix_len,
        rows,
        new_keys,
        new_values,
        suffix_keys,
        suffix_values,
    )

    packed, slots = pl.pallas_call(
        functools.partial(pack_kernel, samples),
        out_shape=(
            pltpu.HBM((engine_count, CAPE * per, HD), jnp.bfloat16),
            shape((seq_count * samples,), jnp.int32),
        ),
        in_specs=[pl.BlockSpec(memory_space=pl.ANY), VMEM],
        out_specs=(VMEM, SMEM),
        scratch_shapes=[pltpu.SMEM((engine_count,), jnp.int32)],
        compiler_params=params(16),
        name="pack",
    )(suffix_log, received)
    dispatched = lax.all_to_all(packed, "engine", split_axis=0, concat_axis=0, tiled=True)

    reply = pl.pallas_call(
        functools.partial(prefix_kernel, 16),
        out_shape=shape((engine_count, CAPE * per // 8 + 1, 4, HD), jnp.int32),
        in_specs=[VMEM] * (1 + KVH),
        out_specs=VMEM,
        compiler_params=params(16),
        name="prefix",
    )(
        dispatched.reshape(engine_count * CAPE, per, HD),
        *[pltpu.with_memory_space_constraint(block, pltpu.VMEM) for block in blocks],
    )
    returned = lax.all_to_all(reply, "engine", split_axis=0, concat_axis=0, tiled=True)

    chosen = pl.pallas_call(
        functools.partial(select_kernel, samples),
        out_shape=shape((seq_count, samples * per // 8 + 1, 4, HD), jnp.int32),
        in_specs=[SMEM, VMEM],
        out_specs=VMEM,
        compiler_params=params(16),
        name="select",
    )(slots, returned)
    gathered = lax.all_to_all(chosen, "seq", split_axis=0, concat_axis=0, tiled=True)

    return pl.pallas_call(
        combine_kernel,
        out_shape=shape((samples, steps, features), jnp.bfloat16),
        in_specs=[VMEM] * 3,
        out_specs=VMEM,
        compiler_params=params(16),
        name="combine",
    )(gathered, suffix_out, suffix_log)


def solution(mesh):
    return jax.shard_map(
        local,
        mesh=mesh,
        in_specs=(
            P(("engine", "seq"), None, None),
            P(("engine", "seq"), None, None),
            P(("engine", "seq"), None, None),
            P(("engine", "seq"), None, None),
            P(("engine", "seq"), None, None),
            P(("engine", "seq")),
            P(("engine", "seq"), None),
            P("engine", "seq", None),
            P("engine", "seq", None),
        ),
        out_specs=P(("engine", "seq"), None, None),
        check_vma=False,
    )
```

```python
import functools
import math

import jax
import jax.numpy as jnp
from jax import lax
from jax.experimental import pallas as pl
from jax.experimental.pallas import tpu as pltpu
from jax.sharding import PartitionSpec as P

KVH = 4
GROUP = 8
HD = 128
CAPE = 3
SCALING = HD ** (-0.5)
LOG2E = math.log2(math.e)
LSE_ONE = float(2**20)
VMEM = pl.BlockSpec(memory_space=pltpu.VMEM)
SMEM = pl.BlockSpec(memory_space=pltpu.SMEM)


def params(mib):
    return pltpu.CompilerParams(vmem_limit_bytes=mib * 1024 * 1024)


def shape(dims, dtype):
    return jax.ShapeDtypeStruct(dims, dtype)


def prepare_kernel(prompt_ref, queries_ref, rows_ref, payload_ref):
    samples, steps, features = queries_ref.shape
    heads = features // HD
    part = heads * steps // KVH
    extra = payload_ref.shape[1] - samples * part
    lanes = lax.broadcasted_iota(jnp.int32, (extra, HD), 1)
    note = jnp.zeros((extra, HD), jnp.int32)
    for sample in range(samples):
        note = jnp.where(lanes == sample, prompt_ref[sample], note)
    note = note.astype(jnp.float32).astype(jnp.bfloat16)
    for sample in range(samples):
        for first in range(0, heads, 4):
            tile = jnp.concatenate(
                [
                    queries_ref[sample, :, (first + i) * HD : (first + i + 1) * HD].astype(jnp.float32)
                    for i in range(4)
                ],
                axis=0,
            ).astype(jnp.bfloat16)
            row = first * steps
            rows_ref[sample, row : row + 4 * steps] = tile
            group, row = row // part, row % part
            for place in range(group, payload_ref.shape[0], KVH):
                payload_ref[place, sample * part + row : sample * part + row + 4 * steps] = tile
    for place in range(payload_ref.shape[0]):
        payload_ref[place, samples * part :] = note


def split_kernel(head_ref, k_ref, v_ref, *refs):
    outs, held, sems = refs[:KVH], refs[KVH], refs[KVH + 1]
    copies = []
    for place, out in enumerate(outs):
        head = jnp.bitwise_xor(head_ref[0], place)
        cols = pl.ds(pl.multiple_of(head * HD, HD), HD)
        keys = pltpu.make_async_copy(k_ref.at[0, :, cols], out.at[0], sems.at[place, 0])
        values = pltpu.make_async_copy(v_ref.at[0, :, cols], held.at[place], sems.at[place, 1])
        copies.append((keys, values))
    for keys, values in copies:
        values.start()
    for keys, values in copies:
        keys.start()
    for place, out in enumerate(outs):
        copies[place][1].wait()
        for first in range(0, held.shape[1], HD):
            out[1, first : first + HD] = held[place, first : first + HD].T
    for keys, values in copies:
        keys.wait()


def pack_kernel(samples, _, received_ref, packed_ref, slots_ref, counts_ref):
    prompts, part = packed_ref.shape[0], packed_ref.shape[1] // CAPE
    packed_ref[...] = jnp.zeros(packed_ref.shape, packed_ref.dtype)
    for prompt in range(prompts):
        counts_ref[prompt] = 0
    for place in range(received_ref.shape[0]):
        note = received_ref[place, samples * part :].astype(jnp.float32).astype(jnp.int32)
        for sample in range(samples):
            prompt = note[0, sample]
            rank = counts_ref[prompt]
            counts_ref[prompt] = rank + 1
            slots_ref[place * samples + sample] = prompt * 4 + rank
            packed_ref[prompt, pl.ds(pl.multiple_of(rank * part, part), part)] = received_ref[
                place, sample * part : (sample + 1) * part
            ]


def block_scores(rows, keys):
    return lax.dot_general(keys, rows, (((1,), (1,)), ((), ())), preferred_element_type=jnp.float32)


def block_softmax(raw):
    top = jnp.max(raw, axis=0, keepdims=True)
    probs = jnp.exp2((raw - top) * (SCALING * LOG2E))
    total = jnp.sum(probs, axis=0, keepdims=True)
    return probs.astype(jnp.bfloat16), top * (SCALING * LOG2E), total


def block_product(probs, values):
    values = jnp.concatenate(
        [values[first : first + HD] for first in range(0, values.shape[0], HD)], axis=1
    )
    return jnp.dot(values, probs, preferred_element_type=jnp.float32)


def encode(out):
    largest = jnp.max(jnp.abs(out), axis=0, keepdims=True)
    power = jnp.floor(jnp.log2(jnp.maximum(largest, 2.0**-112) * 1.0001)) + 1.0
    code = jnp.clip(jnp.round(out * jnp.exp2(15.0 - power)), -32767.0, 32767.0)
    return code.astype(jnp.int32), power.astype(jnp.int32)


def prefix_kernel(chunk, q_ref, *refs):
    blocks, reply_ref = refs[:-1], refs[-1]
    slots, per = q_ref.shape[0], q_ref.shape[1]
    rows_of = per // 2
    wide = chunk * rows_of

    def rows_from(start):
        return jnp.concatenate(
            [
                q_ref[start : start + chunk, 0:rows_of].reshape(wide, HD),
                q_ref[start : start + chunk, rows_of:per].reshape(wide, HD),
            ],
            axis=0,
        )

    def finish(start, parts):
        top = functools.reduce(jnp.maximum, [part[1] for part in parts])
        weights = [jnp.exp2(part[1] - top) for part in parts]
        total = functools.reduce(jnp.add, [w * part[2] for w, part in zip(weights, parts)])
        share = 1.0 / total
        out = functools.reduce(jnp.add, [(w * share) * part[0] for w, part in zip(weights, parts)])
        log = jnp.round((top + jnp.log2(total)) * LSE_ONE).astype(jnp.int32)
        code, power = encode(out)
        packed = jnp.bitwise_or(
            jnp.left_shift(code[:, :wide], 16), jnp.bitwise_and(code[:, wide:], 0xFFFF)
        ).T
        rest = jnp.zeros((1, HD - 2 * per), jnp.int32)
        for slot in range(chunk):
            dest, rank = (start + slot) // CAPE, (start + slot) % CAPE
            first = slot * rows_of
            for part in range(rows_of // 4):
                reply_ref[dest, rank * (rows_of // 4) + part] = packed[
                    first + part * 4 : first + part * 4 + 4
                ]
            pieces = [
                array[:, begin : begin + rows_of]
                for array in (log, power)
                for begin in (first, wide + first)
            ]
            reply_ref[dest, CAPE * (rows_of // 4), rank : rank + 1] = jnp.concatenate(
                pieces + [rest], axis=1
            )

    starts = range(0, slots, chunk)
    stages = [(start, place) for start in starts for place in range(len(blocks))]
    rows = {start: rows_from(start) for start in starts}
    raw, waiting, parts = block_scores(rows[0], blocks[0][0]), None, []

    def product():
        (start, place), (probs, top, total) = waiting
        parts.append((block_product(probs, blocks[place][1]), top, total))
        if place + 1 == len(blocks):
            finish(start, parts)
            parts.clear()

    for number, stage in enumerate(stages):
        ready = raw
        if number + 1 < len(stages):
            later, block = stages[number + 1]
            raw = block_scores(rows[later], blocks[block][0])
        if waiting is not None:
            product()
        waiting = (stage, block_softmax(ready))
    product()


def select_kernel(samples, slots_ref, reply_ref, chosen_ref):
    body = (chosen_ref.shape[1] - 1) // samples
    for sample in range(chosen_ref.shape[0] * samples):
        slot = slots_ref[sample]
        prompt, rank = lax.shift_right_logical(slot, 2), lax.bitwise_and(slot, 3)
        place, which = sample // samples, sample % samples
        chosen_ref[place, which * body : (which + 1) * body] = reply_ref[
            prompt, pl.ds(rank * body, body)
        ]
        chosen_ref[place, samples * body, which : which + 1] = reply_ref[
            prompt, CAPE * body, pl.ds(rank, 1)
        ]


def suffix_kernel(length_ref, rows_ref, fresh_k_ref, fresh_v_ref, k_ref, v_ref, out_ref, log_ref):
    samples, positions = k_ref.shape[0], k_ref.shape[1]
    fresh = 16

    def padded(array):
        rest = jnp.zeros((fresh - array.shape[0], HD), jnp.float32)
        return jnp.concatenate([array.astype(jnp.float32), rest], axis=0).astype(jnp.bfloat16)

    per = rows_ref.shape[1] // KVH
    steps = per // GROUP
    column = lax.broadcasted_iota(jnp.int32, (per, positions), 1)
    step = lax.rem(lax.broadcasted_iota(jnp.int32, (per, fresh), 0), steps)
    causal = lax.broadcasted_iota(jnp.int32, (per, fresh), 1) <= step
    for sample in range(samples):
        live = column < length_ref[sample]
        for group in range(KVH):
            cols = slice(group * HD, (group + 1) * HD)
            rows = rows_ref[sample, group * per : (group + 1) * per]
            dims = (((1,), (1,)), ((), ()))
            cache_raw = lax.dot_general(
                rows, k_ref[sample, :, cols], dims, preferred_element_type=jnp.float32
            )
            fresh_raw = lax.dot_general(
                rows, padded(fresh_k_ref[sample, :, cols]), dims, preferred_element_type=jnp.float32
            )
            cache_raw = jnp.where(live, cache_raw, -jnp.inf)
            fresh_raw = jnp.where(causal, fresh_raw, -jnp.inf)
            top = jnp.maximum(
                jnp.max(cache_raw, axis=1, keepdims=True), jnp.max(fresh_raw, axis=1, keepdims=True)
            )
            cache_probs = jnp.exp2((cache_raw - top) * (SCALING * LOG2E))
            fresh_probs = jnp.exp2((fresh_raw - top) * (SCALING * LOG2E))
            total = jnp.sum(cache_probs, axis=1, keepdims=True) + jnp.sum(
                fresh_probs, axis=1, keepdims=True
            )
            acc = jnp.dot(
                cache_probs.astype(jnp.bfloat16),
                v_ref[sample, :, cols],
                preferred_element_type=jnp.float32,
            ) + jnp.dot(
                fresh_probs.astype(jnp.bfloat16),
                padded(fresh_v_ref[sample, :, cols]),
                preferred_element_type=jnp.float32,
            )
            here = slice(group * per, (group + 1) * per)
            out_ref[sample, here] = acc / total
            log_ref[sample, here] = jnp.broadcast_to(
                top * (SCALING * LOG2E) + jnp.log2(total), (per, HD)
            )


def combine_kernel(chosen_ref, suffix_out_ref, suffix_log_ref, out_ref):
    places, samples = chosen_ref.shape[0], suffix_out_ref.shape[0]
    steps = out_ref.shape[1]
    body = (chosen_ref.shape[1] - 1) // samples
    per = 8 * body
    row = lax.broadcasted_iota(jnp.int32, (per, HD), 0)
    lane = lax.broadcasted_iota(jnp.int32, (per, HD), 1)

    def turn(note, offset):
        spread = jnp.broadcast_to(note, (per, HD))
        return jnp.sum(jnp.where(lane == row + offset, spread, 0.0), axis=1, keepdims=True)

    for sample in range(samples):
        for group in range(KVH):
            logs, scales, codes = [], [], []
            for place in range(group, places, KVH):
                packed = jnp.concatenate(
                    [chosen_ref[place, sample * body + part] for part in range(body)], axis=0
                )
                high = jnp.right_shift(packed, 16)
                low = jnp.right_shift(jnp.left_shift(packed, 16), 16)
                codes.append(jnp.concatenate([high, low], axis=0).astype(jnp.float32))
                note = chosen_ref[place, samples * body, sample : sample + 1].astype(jnp.float32)
                logs.append(turn(note, 0) * (1.0 / LSE_ONE))
                scales.append(jnp.exp2(turn(note, per) - 15.0))
            peak = functools.reduce(jnp.maximum, logs)
            weights = [jnp.exp2(log - peak) for log in logs]
            weight_sum = functools.reduce(jnp.add, weights)
            prefix = functools.reduce(
                jnp.add, [(w * s) * c for w, s, c in zip(weights, scales, codes)]
            )
            prefix_log = peak + jnp.log2(weight_sum)
            first = group * per
            suffix_log = suffix_log_ref[sample, first : first + per][:, 0:1]
            suffix = suffix_out_ref[sample, first : first + per]
            top = jnp.maximum(prefix_log, suffix_log)
            prefix_weight = jnp.exp2(prefix_log - top)
            suffix_weight = jnp.exp2(suffix_log - top)
            whole = prefix_weight + suffix_weight
            result = (prefix_weight / (weight_sum * whole)) * prefix + (
                suffix_weight / whole
            ) * suffix
            for i in range(per // steps):
                head = first // steps + i
                out_ref[sample, :, head * HD : (head + 1) * HD] = result[
                    i * steps : (i + 1) * steps
                ].astype(jnp.bfloat16)


def local(
    queries,
    new_keys,
    new_values,
    suffix_keys,
    suffix_values,
    suffix_len,
    sample_prompt,
    prefix_keys,
    prefix_values,
):
    samples, steps, features = queries.shape
    heads = features // HD
    per = GROUP * steps
    seq_count = lax.axis_size("seq")
    engine_count = lax.axis_size("engine")
    positions = prefix_keys.shape[1]

    head_id = lax.rem(lax.axis_index("seq"), KVH).reshape(1)
    heads_of_block = pl.pallas_call(
        split_kernel,
        out_shape=[shape((2, positions, HD), jnp.bfloat16)] * KVH,
        in_specs=[SMEM] + [pl.BlockSpec(memory_space=pltpu.HBM)] * 2,
        out_specs=[VMEM] * KVH,
        scratch_shapes=[
            pltpu.VMEM((KVH, positions, HD), jnp.bfloat16),
            pltpu.SemaphoreType.DMA((KVH, 2)),
        ],
        compiler_params=params(16),
        name="split",
    )(
        head_id,
        pltpu.with_memory_space_constraint(prefix_keys, pltpu.HBM),
        pltpu.with_memory_space_constraint(prefix_values, pltpu.HBM),
    )

    def swap(array, near, swapped):
        pairs = []
        for place in range(seq_count):
            chip, core = place // 2, place % 2
            chip = (chip + near * (2 * core - 1)) % (seq_count // 2)
            pairs.append((place, 2 * chip + (1 - core if swapped else core)))
        return lax.ppermute(array, "seq", pairs)

    blocks = [
        heads_of_block[0],
        swap(heads_of_block[1], 0, True),
        swap(heads_of_block[2], 1, False),
        swap(heads_of_block[3], 1, True),
    ]

    rows, payload = pl.pallas_call(
        prepare_kernel,
        out_shape=(
            shape((samples, heads * steps, HD), jnp.bfloat16),
            shape((seq_count, samples * per + 8, HD), jnp.bfloat16),
        ),
        in_specs=[SMEM, VMEM],
        out_specs=(VMEM, VMEM),
        name="prepare",
    )(sample_prompt.reshape(samples), queries)
    received = lax.all_to_all(payload, "seq", split_axis=0, concat_axis=0, tiled=True)

    suffix_out, suffix_log = pl.pallas_call(
        suffix_kernel,
        out_shape=(
            shape((samples, heads * steps, HD), jnp.float32),
            shape((samples, heads * steps, HD), jnp.float32),
        ),
        in_specs=[SMEM] + [VMEM] * 5,
        out_specs=(VMEM, VMEM),
        compiler_params=params(16),
        name="suffix",
    )(
        suffix_len,
        rows,
        new_keys,
        new_values,
        suffix_keys,
        suffix_values,
    )

    suffix_out, suffix_log = pl.pallas_call(
        suffix_kernel,
        out_shape=(
            shape((samples, heads * steps, HD), jnp.float32),
            shape((samples, heads * steps, HD), jnp.float32),
        ),
        in_specs=[SMEM] + [VMEM] * 5,
        out_specs=(VMEM, VMEM),
        compiler_params=params(16),
        name="suffix",
    )(
        suffix_len,
        rows,
        new_keys,
        new_values,
        suffix_keys,
        suffix_values,
    )

    packed, slots = pl.pallas_call(
        functools.partial(pack_kernel, samples),
        out_shape=(
            pltpu.HBM((engine_count, CAPE * per, HD), jnp.bfloat16),
            shape((seq_count * samples,), jnp.int32),
        ),
        in_specs=[pl.BlockSpec(memory_space=pl.ANY), VMEM],
        out_specs=(VMEM, SMEM),
        scratch_shapes=[pltpu.SMEM((engine_count,), jnp.int32)],
        compiler_params=params(16),
        name="pack",
    )(suffix_log, received)
    dispatched = lax.all_to_all(packed, "engine", split_axis=0, concat_axis=0, tiled=True)

    reply = pl.pallas_call(
        functools.partial(prefix_kernel, 16),
        out_shape=shape((engine_count, CAPE * per // 8 + 1, 4, HD), jnp.int32),
        in_specs=[VMEM] * (1 + KVH),
        out_specs=VMEM,
        compiler_params=params(16),
        name="prefix",
    )(
        dispatched.reshape(engine_count * CAPE, per, HD),
        *[pltpu.with_memory_space_constraint(block, pltpu.VMEM) for block in blocks],
    )
    returned = lax.all_to_all(reply, "engine", split_axis=0, concat_axis=0, tiled=True)

    chosen = pl.pallas_call(
        functools.partial(select_kernel, samples),
        out_shape=shape((seq_count, samples * per // 8 + 1, 4, HD), jnp.int32),
        in_specs=[SMEM, VMEM],
        out_specs=VMEM,
        compiler_params=params(16),
        name="select",
    )(slots, returned)
    gathered = lax.all_to_all(chosen, "seq", split_axis=0, concat_axis=0, tiled=True)

    return pl.pallas_call(
        combine_kernel,
        out_shape=shape((samples, steps, features), jnp.bfloat16),
        in_specs=[VMEM] * 3,
        out_specs=VMEM,
        compiler_params=params(16),
        name="combine",
    )(gathered, suffix_out, suffix_log)


def solution(mesh):
    return jax.shard_map(
        local,
        mesh=mesh,
        in_specs=(
            P(("engine", "seq"), None, None),
            P(("engine", "seq"), None, None),
            P(("engine", "seq"), None, None),
            P(("engine", "seq"), None, None),
            P(("engine", "seq"), None, None),
            P(("engine", "seq")),
            P(("engine", "seq"), None),
            P("engine", "seq", None),
            P("engine", "seq", None),
        ),
        out_specs=P(("engine", "seq"), None, None),
        check_vma=False,
    )
```

```python
import functools
import math

import jax
import jax.numpy as jnp
from jax import lax
from jax.experimental import pallas as pl
from jax.experimental.pallas import tpu as pltpu
from jax.sharding import PartitionSpec as P

KVH = 4
GROUP = 8
HD = 128
CAPE = 3
SCALING = HD ** (-0.5)
LOG2E = math.log2(math.e)
LSE_ONE = float(2**20)
VMEM = pl.BlockSpec(memory_space=pltpu.VMEM)
SMEM = pl.BlockSpec(memory_space=pltpu.SMEM)


def params(mib):
    return pltpu.CompilerParams(vmem_limit_bytes=mib * 1024 * 1024)


def shape(dims, dtype):
    return jax.ShapeDtypeStruct(dims, dtype)


def prepare_kernel(prompt_ref, queries_ref, rows_ref, payload_ref):
    samples, steps, features = queries_ref.shape
    heads = features // HD
    part = heads * steps // KVH
    extra = payload_ref.shape[1] - samples * part
    lanes = lax.broadcasted_iota(jnp.int32, (extra, HD), 1)
    note = jnp.zeros((extra, HD), jnp.int32)
    for sample in range(samples):
        note = jnp.where(lanes == sample, prompt_ref[sample], note)
    note = note.astype(jnp.float32).astype(jnp.bfloat16)
    for sample in range(samples):
        for first in range(0, heads, 4):
            tile = jnp.concatenate(
                [
                    queries_ref[sample, :, (first + i) * HD : (first + i + 1) * HD].astype(jnp.float32)
                    for i in range(4)
                ],
                axis=0,
            ).astype(jnp.bfloat16)
            row = first * steps
            rows_ref[sample, row : row + 4 * steps] = tile
            group, row = row // part, row % part
            for place in range(group, payload_ref.shape[0], KVH):
                payload_ref[place, sample * part + row : sample * part + row + 4 * steps] = tile
    for place in range(payload_ref.shape[0]):
        payload_ref[place, samples * part :] = note


def split_kernel(head_ref, k_ref, v_ref, *refs):
    outs, held, sems = refs[:KVH], refs[KVH], refs[KVH + 1]
    copies = []
    for place, out in enumerate(outs):
        head = jnp.bitwise_xor(head_ref[0], place)
        cols = pl.ds(pl.multiple_of(head * HD, HD), HD)
        keys = pltpu.make_async_copy(k_ref.at[0, :, cols], out.at[0], sems.at[place, 0])
        values = pltpu.make_async_copy(v_ref.at[0, :, cols], held.at[place], sems.at[place, 1])
        copies.append((keys, values))
    for keys, values in copies:
        values.start()
    for keys, values in copies:
        keys.start()
    for place, out in enumerate(outs):
        copies[place][1].wait()
        for first in range(0, held.shape[1], HD):
            out[1, first : first + HD] = held[place, first : first + HD].T
    for keys, values in copies:
        keys.wait()


def pack_kernel(samples, _, received_ref, packed_ref, slots_ref, counts_ref):
    prompts, part = packed_ref.shape[0], packed_ref.shape[1] // CAPE
    packed_ref[...] = jnp.zeros(packed_ref.shape, packed_ref.dtype)
    for prompt in range(prompts):
        counts_ref[prompt] = 0
    for place in range(received_ref.shape[0]):
        note = received_ref[place, samples * part :].astype(jnp.float32).astype(jnp.int32)
        for sample in range(samples):
            prompt = note[0, sample]
            rank = counts_ref[prompt]
            counts_ref[prompt] = rank + 1
            slots_ref[place * samples + sample] = prompt * 4 + rank
            packed_ref[prompt, pl.ds(pl.multiple_of(rank * part, part), part)] = received_ref[
                place, sample * part : (sample + 1) * part
            ]


def block_scores(rows, keys):
    return lax.dot_general(keys, rows, (((1,), (1,)), ((), ())), preferred_element_type=jnp.float32)


def block_softmax(raw):
    top = jnp.max(raw, axis=0, keepdims=True) * (SCALING * LOG2E)
    probs = jnp.exp2(raw * (SCALING * LOG2E) - top)
    total = jnp.sum(probs, axis=0, keepdims=True)
    return probs.astype(jnp.bfloat16), top, total


def block_product(probs, values):
    values = jnp.concatenate(
        [values[first : first + HD] for first in range(0, values.shape[0], HD)], axis=1
    )
    return jnp.dot(values, probs, preferred_element_type=jnp.float32)


def encode(out):
    largest = jnp.max(jnp.abs(out), axis=0, keepdims=True)
    power = jnp.floor(jnp.log2(jnp.maximum(largest, 2.0**-112) * 1.0001)) + 1.0
    code = jnp.clip(jnp.round(out * jnp.exp2(15.0 - power)), -32767.0, 32767.0)
    return code.astype(jnp.int32), power.astype(jnp.int32)


def prefix_kernel(chunk, q_ref, *refs):
    blocks, reply_ref = refs[:-1], refs[-1]
    slots, per = q_ref.shape[0], q_ref.shape[1]
    rows_of = per // 2
    wide = chunk * rows_of

    def rows_from(start):
        return jnp.concatenate(
            [
                q_ref[start : start + chunk, 0:rows_of].reshape(wide, HD),
                q_ref[start : start + chunk, rows_of:per].reshape(wide, HD),
            ],
            axis=0,
        )

    def finish(start, parts):
        top = functools.reduce(jnp.maximum, [part[1] for part in parts])
        weights = [jnp.exp2(part[1] - top) for part in parts]
        total = functools.reduce(jnp.add, [w * part[2] for w, part in zip(weights, parts)])
        share = 1.0 / total
        out = functools.reduce(jnp.add, [(w * share) * part[0] for w, part in zip(weights, parts)])
        log = jnp.round((top + jnp.log2(total)) * LSE_ONE).astype(jnp.int32)
        code, power = encode(out)
        packed = jnp.bitwise_or(
            jnp.left_shift(code[:, :wide], 16), jnp.bitwise_and(code[:, wide:], 0xFFFF)
        ).T
        rest = jnp.zeros((1, HD - 2 * per), jnp.int32)
        for slot in range(chunk):
            dest, rank = (start + slot) // CAPE, (start + slot) % CAPE
            first = slot * rows_of
            for part in range(rows_of // 4):
                reply_ref[dest, rank * (rows_of // 4) + part] = packed[
                    first + part * 4 : first + part * 4 + 4
                ]
            pieces = [
                array[:, begin : begin + rows_of]
                for array in (log, power)
                for begin in (first, wide + first)
            ]
            reply_ref[dest, CAPE * (rows_of // 4), rank : rank + 1] = jnp.concatenate(
                pieces + [rest], axis=1
            )

    starts = range(0, slots, chunk)
    stages = [(start, place) for start in starts for place in range(len(blocks))]
    rows = {start: rows_from(start) for start in starts}
    raw, waiting, parts = block_scores(rows[0], blocks[0][0]), None, []

    def product():
        (start, place), (probs, top, total) = waiting
        parts.append((block_product(probs, blocks[place][1]), top, total))
        if place + 1 == len(blocks):
            finish(start, parts)
            parts.clear()

    for number, stage in enumerate(stages):
        ready = raw
        if number + 1 < len(stages):
            later, block = stages[number + 1]
            raw = block_scores(rows[later], blocks[block][0])
        if waiting is not None:
            product()
        waiting = (stage, block_softmax(ready))
    product()


def select_kernel(samples, slots_ref, reply_ref, chosen_ref):
    body = (chosen_ref.shape[1] - 1) // samples
    for sample in range(chosen_ref.shape[0] * samples):
        slot = slots_ref[sample]
        prompt, rank = lax.shift_right_logical(slot, 2), lax.bitwise_and(slot, 3)
        place, which = sample // samples, sample % samples
        chosen_ref[place, which * body : (which + 1) * body] = reply_ref[
            prompt, pl.ds(rank * body, body)
        ]
        chosen_ref[place, samples * body, which : which + 1] = reply_ref[
            prompt, CAPE * body, pl.ds(rank, 1)
        ]


def suffix_kernel(length_ref, rows_ref, fresh_k_ref, fresh_v_ref, k_ref, v_ref, out_ref, log_ref):
    samples, positions = k_ref.shape[0], k_ref.shape[1]
    fresh = 16

    def padded(array):
        rest = jnp.zeros((fresh - array.shape[0], HD), jnp.float32)
        return jnp.concatenate([array.astype(jnp.float32), rest], axis=0).astype(jnp.bfloat16)

    per = rows_ref.shape[1] // KVH
    steps = per // GROUP
    column = lax.broadcasted_iota(jnp.int32, (per, positions), 1)
    step = lax.rem(lax.broadcasted_iota(jnp.int32, (per, fresh), 0), steps)
    causal = lax.broadcasted_iota(jnp.int32, (per, fresh), 1) <= step
    for sample in range(samples):
        live = column < length_ref[sample]
        for group in range(KVH):
            cols = slice(group * HD, (group + 1) * HD)
            rows = rows_ref[sample, group * per : (group + 1) * per]
            dims = (((1,), (1,)), ((), ()))
            cache_raw = lax.dot_general(
                rows, k_ref[sample, :, cols], dims, preferred_element_type=jnp.float32
            )
            fresh_raw = lax.dot_general(
                rows, padded(fresh_k_ref[sample, :, cols]), dims, preferred_element_type=jnp.float32
            )
            cache_raw = jnp.where(live, cache_raw, -jnp.inf)
            fresh_raw = jnp.where(causal, fresh_raw, -jnp.inf)
            top = jnp.maximum(
                jnp.max(cache_raw, axis=1, keepdims=True), jnp.max(fresh_raw, axis=1, keepdims=True)
            )
            cache_probs = jnp.exp2((cache_raw - top) * (SCALING * LOG2E))
            fresh_probs = jnp.exp2((fresh_raw - top) * (SCALING * LOG2E))
            total = jnp.sum(cache_probs, axis=1, keepdims=True) + jnp.sum(
                fresh_probs, axis=1, keepdims=True
            )
            acc = jnp.dot(
                cache_probs.astype(jnp.bfloat16),
                v_ref[sample, :, cols],
                preferred_element_type=jnp.float32,
            ) + jnp.dot(
                fresh_probs.astype(jnp.bfloat16),
                padded(fresh_v_ref[sample, :, cols]),
                preferred_element_type=jnp.float32,
            )
            here = slice(group * per, (group + 1) * per)
            out_ref[sample, here] = acc / total
            log_ref[sample, here] = jnp.broadcast_to(
                top * (SCALING * LOG2E) + jnp.log2(total), (per, HD)
            )


def combine_kernel(chosen_ref, suffix_out_ref, suffix_log_ref, out_ref):
    places, samples = chosen_ref.shape[0], suffix_out_ref.shape[0]
    steps = out_ref.shape[1]
    body = (chosen_ref.shape[1] - 1) // samples
    per = 8 * body
    row = lax.broadcasted_iota(jnp.int32, (per, HD), 0)
    lane = lax.broadcasted_iota(jnp.int32, (per, HD), 1)

    def turn(note, offset):
        spread = jnp.broadcast_to(note, (per, HD))
        return jnp.sum(jnp.where(lane == row + offset, spread, 0.0), axis=1, keepdims=True)

    for sample in range(samples):
        for group in range(KVH):
            logs, scales, codes = [], [], []
            for place in range(group, places, KVH):
                packed = jnp.concatenate(
                    [chosen_ref[place, sample * body + part] for part in range(body)], axis=0
                )
                high = jnp.right_shift(packed, 16)
                low = jnp.right_shift(jnp.left_shift(packed, 16), 16)
                codes.append(jnp.concatenate([high, low], axis=0).astype(jnp.float32))
                note = chosen_ref[place, samples * body, sample : sample + 1].astype(jnp.float32)
                logs.append(turn(note, 0) * (1.0 / LSE_ONE))
                scales.append(jnp.exp2(turn(note, per) - 15.0))
            peak = functools.reduce(jnp.maximum, logs)
            weights = [jnp.exp2(log - peak) for log in logs]
            weight_sum = functools.reduce(jnp.add, weights)
            prefix = functools.reduce(
                jnp.add, [(w * s) * c for w, s, c in zip(weights, scales, codes)]
            )
            prefix_log = peak + jnp.log2(weight_sum)
            first = group * per
            suffix_log = suffix_log_ref[sample, first : first + per][:, 0:1]
            suffix = suffix_out_ref[sample, first : first + per]
            top = jnp.maximum(prefix_log, suffix_log)
            prefix_weight = jnp.exp2(prefix_log - top)
            suffix_weight = jnp.exp2(suffix_log - top)
            whole = prefix_weight + suffix_weight
            result = (prefix_weight / (weight_sum * whole)) * prefix + (
                suffix_weight / whole
            ) * suffix
            for i in range(per // steps):
                head = first // steps + i
                out_ref[sample, :, head * HD : (head + 1) * HD] = result[
                    i * steps : (i + 1) * steps
                ].astype(jnp.bfloat16)


def local(
    queries,
    new_keys,
    new_values,
    suffix_keys,
    suffix_values,
    suffix_len,
    sample_prompt,
    prefix_keys,
    prefix_values,
):
    samples, steps, features = queries.shape
    heads = features // HD
    per = GROUP * steps
    seq_count = lax.axis_size("seq")
    engine_count = lax.axis_size("engine")
    positions = prefix_keys.shape[1]

    head_id = lax.rem(lax.axis_index("seq"), KVH).reshape(1)
    heads_of_block = pl.pallas_call(
        split_kernel,
        out_shape=[shape((2, positions, HD), jnp.bfloat16)] * KVH,
        in_specs=[SMEM] + [pl.BlockSpec(memory_space=pltpu.HBM)] * 2,
        out_specs=[VMEM] * KVH,
        scratch_shapes=[
            pltpu.VMEM((KVH, positions, HD), jnp.bfloat16),
            pltpu.SemaphoreType.DMA((KVH, 2)),
        ],
        compiler_params=params(16),
        name="split",
    )(
        head_id,
        pltpu.with_memory_space_constraint(prefix_keys, pltpu.HBM),
        pltpu.with_memory_space_constraint(prefix_values, pltpu.HBM),
    )

    def swap(array, near, swapped):
        pairs = []
        for place in range(seq_count):
            chip, core = place // 2, place % 2
            chip = (chip + near * (2 * core - 1)) % (seq_count // 2)
            pairs.append((place, 2 * chip + (1 - core if swapped else core)))
        return lax.ppermute(array, "seq", pairs)

    blocks = [
        heads_of_block[0],
        swap(heads_of_block[1], 0, True),
        swap(heads_of_block[2], 1, False),
        swap(heads_of_block[3], 1, True),
    ]

    rows, payload = pl.pallas_call(
        prepare_kernel,
        out_shape=(
            shape((samples, heads * steps, HD), jnp.bfloat16),
            shape((seq_count, samples * per + 8, HD), jnp.bfloat16),
        ),
        in_specs=[SMEM, VMEM],
        out_specs=(VMEM, VMEM),
        name="prepare",
    )(sample_prompt.reshape(samples), queries)
    received = lax.all_to_all(payload, "seq", split_axis=0, concat_axis=0, tiled=True)

    suffix_out, suffix_log = pl.pallas_call(
        suffix_kernel,
        out_shape=(
            shape((samples, heads * steps, HD), jnp.float32),
            shape((samples, heads * steps, HD), jnp.float32),
        ),
        in_specs=[SMEM] + [VMEM] * 5,
        out_specs=(VMEM, VMEM),
        compiler_params=params(16),
        name="suffix",
    )(
        suffix_len,
        rows,
        new_keys,
        new_values,
        suffix_keys,
        suffix_values,
    )

    suffix_out, suffix_log = pl.pallas_call(
        suffix_kernel,
        out_shape=(
            shape((samples, heads * steps, HD), jnp.float32),
            shape((samples, heads * steps, HD), jnp.float32),
        ),
        in_specs=[SMEM] + [VMEM] * 5,
        out_specs=(VMEM, VMEM),
        compiler_params=params(16),
        name="suffix",
    )(
        suffix_len,
        rows,
        new_keys,
        new_values,
        suffix_keys,
        suffix_values,
    )

    packed, slots = pl.pallas_call(
        functools.partial(pack_kernel, samples),
        out_shape=(
            pltpu.HBM((engine_count, CAPE * per, HD), jnp.bfloat16),
            shape((seq_count * samples,), jnp.int32),
        ),
        in_specs=[pl.BlockSpec(memory_space=pl.ANY), VMEM],
        out_specs=(VMEM, SMEM),
        scratch_shapes=[pltpu.SMEM((engine_count,), jnp.int32)],
        compiler_params=params(16),
        name="pack",
    )(suffix_log, received)
    dispatched = lax.all_to_all(packed, "engine", split_axis=0, concat_axis=0, tiled=True)

    reply = pl.pallas_call(
        functools.partial(prefix_kernel, 16),
        out_shape=shape((engine_count, CAPE * per // 8 + 1, 4, HD), jnp.int32),
        in_specs=[VMEM] * (1 + KVH),
        out_specs=VMEM,
        compiler_params=params(16),
        name="prefix",
    )(
        dispatched.reshape(engine_count * CAPE, per, HD),
        *[pltpu.with_memory_space_constraint(block, pltpu.VMEM) for block in blocks],
    )
    returned = lax.all_to_all(reply, "engine", split_axis=0, concat_axis=0, tiled=True)

    chosen = pl.pallas_call(
        functools.partial(select_kernel, samples),
        out_shape=shape((seq_count, samples * per // 8 + 1, 4, HD), jnp.int32),
        in_specs=[SMEM, VMEM],
        out_specs=VMEM,
        compiler_params=params(16),
        name="select",
    )(slots, returned)
    gathered = lax.all_to_all(chosen, "seq", split_axis=0, concat_axis=0, tiled=True)

    return pl.pallas_call(
        combine_kernel,
        out_shape=shape((samples, steps, features), jnp.bfloat16),
        in_specs=[VMEM] * 3,
        out_specs=VMEM,
        compiler_params=params(16),
        name="combine",
    )(gathered, suffix_out, suffix_log)


def solution(mesh):
    return jax.shard_map(
        local,
        mesh=mesh,
        in_specs=(
            P(("engine", "seq"), None, None),
            P(("engine", "seq"), None, None),
            P(("engine", "seq"), None, None),
            P(("engine", "seq"), None, None),
            P(("engine", "seq"), None, None),
            P(("engine", "seq")),
            P(("engine", "seq"), None),
            P("engine", "seq", None),
            P("engine", "seq", None),
        ),
        out_specs=P(("engine", "seq"), None, None),
        check_vma=False,
    )
```

```python
import functools
import math

import jax
import jax.numpy as jnp
from jax import lax
from jax.experimental import pallas as pl
from jax.experimental.pallas import tpu as pltpu
from jax.sharding import PartitionSpec as P

KVH = 4
GROUP = 8
HD = 128
CAPE = 3
SCALING = HD ** (-0.5)
LOG2E = math.log2(math.e)
LSE_ONE = float(2**20)
VMEM = pl.BlockSpec(memory_space=pltpu.VMEM)
SMEM = pl.BlockSpec(memory_space=pltpu.SMEM)


def params(mib):
    return pltpu.CompilerParams(vmem_limit_bytes=mib * 1024 * 1024)


def shape(dims, dtype):
    return jax.ShapeDtypeStruct(dims, dtype)


def prepare_kernel(prompt_ref, queries_ref, rows_ref, payload_ref):
    samples, steps, features = queries_ref.shape
    heads = features // HD
    part = heads * steps // KVH
    extra = payload_ref.shape[1] - samples * part
    lanes = lax.broadcasted_iota(jnp.int32, (extra, HD), 1)
    note = jnp.zeros((extra, HD), jnp.int32)
    for sample in range(samples):
        note = jnp.where(lanes == sample, prompt_ref[sample], note)
    note = note.astype(jnp.float32).astype(jnp.bfloat16)
    for sample in range(samples):
        for first in range(0, heads, 4):
            tile = jnp.concatenate(
                [
                    queries_ref[sample, :, (first + i) * HD : (first + i + 1) * HD].astype(jnp.float32)
                    for i in range(4)
                ],
                axis=0,
            ).astype(jnp.bfloat16)
            row = first * steps
            rows_ref[sample, row : row + 4 * steps] = tile
            group, row = row // part, row % part
            for place in range(group, payload_ref.shape[0], KVH):
                payload_ref[place, sample * part + row : sample * part + row + 4 * steps] = tile
    for place in range(payload_ref.shape[0]):
        payload_ref[place, samples * part :] = note


def split_kernel(_, head_ref, k_ref, v_ref, *refs):
    outs, held, sems = refs[:KVH], refs[KVH], refs[KVH + 1]
    copies = []
    for place, out in enumerate(outs):
        head = jnp.bitwise_xor(head_ref[0], place)
        cols = pl.ds(pl.multiple_of(head * HD, HD), HD)
        keys = pltpu.make_async_copy(k_ref.at[0, :, cols], out.at[0], sems.at[place, 0])
        values = pltpu.make_async_copy(v_ref.at[0, :, cols], held.at[place], sems.at[place, 1])
        copies.append((keys, values))
    for keys, values in copies:
        values.start()
    for keys, values in copies:
        keys.start()
    for place, out in enumerate(outs):
        copies[place][1].wait()
        for first in range(0, held.shape[1], HD):
            out[1, first : first + HD] = held[place, first : first + HD].T
    for keys, values in copies:
        keys.wait()


def pack_kernel(samples, _, received_ref, packed_ref, slots_ref, counts_ref):
    prompts, part = packed_ref.shape[0], packed_ref.shape[1] // CAPE
    packed_ref[...] = jnp.zeros(packed_ref.shape, packed_ref.dtype)
    for prompt in range(prompts):
        counts_ref[prompt] = 0
    for place in range(received_ref.shape[0]):
        note = received_ref[place, samples * part :].astype(jnp.float32).astype(jnp.int32)
        for sample in range(samples):
            prompt = note[0, sample]
            rank = counts_ref[prompt]
            counts_ref[prompt] = rank + 1
            slots_ref[place * samples + sample] = prompt * 4 + rank
            packed_ref[prompt, pl.ds(pl.multiple_of(rank * part, part), part)] = received_ref[
                place, sample * part : (sample + 1) * part
            ]


def block_scores(rows, keys):
    return lax.dot_general(keys, rows, (((1,), (1,)), ((), ())), preferred_element_type=jnp.float32)


def block_softmax(raw):
    top = jnp.max(raw, axis=0, keepdims=True)
    probs = jnp.exp2((raw - top) * (SCALING * LOG2E))
    total = jnp.sum(probs, axis=0, keepdims=True)
    return probs.astype(jnp.bfloat16), top * (SCALING * LOG2E), total


def block_product(probs, values):
    values = jnp.concatenate(
        [values[first : first + HD] for first in range(0, values.shape[0], HD)], axis=1
    )
    return jnp.dot(values, probs, preferred_element_type=jnp.float32)


def encode(out):
    largest = jnp.max(jnp.abs(out), axis=0, keepdims=True)
    power = jnp.floor(jnp.log2(jnp.maximum(largest, 2.0**-112) * 1.0001)) + 1.0
    code = jnp.clip(jnp.round(out * jnp.exp2(15.0 - power)), -32767.0, 32767.0)
    return code.astype(jnp.int32), power.astype(jnp.int32)


def prefix_kernel(chunk, q_ref, *refs):
    blocks, reply_ref = refs[:-1], refs[-1]
    slots, per = q_ref.shape[0], q_ref.shape[1]
    rows_of = per // 2
    wide = chunk * rows_of

    def rows_from(start):
        return jnp.concatenate(
            [
                q_ref[start : start + chunk, 0:rows_of].reshape(wide, HD),
                q_ref[start : start + chunk, rows_of:per].reshape(wide, HD),
            ],
            axis=0,
        )

    def finish(start, parts):
        top = functools.reduce(jnp.maximum, [part[1] for part in parts])
        weights = [jnp.exp2(part[1] - top) for part in parts]
        total = functools.reduce(jnp.add, [w * part[2] for w, part in zip(weights, parts)])
        share = 1.0 / total
        out = functools.reduce(jnp.add, [(w * share) * part[0] for w, part in zip(weights, parts)])
        log = jnp.round((top + jnp.log2(total)) * LSE_ONE).astype(jnp.int32)
        code, power = encode(out)
        packed = jnp.bitwise_or(
            jnp.left_shift(code[:, :wide], 16), jnp.bitwise_and(code[:, wide:], 0xFFFF)
        ).T
        rest = jnp.zeros((1, HD - 2 * per), jnp.int32)
        for slot in range(chunk):
            dest, rank = (start + slot) // CAPE, (start + slot) % CAPE
            first = slot * rows_of
            for part in range(rows_of // 4):
                reply_ref[dest, rank * (rows_of // 4) + part] = packed[
                    first + part * 4 : first + part * 4 + 4
                ]
            pieces = [
                array[:, begin : begin + rows_of]
                for array in (log, power)
                for begin in (first, wide + first)
            ]
            reply_ref[dest, CAPE * (rows_of // 4), rank : rank + 1] = jnp.concatenate(
                pieces + [rest], axis=1
            )

    starts = range(0, slots, chunk)
    stages = [(start, place) for start in starts for place in range(len(blocks))]
    rows = {start: rows_from(start) for start in starts}
    raw, waiting, parts = block_scores(rows[0], blocks[0][0]), None, []

    def product():
        (start, place), (probs, top, total) = waiting
        parts.append((block_product(probs, blocks[place][1]), top, total))
        if place + 1 == len(blocks):
            finish(start, parts)
            parts.clear()

    for number, stage in enumerate(stages):
        ready = raw
        if number + 1 < len(stages):
            later, block = stages[number + 1]
            raw = block_scores(rows[later], blocks[block][0])
        if waiting is not None:
            product()
        waiting = (stage, block_softmax(ready))
    product()


def select_kernel(samples, slots_ref, reply_ref, chosen_ref):
    body = (chosen_ref.shape[1] - 1) // samples
    for sample in range(chosen_ref.shape[0] * samples):
        slot = slots_ref[sample]
        prompt, rank = lax.shift_right_logical(slot, 2), lax.bitwise_and(slot, 3)
        place, which = sample // samples, sample % samples
        chosen_ref[place, which * body : (which + 1) * body] = reply_ref[
            prompt, pl.ds(rank * body, body)
        ]
        chosen_ref[place, samples * body, which : which + 1] = reply_ref[
            prompt, CAPE * body, pl.ds(rank, 1)
        ]


def suffix_kernel(length_ref, rows_ref, fresh_k_ref, fresh_v_ref, k_ref, v_ref, out_ref, log_ref):
    samples, positions = k_ref.shape[0], k_ref.shape[1]
    fresh = 16

    def padded(array):
        rest = jnp.zeros((fresh - array.shape[0], HD), jnp.float32)
        return jnp.concatenate([array.astype(jnp.float32), rest], axis=0).astype(jnp.bfloat16)

    per = rows_ref.shape[1] // KVH
    steps = per // GROUP
    column = lax.broadcasted_iota(jnp.int32, (per, positions), 1)
    step = lax.rem(lax.broadcasted_iota(jnp.int32, (per, fresh), 0), steps)
    causal = lax.broadcasted_iota(jnp.int32, (per, fresh), 1) <= step
    for sample in range(samples):
        live = column < length_ref[sample]
        for group in range(KVH):
            cols = slice(group * HD, (group + 1) * HD)
            rows = rows_ref[sample, group * per : (group + 1) * per]
            dims = (((1,), (1,)), ((), ()))
            cache_raw = lax.dot_general(
                rows, k_ref[sample, :, cols], dims, preferred_element_type=jnp.float32
            )
            fresh_raw = lax.dot_general(
                rows, padded(fresh_k_ref[sample, :, cols]), dims, preferred_element_type=jnp.float32
            )
            cache_raw = jnp.where(live, cache_raw, -jnp.inf)
            fresh_raw = jnp.where(causal, fresh_raw, -jnp.inf)
            top = jnp.maximum(
                jnp.max(cache_raw, axis=1, keepdims=True), jnp.max(fresh_raw, axis=1, keepdims=True)
            )
            cache_probs = jnp.exp2((cache_raw - top) * (SCALING * LOG2E))
            fresh_probs = jnp.exp2((fresh_raw - top) * (SCALING * LOG2E))
            total = jnp.sum(cache_probs, axis=1, keepdims=True) + jnp.sum(
                fresh_probs, axis=1, keepdims=True
            )
            acc = jnp.dot(
                cache_probs.astype(jnp.bfloat16),
                v_ref[sample, :, cols],
                preferred_element_type=jnp.float32,
            ) + jnp.dot(
                fresh_probs.astype(jnp.bfloat16),
                padded(fresh_v_ref[sample, :, cols]),
                preferred_element_type=jnp.float32,
            )
            here = slice(group * per, (group + 1) * per)
            out_ref[sample, here] = acc / total
            log_ref[sample, here] = jnp.broadcast_to(
                top * (SCALING * LOG2E) + jnp.log2(total), (per, HD)
            )


def combine_kernel(chosen_ref, suffix_out_ref, suffix_log_ref, out_ref):
    places, samples = chosen_ref.shape[0], suffix_out_ref.shape[0]
    steps = out_ref.shape[1]
    body = (chosen_ref.shape[1] - 1) // samples
    per = 8 * body
    row = lax.broadcasted_iota(jnp.int32, (per, HD), 0)
    lane = lax.broadcasted_iota(jnp.int32, (per, HD), 1)

    def turn(note, offset):
        spread = jnp.broadcast_to(note, (per, HD))
        return jnp.sum(jnp.where(lane == row + offset, spread, 0.0), axis=1, keepdims=True)

    for sample in range(samples):
        for group in range(KVH):
            logs, scales, codes = [], [], []
            for place in range(group, places, KVH):
                packed = jnp.concatenate(
                    [chosen_ref[place, sample * body + part] for part in range(body)], axis=0
                )
                high = jnp.right_shift(packed, 16)
                low = jnp.right_shift(jnp.left_shift(packed, 16), 16)
                codes.append(jnp.concatenate([high, low], axis=0).astype(jnp.float32))
                note = chosen_ref[place, samples * body, sample : sample + 1].astype(jnp.float32)
                logs.append(turn(note, 0) * (1.0 / LSE_ONE))
                scales.append(jnp.exp2(turn(note, per) - 15.0))
            peak = functools.reduce(jnp.maximum, logs)
            weights = [jnp.exp2(log - peak) for log in logs]
            weight_sum = functools.reduce(jnp.add, weights)
            prefix = functools.reduce(
                jnp.add, [(w * s) * c for w, s, c in zip(weights, scales, codes)]
            )
            prefix_log = peak + jnp.log2(weight_sum)
            first = group * per
            suffix_log = suffix_log_ref[sample, first : first + per][:, 0:1]
            suffix = suffix_out_ref[sample, first : first + per]
            top = jnp.maximum(prefix_log, suffix_log)
            prefix_weight = jnp.exp2(prefix_log - top)
            suffix_weight = jnp.exp2(suffix_log - top)
            whole = prefix_weight + suffix_weight
            result = (prefix_weight / (weight_sum * whole)) * prefix + (
                suffix_weight / whole
            ) * suffix
            for i in range(per // steps):
                head = first // steps + i
                out_ref[sample, :, head * HD : (head + 1) * HD] = result[
                    i * steps : (i + 1) * steps
                ].astype(jnp.bfloat16)


def local(
    queries,
    new_keys,
    new_values,
    suffix_keys,
    suffix_values,
    suffix_len,
    sample_prompt,
    prefix_keys,
    prefix_values,
):
    samples, steps, features = queries.shape
    heads = features // HD
    per = GROUP * steps
    seq_count = lax.axis_size("seq")
    engine_count = lax.axis_size("engine")
    positions = prefix_keys.shape[1]

    rows, payload = pl.pallas_call(
        prepare_kernel,
        out_shape=(
            shape((samples, heads * steps, HD), jnp.bfloat16),
            shape((seq_count, samples * per + 8, HD), jnp.bfloat16),
        ),
        in_specs=[SMEM, VMEM],
        out_specs=(VMEM, VMEM),
        name="prepare",
    )(sample_prompt.reshape(samples), queries)
    received = lax.all_to_all(payload, "seq", split_axis=0, concat_axis=0, tiled=True)

    suffix_out, suffix_log = pl.pallas_call(
        suffix_kernel,
        out_shape=(
            shape((samples, heads * steps, HD), jnp.float32),
            shape((samples, heads * steps, HD), jnp.float32),
        ),
        in_specs=[SMEM] + [VMEM] * 5,
        out_specs=(VMEM, VMEM),
        compiler_params=params(16),
        name="suffix",
    )(
        suffix_len,
        rows,
        new_keys,
        new_values,
        suffix_keys,
        suffix_values,
    )

    suffix_out, suffix_log = pl.pallas_call(
        suffix_kernel,
        out_shape=(
            shape((samples, heads * steps, HD), jnp.float32),
            shape((samples, heads * steps, HD), jnp.float32),
        ),
        in_specs=[SMEM] + [VMEM] * 5,
        out_specs=(VMEM, VMEM),
        compiler_params=params(16),
        name="suffix",
    )(
        suffix_len,
        rows,
        new_keys,
        new_values,
        suffix_keys,
        suffix_values,
    )

    head_id = lax.rem(lax.axis_index("seq"), KVH).reshape(1)
    heads_of_block = pl.pallas_call(
        split_kernel,
        out_shape=[shape((2, positions, HD), jnp.bfloat16)] * KVH,
        in_specs=[pl.BlockSpec(memory_space=pl.ANY), SMEM]
        + [pl.BlockSpec(memory_space=pltpu.HBM)] * 2,
        out_specs=[VMEM] * KVH,
        scratch_shapes=[
            pltpu.VMEM((KVH, positions, HD), jnp.bfloat16),
            pltpu.SemaphoreType.DMA((KVH, 2)),
        ],
        compiler_params=params(16),
        name="split",
    )(
        suffix_log,
        head_id,
        pltpu.with_memory_space_constraint(prefix_keys, pltpu.HBM),
        pltpu.with_memory_space_constraint(prefix_values, pltpu.HBM),
    )

    def swap(array, near, swapped):
        pairs = []
        for place in range(seq_count):
            chip, core = place // 2, place % 2
            chip = (chip + near * (2 * core - 1)) % (seq_count // 2)
            pairs.append((place, 2 * chip + (1 - core if swapped else core)))
        return lax.ppermute(array, "seq", pairs)

    blocks = [
        heads_of_block[0],
        swap(heads_of_block[1], 0, True),
        swap(heads_of_block[2], 1, False),
        swap(heads_of_block[3], 1, True),
    ]

    packed, slots = pl.pallas_call(
        functools.partial(pack_kernel, samples),
        out_shape=(
            pltpu.HBM((engine_count, CAPE * per, HD), jnp.bfloat16),
            shape((seq_count * samples,), jnp.int32),
        ),
        in_specs=[pl.BlockSpec(memory_space=pl.ANY), VMEM],
        out_specs=(VMEM, SMEM),
        scratch_shapes=[pltpu.SMEM((engine_count,), jnp.int32)],
        compiler_params=params(16),
        name="pack",
    )(heads_of_block[0], received)
    dispatched = lax.all_to_all(packed, "engine", split_axis=0, concat_axis=0, tiled=True)

    reply = pl.pallas_call(
        functools.partial(prefix_kernel, 16),
        out_shape=shape((engine_count, CAPE * per // 8 + 1, 4, HD), jnp.int32),
        in_specs=[VMEM] * (1 + KVH),
        out_specs=VMEM,
        compiler_params=params(16),
        name="prefix",
    )(
        dispatched.reshape(engine_count * CAPE, per, HD),
        *[pltpu.with_memory_space_constraint(block, pltpu.VMEM) for block in blocks],
    )
    returned = lax.all_to_all(reply, "engine", split_axis=0, concat_axis=0, tiled=True)

    chosen = pl.pallas_call(
        functools.partial(select_kernel, samples),
        out_shape=shape((seq_count, samples * per // 8 + 1, 4, HD), jnp.int32),
        in_specs=[SMEM, VMEM],
        out_specs=VMEM,
        compiler_params=params(16),
        name="select",
    )(slots, returned)
    gathered = lax.all_to_all(chosen, "seq", split_axis=0, concat_axis=0, tiled=True)

    return pl.pallas_call(
        combine_kernel,
        out_shape=shape((samples, steps, features), jnp.bfloat16),
        in_specs=[VMEM] * 3,
        out_specs=VMEM,
        compiler_params=params(16),
        name="combine",
    )(gathered, suffix_out, suffix_log)


def solution(mesh):
    return jax.shard_map(
        local,
        mesh=mesh,
        in_specs=(
            P(("engine", "seq"), None, None),
            P(("engine", "seq"), None, None),
            P(("engine", "seq"), None, None),
            P(("engine", "seq"), None, None),
            P(("engine", "seq"), None, None),
            P(("engine", "seq")),
            P(("engine", "seq"), None),
            P("engine", "seq", None),
            P("engine", "seq", None),
        ),
        out_specs=P(("engine", "seq"), None, None),
        check_vma=False,
    )
```

```python
import functools
import math

import jax
import jax.numpy as jnp
from jax import lax
from jax.experimental import pallas as pl
from jax.experimental.pallas import tpu as pltpu
from jax.sharding import PartitionSpec as P

KVH = 4
GROUP = 8
HD = 128
CAPE = 3
SCALING = HD ** (-0.5)
LOG2E = math.log2(math.e)
LSE_ONE = float(2**20)
VMEM = pl.BlockSpec(memory_space=pltpu.VMEM)
SMEM = pl.BlockSpec(memory_space=pltpu.SMEM)


def params(mib):
    return pltpu.CompilerParams(vmem_limit_bytes=mib * 1024 * 1024)


def shape(dims, dtype):
    return jax.ShapeDtypeStruct(dims, dtype)


def prepare_kernel(prompt_ref, queries_ref, rows_ref, payload_ref):
    samples, steps, features = queries_ref.shape
    heads = features // HD
    part = heads * steps // KVH
    extra = payload_ref.shape[1] - samples * part
    lanes = lax.broadcasted_iota(jnp.int32, (extra, HD), 1)
    note = jnp.zeros((extra, HD), jnp.int32)
    for sample in range(samples):
        note = jnp.where(lanes == sample, prompt_ref[sample], note)
    note = note.astype(jnp.float32).astype(jnp.bfloat16)
    for sample in range(samples):
        for first in range(0, heads, 4):
            tile = jnp.concatenate(
                [
                    queries_ref[sample, :, (first + i) * HD : (first + i + 1) * HD].astype(jnp.float32)
                    for i in range(4)
                ],
                axis=0,
            ).astype(jnp.bfloat16)
            row = first * steps
            rows_ref[sample, row : row + 4 * steps] = tile
            group, row = row // part, row % part
            for place in range(group, payload_ref.shape[0], KVH):
                payload_ref[place, sample * part + row : sample * part + row + 4 * steps] = tile
    for place in range(payload_ref.shape[0]):
        payload_ref[place, samples * part :] = note


def split_kernel(head_ref, k_ref, v_ref, *refs):
    outs, held, sems = refs[:KVH], refs[KVH], refs[KVH + 1]
    copies = []
    for place, out in enumerate(outs):
        head = jnp.bitwise_xor(head_ref[0], place)
        cols = pl.ds(pl.multiple_of(head * HD, HD), HD)
        keys = pltpu.make_async_copy(k_ref.at[0, :, cols], out.at[0], sems.at[place, 0])
        values = pltpu.make_async_copy(v_ref.at[0, :, cols], held.at[place], sems.at[place, 1])
        copies.append((keys, values))
    for keys, values in copies:
        values.start()
    for keys, values in copies:
        keys.start()
    for place, out in enumerate(outs):
        copies[place][1].wait()
        for first in range(0, held.shape[1], HD):
            out[1, first : first + HD] = held[place, first : first + HD].T
    for keys, values in copies:
        keys.wait()


def pack_kernel(samples, received_ref, packed_ref, slots_ref, counts_ref):
    prompts, part = packed_ref.shape[0], packed_ref.shape[1] // CAPE
    packed_ref[...] = jnp.zeros(packed_ref.shape, packed_ref.dtype)
    for prompt in range(prompts):
        counts_ref[prompt] = 0
    for place in range(received_ref.shape[0]):
        note = received_ref[place, samples * part :].astype(jnp.float32).astype(jnp.int32)
        for sample in range(samples):
            prompt = note[0, sample]
            rank = counts_ref[prompt]
            counts_ref[prompt] = rank + 1
            slots_ref[place * samples + sample] = prompt * 4 + rank
            packed_ref[prompt, pl.ds(pl.multiple_of(rank * part, part), part)] = received_ref[
                place, sample * part : (sample + 1) * part
            ]


def block_scores(rows, keys):
    return lax.dot_general(keys, rows, (((1,), (1,)), ((), ())), preferred_element_type=jnp.float32)


def block_softmax(raw):
    top = jnp.max(raw, axis=0, keepdims=True)
    probs = jnp.exp2((raw - top) * (SCALING * LOG2E))
    total = jnp.sum(probs, axis=0, keepdims=True)
    return probs.astype(jnp.bfloat16), top * (SCALING * LOG2E), total


def block_product(probs, values):
    values = jnp.concatenate(
        [values[first : first + HD] for first in range(0, values.shape[0], HD)], axis=1
    )
    return jnp.dot(values, probs, preferred_element_type=jnp.float32)


def encode(out):
    largest = jnp.max(jnp.abs(out), axis=0, keepdims=True)
    power = jnp.floor(jnp.log2(jnp.maximum(largest, 2.0**-112) * 1.0001)) + 1.0
    code = jnp.clip(jnp.round(out * jnp.exp2(15.0 - power)), -32767.0, 32767.0)
    return code.astype(jnp.int32), power.astype(jnp.int32)


def prefix_kernel(chunk, _, q_ref, *refs):
    blocks, reply_ref = refs[:-1], refs[-1]
    slots, per = q_ref.shape[0], q_ref.shape[1]
    rows_of = per // 2
    wide = chunk * rows_of

    def rows_from(start):
        return jnp.concatenate(
            [
                q_ref[start : start + chunk, 0:rows_of].reshape(wide, HD),
                q_ref[start : start + chunk, rows_of:per].reshape(wide, HD),
            ],
            axis=0,
        )

    def finish(start, parts):
        top = functools.reduce(jnp.maximum, [part[1] for part in parts])
        weights = [jnp.exp2(part[1] - top) for part in parts]
        total = functools.reduce(jnp.add, [w * part[2] for w, part in zip(weights, parts)])
        share = 1.0 / total
        out = functools.reduce(jnp.add, [(w * share) * part[0] for w, part in zip(weights, parts)])
        log = jnp.round((top + jnp.log2(total)) * LSE_ONE).astype(jnp.int32)
        code, power = encode(out)
        packed = jnp.bitwise_or(
            jnp.left_shift(code[:, :wide], 16), jnp.bitwise_and(code[:, wide:], 0xFFFF)
        ).T
        rest = jnp.zeros((1, HD - 2 * per), jnp.int32)
        for slot in range(chunk):
            dest, rank = (start + slot) // CAPE, (start + slot) % CAPE
            first = slot * rows_of
            for part in range(rows_of // 4):
                reply_ref[dest, rank * (rows_of // 4) + part] = packed[
                    first + part * 4 : first + part * 4 + 4
                ]
            pieces = [
                array[:, begin : begin + rows_of]
                for array in (log, power)
                for begin in (first, wide + first)
            ]
            reply_ref[dest, CAPE * (rows_of // 4), rank : rank + 1] = jnp.concatenate(
                pieces + [rest], axis=1
            )

    starts = range(0, slots, chunk)
    stages = [(start, place) for start in starts for place in range(len(blocks))]
    rows = {start: rows_from(start) for start in starts}
    raw, waiting, parts = block_scores(rows[0], blocks[0][0]), None, []

    def product():
        (start, place), (probs, top, total) = waiting
        parts.append((block_product(probs, blocks[place][1]), top, total))
        if place + 1 == len(blocks):
            finish(start, parts)
            parts.clear()

    for number, stage in enumerate(stages):
        ready = raw
        if number + 1 < len(stages):
            later, block = stages[number + 1]
            raw = block_scores(rows[later], blocks[block][0])
        if waiting is not None:
            product()
        waiting = (stage, block_softmax(ready))
    product()


def select_kernel(samples, slots_ref, reply_ref, chosen_ref):
    body = (chosen_ref.shape[1] - 1) // samples
    for sample in range(chosen_ref.shape[0] * samples):
        slot = slots_ref[sample]
        prompt, rank = lax.shift_right_logical(slot, 2), lax.bitwise_and(slot, 3)
        place, which = sample // samples, sample % samples
        chosen_ref[place, which * body : (which + 1) * body] = reply_ref[
            prompt, pl.ds(rank * body, body)
        ]
        chosen_ref[place, samples * body, which : which + 1] = reply_ref[
            prompt, CAPE * body, pl.ds(rank, 1)
        ]


def suffix_kernel(length_ref, rows_ref, fresh_k_ref, fresh_v_ref, k_ref, v_ref, out_ref, log_ref):
    samples, positions = k_ref.shape[0], k_ref.shape[1]
    fresh = 16

    def padded(array):
        rest = jnp.zeros((fresh - array.shape[0], HD), jnp.float32)
        return jnp.concatenate([array.astype(jnp.float32), rest], axis=0).astype(jnp.bfloat16)

    per = rows_ref.shape[1] // KVH
    steps = per // GROUP
    column = lax.broadcasted_iota(jnp.int32, (per, positions), 1)
    step = lax.rem(lax.broadcasted_iota(jnp.int32, (per, fresh), 0), steps)
    causal = lax.broadcasted_iota(jnp.int32, (per, fresh), 1) <= step
    for sample in range(samples):
        live = column < length_ref[sample]
        for group in range(KVH):
            cols = slice(group * HD, (group + 1) * HD)
            rows = rows_ref[sample, group * per : (group + 1) * per]
            dims = (((1,), (1,)), ((), ()))
            cache_raw = lax.dot_general(
                rows, k_ref[sample, :, cols], dims, preferred_element_type=jnp.float32
            )
            fresh_raw = lax.dot_general(
                rows, padded(fresh_k_ref[sample, :, cols]), dims, preferred_element_type=jnp.float32
            )
            cache_raw = jnp.where(live, cache_raw, -jnp.inf)
            fresh_raw = jnp.where(causal, fresh_raw, -jnp.inf)
            top = jnp.maximum(
                jnp.max(cache_raw, axis=1, keepdims=True), jnp.max(fresh_raw, axis=1, keepdims=True)
            )
            cache_probs = jnp.exp2((cache_raw - top) * (SCALING * LOG2E))
            fresh_probs = jnp.exp2((fresh_raw - top) * (SCALING * LOG2E))
            total = jnp.sum(cache_probs, axis=1, keepdims=True) + jnp.sum(
                fresh_probs, axis=1, keepdims=True
            )
            acc = jnp.dot(
                cache_probs.astype(jnp.bfloat16),
                v_ref[sample, :, cols],
                preferred_element_type=jnp.float32,
            ) + jnp.dot(
                fresh_probs.astype(jnp.bfloat16),
                padded(fresh_v_ref[sample, :, cols]),
                preferred_element_type=jnp.float32,
            )
            here = slice(group * per, (group + 1) * per)
            out_ref[sample, here] = acc / total
            log_ref[sample, here] = jnp.broadcast_to(
                top * (SCALING * LOG2E) + jnp.log2(total), (per, HD)
            )


def combine_kernel(chosen_ref, suffix_out_ref, suffix_log_ref, out_ref):
    places, samples = chosen_ref.shape[0], suffix_out_ref.shape[0]
    steps = out_ref.shape[1]
    body = (chosen_ref.shape[1] - 1) // samples
    per = 8 * body
    row = lax.broadcasted_iota(jnp.int32, (per, HD), 0)
    lane = lax.broadcasted_iota(jnp.int32, (per, HD), 1)

    def turn(note, offset):
        spread = jnp.broadcast_to(note, (per, HD))
        return jnp.sum(jnp.where(lane == row + offset, spread, 0.0), axis=1, keepdims=True)

    for sample in range(samples):
        for group in range(KVH):
            logs, scales, codes = [], [], []
            for place in range(group, places, KVH):
                packed = jnp.concatenate(
                    [chosen_ref[place, sample * body + part] for part in range(body)], axis=0
                )
                high = jnp.right_shift(packed, 16)
                low = jnp.right_shift(jnp.left_shift(packed, 16), 16)
                codes.append(jnp.concatenate([high, low], axis=0).astype(jnp.float32))
                note = chosen_ref[place, samples * body, sample : sample + 1].astype(jnp.float32)
                logs.append(turn(note, 0) * (1.0 / LSE_ONE))
                scales.append(jnp.exp2(turn(note, per) - 15.0))
            peak = functools.reduce(jnp.maximum, logs)
            weights = [jnp.exp2(log - peak) for log in logs]
            weight_sum = functools.reduce(jnp.add, weights)
            prefix = functools.reduce(
                jnp.add, [(w * s) * c for w, s, c in zip(weights, scales, codes)]
            )
            prefix_log = peak + jnp.log2(weight_sum)
            first = group * per
            suffix_log = suffix_log_ref[sample, first : first + per][:, 0:1]
            suffix = suffix_out_ref[sample, first : first + per]
            top = jnp.maximum(prefix_log, suffix_log)
            prefix_weight = jnp.exp2(prefix_log - top)
            suffix_weight = jnp.exp2(suffix_log - top)
            whole = prefix_weight + suffix_weight
            result = (prefix_weight / (weight_sum * whole)) * prefix + (
                suffix_weight / whole
            ) * suffix
            for i in range(per // steps):
                head = first // steps + i
                out_ref[sample, :, head * HD : (head + 1) * HD] = result[
                    i * steps : (i + 1) * steps
                ].astype(jnp.bfloat16)


def local(
    queries,
    new_keys,
    new_values,
    suffix_keys,
    suffix_values,
    suffix_len,
    sample_prompt,
    prefix_keys,
    prefix_values,
):
    samples, steps, features = queries.shape
    heads = features // HD
    per = GROUP * steps
    seq_count = lax.axis_size("seq")
    engine_count = lax.axis_size("engine")
    positions = prefix_keys.shape[1]

    head_id = lax.rem(lax.axis_index("seq"), KVH).reshape(1)
    heads_of_block = pl.pallas_call(
        split_kernel,
        out_shape=[shape((2, positions, HD), jnp.bfloat16)] * KVH,
        in_specs=[SMEM] + [pl.BlockSpec(memory_space=pltpu.HBM)] * 2,
        out_specs=[VMEM] * KVH,
        scratch_shapes=[
            pltpu.VMEM((KVH, positions, HD), jnp.bfloat16),
            pltpu.SemaphoreType.DMA((KVH, 2)),
        ],
        compiler_params=params(16),
        name="split",
    )(
        head_id,
        pltpu.with_memory_space_constraint(prefix_keys, pltpu.HBM),
        pltpu.with_memory_space_constraint(prefix_values, pltpu.HBM),
    )

    def swap(array, near, swapped):
        pairs = []
        for place in range(seq_count):
            chip, core = place // 2, place % 2
            chip = (chip + near * (2 * core - 1)) % (seq_count // 2)
            pairs.append((place, 2 * chip + (1 - core if swapped else core)))
        return lax.ppermute(array, "seq", pairs)

    blocks = [
        heads_of_block[0],
        swap(heads_of_block[1], 0, True),
        swap(heads_of_block[2], 1, False),
        swap(heads_of_block[3], 1, True),
    ]

    rows, payload = pl.pallas_call(
        prepare_kernel,
        out_shape=(
            shape((samples, heads * steps, HD), jnp.bfloat16),
            shape((seq_count, samples * per + 8, HD), jnp.bfloat16),
        ),
        in_specs=[SMEM, VMEM],
        out_specs=(VMEM, VMEM),
        name="prepare",
    )(sample_prompt.reshape(samples), queries)
    received = lax.all_to_all(payload, "seq", split_axis=0, concat_axis=0, tiled=True)

    suffix_out, suffix_log = pl.pallas_call(
        suffix_kernel,
        out_shape=(
            shape((samples, heads * steps, HD), jnp.float32),
            shape((samples, heads * steps, HD), jnp.float32),
        ),
        in_specs=[SMEM] + [VMEM] * 5,
        out_specs=(VMEM, VMEM),
        compiler_params=params(16),
        name="suffix",
    )(
        suffix_len,
        rows,
        new_keys,
        new_values,
        suffix_keys,
        suffix_values,
    )

    suffix_out, suffix_log = pl.pallas_call(
        suffix_kernel,
        out_shape=(
            shape((samples, heads * steps, HD), jnp.float32),
            shape((samples, heads * steps, HD), jnp.float32),
        ),
        in_specs=[SMEM] + [VMEM] * 5,
        out_specs=(VMEM, VMEM),
        compiler_params=params(16),
        name="suffix",
    )(
        suffix_len,
        rows,
        new_keys,
        new_values,
        suffix_keys,
        suffix_values,
    )

    packed, slots = pl.pallas_call(
        functools.partial(pack_kernel, samples),
        out_shape=(
            pltpu.HBM((engine_count, CAPE * per, HD), jnp.bfloat16),
            shape((seq_count * samples,), jnp.int32),
        ),
        in_specs=[VMEM],
        out_specs=(VMEM, SMEM),
        scratch_shapes=[pltpu.SMEM((engine_count,), jnp.int32)],
        compiler_params=params(16),
        name="pack",
    )(received)
    dispatched = lax.all_to_all(packed, "engine", split_axis=0, concat_axis=0, tiled=True)

    reply = pl.pallas_call(
        functools.partial(prefix_kernel, 16),
        out_shape=shape((engine_count, CAPE * per // 8 + 1, 4, HD), jnp.int32),
        in_specs=[pl.BlockSpec(memory_space=pl.ANY)] + [VMEM] * (1 + KVH),
        out_specs=VMEM,
        compiler_params=params(16),
        name="prefix",
    )(
        suffix_log,
        dispatched.reshape(engine_count * CAPE, per, HD),
        *[pltpu.with_memory_space_constraint(block, pltpu.VMEM) for block in blocks],
    )
    returned = lax.all_to_all(reply, "engine", split_axis=0, concat_axis=0, tiled=True)

    chosen = pl.pallas_call(
        functools.partial(select_kernel, samples),
        out_shape=shape((seq_count, samples * per // 8 + 1, 4, HD), jnp.int32),
        in_specs=[SMEM, VMEM],
        out_specs=VMEM,
        compiler_params=params(16),
        name="select",
    )(slots, returned)
    gathered = lax.all_to_all(chosen, "seq", split_axis=0, concat_axis=0, tiled=True)

    return pl.pallas_call(
        combine_kernel,
        out_shape=shape((samples, steps, features), jnp.bfloat16),
        in_specs=[VMEM] * 3,
        out_specs=VMEM,
        compiler_params=params(16),
        name="combine",
    )(gathered, suffix_out, suffix_log)


def solution(mesh):
    return jax.shard_map(
        local,
        mesh=mesh,
        in_specs=(
            P(("engine", "seq"), None, None),
            P(("engine", "seq"), None, None),
            P(("engine", "seq"), None, None),
            P(("engine", "seq"), None, None),
            P(("engine", "seq"), None, None),
            P(("engine", "seq")),
            P(("engine", "seq"), None),
            P("engine", "seq", None),
            P("engine", "seq", None),
        ),
        out_specs=P(("engine", "seq"), None, None),
        check_vma=False,
    )
```

```python
import functools
import math

import jax
import jax.numpy as jnp
from jax import lax
from jax.experimental import pallas as pl
from jax.experimental.pallas import tpu as pltpu
from jax.sharding import PartitionSpec as P

KVH = 4
GROUP = 8
HD = 128
CAPE = 3
SCALING = HD ** (-0.5)
LOG2E = math.log2(math.e)
LSE_ONE = float(2**20)
VMEM = pl.BlockSpec(memory_space=pltpu.VMEM)
SMEM = pl.BlockSpec(memory_space=pltpu.SMEM)


def params(mib):
    return pltpu.CompilerParams(vmem_limit_bytes=mib * 1024 * 1024)


def shape(dims, dtype):
    return jax.ShapeDtypeStruct(dims, dtype)


def prepare_kernel(prompt_ref, queries_ref, rows_ref, payload_ref):
    samples, steps, features = queries_ref.shape
    heads = features // HD
    part = heads * steps // KVH
    extra = payload_ref.shape[1] - samples * part
    lanes = lax.broadcasted_iota(jnp.int32, (extra, HD), 1)
    note = jnp.zeros((extra, HD), jnp.int32)
    for sample in range(samples):
        note = jnp.where(lanes == sample, prompt_ref[sample], note)
    note = note.astype(jnp.float32).astype(jnp.bfloat16)
    for sample in range(samples):
        for first in range(0, heads, 4):
            tile = jnp.concatenate(
                [
                    queries_ref[sample, :, (first + i) * HD : (first + i + 1) * HD].astype(jnp.float32)
                    for i in range(4)
                ],
                axis=0,
            ).astype(jnp.bfloat16)
            row = first * steps
            rows_ref[sample, row : row + 4 * steps] = tile
            group, row = row // part, row % part
            for place in range(group, payload_ref.shape[0], KVH):
                payload_ref[place, sample * part + row : sample * part + row + 4 * steps] = tile
    for place in range(payload_ref.shape[0]):
        payload_ref[place, samples * part :] = note


def split_kernel(head_ref, k_ref, v_ref, *refs):
    outs, held, sems = refs[:KVH], refs[KVH], refs[KVH + 1]
    copies = []
    for place, out in enumerate(outs):
        head = jnp.bitwise_xor(head_ref[0], place)
        cols = pl.ds(pl.multiple_of(head * HD, HD), HD)
        keys = pltpu.make_async_copy(k_ref.at[0, :, cols], out.at[0], sems.at[place, 0])
        values = pltpu.make_async_copy(v_ref.at[0, :, cols], held.at[place], sems.at[place, 1])
        copies.append((keys, values))
    for keys, values in copies:
        values.start()
    for keys, values in copies:
        keys.start()
    for place, out in enumerate(outs):
        copies[place][1].wait()
        for first in range(0, held.shape[1], HD):
            out[1, first : first + HD] = held[place, first : first + HD].T
    for keys, values in copies:
        keys.wait()


def pack_kernel(samples, _, received_ref, packed_ref, slots_ref, counts_ref):
    prompts, part = packed_ref.shape[0], packed_ref.shape[1] // CAPE
    packed_ref[...] = jnp.zeros(packed_ref.shape, packed_ref.dtype)
    for prompt in range(prompts):
        counts_ref[prompt] = 0
    for place in range(received_ref.shape[0]):
        note = received_ref[place, samples * part :].astype(jnp.float32).astype(jnp.int32)
        for sample in range(samples):
            prompt = note[0, sample]
            rank = counts_ref[prompt]
            counts_ref[prompt] = rank + 1
            slots_ref[place * samples + sample] = prompt * 4 + rank
            packed_ref[prompt, pl.ds(pl.multiple_of(rank * part, part), part)] = received_ref[
                place, sample * part : (sample + 1) * part
            ]


def block_scores(rows, keys):
    return lax.dot_general(keys, rows, (((1,), (1,)), ((), ())), preferred_element_type=jnp.float32)


def block_softmax(raw):
    top = jnp.max(raw, axis=0, keepdims=True)
    probs = jnp.exp2((raw - top) * (SCALING * LOG2E))
    total = jnp.sum(probs, axis=0, keepdims=True)
    return probs.astype(jnp.bfloat16), top * (SCALING * LOG2E), total


def block_product(probs, values):
    values = jnp.concatenate(
        [values[first : first + HD] for first in range(0, values.shape[0], HD)], axis=1
    )
    return jnp.dot(values, probs, preferred_element_type=jnp.float32)


def encode(out):
    largest = jnp.max(jnp.abs(out), axis=0, keepdims=True)
    power = jnp.floor(jnp.log2(jnp.maximum(largest, 2.0**-112) * 1.0001)) + 1.0
    code = jnp.round(out * jnp.exp2(15.0 - power))
    return code.astype(jnp.int32), power.astype(jnp.int32)


def prefix_kernel(chunk, q_ref, *refs):
    blocks, reply_ref = refs[:-1], refs[-1]
    slots, per = q_ref.shape[0], q_ref.shape[1]
    rows_of = per // 2
    wide = chunk * rows_of

    def rows_from(start):
        return jnp.concatenate(
            [
                q_ref[start : start + chunk, 0:rows_of].reshape(wide, HD),
                q_ref[start : start + chunk, rows_of:per].reshape(wide, HD),
            ],
            axis=0,
        )

    def finish(start, parts):
        top = functools.reduce(jnp.maximum, [part[1] for part in parts])
        weights = [jnp.exp2(part[1] - top) for part in parts]
        total = functools.reduce(jnp.add, [w * part[2] for w, part in zip(weights, parts)])
        share = 1.0 / total
        out = functools.reduce(jnp.add, [(w * share) * part[0] for w, part in zip(weights, parts)])
        log = jnp.round((top + jnp.log2(total)) * LSE_ONE).astype(jnp.int32)
        code, power = encode(out)
        packed = jnp.bitwise_or(
            jnp.left_shift(code[:, :wide], 16), jnp.bitwise_and(code[:, wide:], 0xFFFF)
        ).T
        rest = jnp.zeros((1, HD - 2 * per), jnp.int32)
        for slot in range(chunk):
            dest, rank = (start + slot) // CAPE, (start + slot) % CAPE
            first = slot * rows_of
            for part in range(rows_of // 4):
                reply_ref[dest, rank * (rows_of // 4) + part] = packed[
                    first + part * 4 : first + part * 4 + 4
                ]
            pieces = [
                array[:, begin : begin + rows_of]
                for array in (log, power)
                for begin in (first, wide + first)
            ]
            reply_ref[dest, CAPE * (rows_of // 4), rank : rank + 1] = jnp.concatenate(
                pieces + [rest], axis=1
            )

    starts = range(0, slots, chunk)
    stages = [(start, place) for start in starts for place in range(len(blocks))]
    rows = {start: rows_from(start) for start in starts}
    raw, waiting, parts = block_scores(rows[0], blocks[0][0]), None, []

    def product():
        (start, place), (probs, top, total) = waiting
        parts.append((block_product(probs, blocks[place][1]), top, total))
        if place + 1 == len(blocks):
            finish(start, parts)
            parts.clear()

    for number, stage in enumerate(stages):
        ready = raw
        if number + 1 < len(stages):
            later, block = stages[number + 1]
            raw = block_scores(rows[later], blocks[block][0])
        if waiting is not None:
            product()
        waiting = (stage, block_softmax(ready))
    product()


def select_kernel(samples, slots_ref, reply_ref, chosen_ref):
    body = (chosen_ref.shape[1] - 1) // samples
    for sample in range(chosen_ref.shape[0] * samples):
        slot = slots_ref[sample]
        prompt, rank = lax.shift_right_logical(slot, 2), lax.bitwise_and(slot, 3)
        place, which = sample // samples, sample % samples
        chosen_ref[place, which * body : (which + 1) * body] = reply_ref[
            prompt, pl.ds(rank * body, body)
        ]
        chosen_ref[place, samples * body, which : which + 1] = reply_ref[
            prompt, CAPE * body, pl.ds(rank, 1)
        ]


def suffix_kernel(length_ref, rows_ref, fresh_k_ref, fresh_v_ref, k_ref, v_ref, out_ref, log_ref):
    samples, positions = k_ref.shape[0], k_ref.shape[1]
    fresh = 16

    def padded(array):
        rest = jnp.zeros((fresh - array.shape[0], HD), jnp.float32)
        return jnp.concatenate([array.astype(jnp.float32), rest], axis=0).astype(jnp.bfloat16)

    per = rows_ref.shape[1] // KVH
    steps = per // GROUP
    column = lax.broadcasted_iota(jnp.int32, (per, positions), 1)
    step = lax.rem(lax.broadcasted_iota(jnp.int32, (per, fresh), 0), steps)
    causal = lax.broadcasted_iota(jnp.int32, (per, fresh), 1) <= step
    for sample in range(samples):
        live = column < length_ref[sample]
        for group in range(KVH):
            cols = slice(group * HD, (group + 1) * HD)
            rows = rows_ref[sample, group * per : (group + 1) * per]
            dims = (((1,), (1,)), ((), ()))
            cache_raw = lax.dot_general(
                rows, k_ref[sample, :, cols], dims, preferred_element_type=jnp.float32
            )
            fresh_raw = lax.dot_general(
                rows, padded(fresh_k_ref[sample, :, cols]), dims, preferred_element_type=jnp.float32
            )
            cache_raw = jnp.where(live, cache_raw, -jnp.inf)
            fresh_raw = jnp.where(causal, fresh_raw, -jnp.inf)
            top = jnp.maximum(
                jnp.max(cache_raw, axis=1, keepdims=True), jnp.max(fresh_raw, axis=1, keepdims=True)
            )
            cache_probs = jnp.exp2((cache_raw - top) * (SCALING * LOG2E))
            fresh_probs = jnp.exp2((fresh_raw - top) * (SCALING * LOG2E))
            total = jnp.sum(cache_probs, axis=1, keepdims=True) + jnp.sum(
                fresh_probs, axis=1, keepdims=True
            )
            acc = jnp.dot(
                cache_probs.astype(jnp.bfloat16),
                v_ref[sample, :, cols],
                preferred_element_type=jnp.float32,
            ) + jnp.dot(
                fresh_probs.astype(jnp.bfloat16),
                padded(fresh_v_ref[sample, :, cols]),
                preferred_element_type=jnp.float32,
            )
            here = slice(group * per, (group + 1) * per)
            out_ref[sample, here] = acc / total
            log_ref[sample, here] = jnp.broadcast_to(
                top * (SCALING * LOG2E) + jnp.log2(total), (per, HD)
            )


def combine_kernel(chosen_ref, suffix_out_ref, suffix_log_ref, out_ref):
    places, samples = chosen_ref.shape[0], suffix_out_ref.shape[0]
    steps = out_ref.shape[1]
    body = (chosen_ref.shape[1] - 1) // samples
    per = 8 * body
    row = lax.broadcasted_iota(jnp.int32, (per, HD), 0)
    lane = lax.broadcasted_iota(jnp.int32, (per, HD), 1)

    def turn(note, offset):
        spread = jnp.broadcast_to(note, (per, HD))
        return jnp.sum(jnp.where(lane == row + offset, spread, 0.0), axis=1, keepdims=True)

    for sample in range(samples):
        for group in range(KVH):
            logs, scales, codes = [], [], []
            for place in range(group, places, KVH):
                packed = jnp.concatenate(
                    [chosen_ref[place, sample * body + part] for part in range(body)], axis=0
                )
                high = jnp.right_shift(packed, 16)
                low = jnp.right_shift(jnp.left_shift(packed, 16), 16)
                codes.append(jnp.concatenate([high, low], axis=0).astype(jnp.float32))
                note = chosen_ref[place, samples * body, sample : sample + 1].astype(jnp.float32)
                logs.append(turn(note, 0) * (1.0 / LSE_ONE))
                scales.append(jnp.exp2(turn(note, per) - 15.0))
            peak = functools.reduce(jnp.maximum, logs)
            weights = [jnp.exp2(log - peak) for log in logs]
            weight_sum = functools.reduce(jnp.add, weights)
            prefix = functools.reduce(
                jnp.add, [(w * s) * c for w, s, c in zip(weights, scales, codes)]
            )
            prefix_log = peak + jnp.log2(weight_sum)
            first = group * per
            suffix_log = suffix_log_ref[sample, first : first + per][:, 0:1]
            suffix = suffix_out_ref[sample, first : first + per]
            top = jnp.maximum(prefix_log, suffix_log)
            prefix_weight = jnp.exp2(prefix_log - top)
            suffix_weight = jnp.exp2(suffix_log - top)
            whole = prefix_weight + suffix_weight
            result = (prefix_weight / (weight_sum * whole)) * prefix + (
                suffix_weight / whole
            ) * suffix
            for i in range(per // steps):
                head = first // steps + i
                out_ref[sample, :, head * HD : (head + 1) * HD] = result[
                    i * steps : (i + 1) * steps
                ].astype(jnp.bfloat16)


def local(
    queries,
    new_keys,
    new_values,
    suffix_keys,
    suffix_values,
    suffix_len,
    sample_prompt,
    prefix_keys,
    prefix_values,
):
    samples, steps, features = queries.shape
    heads = features // HD
    per = GROUP * steps
    seq_count = lax.axis_size("seq")
    engine_count = lax.axis_size("engine")
    positions = prefix_keys.shape[1]

    head_id = lax.rem(lax.axis_index("seq"), KVH).reshape(1)
    heads_of_block = pl.pallas_call(
        split_kernel,
        out_shape=[shape((2, positions, HD), jnp.bfloat16)] * KVH,
        in_specs=[SMEM] + [pl.BlockSpec(memory_space=pltpu.HBM)] * 2,
        out_specs=[VMEM] * KVH,
        scratch_shapes=[
            pltpu.VMEM((KVH, positions, HD), jnp.bfloat16),
            pltpu.SemaphoreType.DMA((KVH, 2)),
        ],
        compiler_params=params(16),
        name="split",
    )(
        head_id,
        pltpu.with_memory_space_constraint(prefix_keys, pltpu.HBM),
        pltpu.with_memory_space_constraint(prefix_values, pltpu.HBM),
    )

    def swap(array, near, swapped):
        pairs = []
        for place in range(seq_count):
            chip, core = place // 2, place % 2
            chip = (chip + near * (2 * core - 1)) % (seq_count // 2)
            pairs.append((place, 2 * chip + (1 - core if swapped else core)))
        return lax.ppermute(array, "seq", pairs)

    blocks = [
        heads_of_block[0],
        swap(heads_of_block[1], 0, True),
        swap(heads_of_block[2], 1, False),
        swap(heads_of_block[3], 1, True),
    ]

    rows, payload = pl.pallas_call(
        prepare_kernel,
        out_shape=(
            shape((samples, heads * steps, HD), jnp.bfloat16),
            shape((seq_count, samples * per + 8, HD), jnp.bfloat16),
        ),
        in_specs=[SMEM, VMEM],
        out_specs=(VMEM, VMEM),
        name="prepare",
    )(sample_prompt.reshape(samples), queries)
    received = lax.all_to_all(payload, "seq", split_axis=0, concat_axis=0, tiled=True)

    suffix_out, suffix_log = pl.pallas_call(
        suffix_kernel,
        out_shape=(
            shape((samples, heads * steps, HD), jnp.float32),
            shape((samples, heads * steps, HD), jnp.float32),
        ),
        in_specs=[SMEM] + [VMEM] * 5,
        out_specs=(VMEM, VMEM),
        compiler_params=params(16),
        name="suffix",
    )(
        suffix_len,
        rows,
        new_keys,
        new_values,
        suffix_keys,
        suffix_values,
    )

    suffix_out, suffix_log = pl.pallas_call(
        suffix_kernel,
        out_shape=(
            shape((samples, heads * steps, HD), jnp.float32),
            shape((samples, heads * steps, HD), jnp.float32),
        ),
        in_specs=[SMEM] + [VMEM] * 5,
        out_specs=(VMEM, VMEM),
        compiler_params=params(16),
        name="suffix",
    )(
        suffix_len,
        rows,
        new_keys,
        new_values,
        suffix_keys,
        suffix_values,
    )

    packed, slots = pl.pallas_call(
        functools.partial(pack_kernel, samples),
        out_shape=(
            pltpu.HBM((engine_count, CAPE * per, HD), jnp.bfloat16),
            shape((seq_count * samples,), jnp.int32),
        ),
        in_specs=[pl.BlockSpec(memory_space=pl.ANY), VMEM],
        out_specs=(VMEM, SMEM),
        scratch_shapes=[pltpu.SMEM((engine_count,), jnp.int32)],
        compiler_params=params(16),
        name="pack",
    )(suffix_log, received)
    dispatched = lax.all_to_all(packed, "engine", split_axis=0, concat_axis=0, tiled=True)

    reply = pl.pallas_call(
        functools.partial(prefix_kernel, 8 * CAPE),
        out_shape=shape((engine_count, CAPE * per // 8 + 1, 4, HD), jnp.int32),
        in_specs=[VMEM] * (1 + KVH),
        out_specs=VMEM,
        compiler_params=params(16),
        name="prefix",
    )(
        dispatched.reshape(engine_count * CAPE, per, HD),
        *[pltpu.with_memory_space_constraint(block, pltpu.VMEM) for block in blocks],
    )
    returned = lax.all_to_all(reply, "engine", split_axis=0, concat_axis=0, tiled=True)

    chosen = pl.pallas_call(
        functools.partial(select_kernel, samples),
        out_shape=shape((seq_count, samples * per // 8 + 1, 4, HD), jnp.int32),
        in_specs=[SMEM, VMEM],
        out_specs=VMEM,
        compiler_params=params(16),
        name="select",
    )(slots, returned)
    gathered = lax.all_to_all(chosen, "seq", split_axis=0, concat_axis=0, tiled=True)

    return pl.pallas_call(
        combine_kernel,
        out_shape=shape((samples, steps, features), jnp.bfloat16),
        in_specs=[VMEM] * 3,
        out_specs=VMEM,
        compiler_params=params(16),
        name="combine",
    )(gathered, suffix_out, suffix_log)


def solution(mesh):
    return jax.shard_map(
        local,
        mesh=mesh,
        in_specs=(
            P(("engine", "seq"), None, None),
            P(("engine", "seq"), None, None),
            P(("engine", "seq"), None, None),
            P(("engine", "seq"), None, None),
            P(("engine", "seq"), None, None),
            P(("engine", "seq")),
            P(("engine", "seq"), None),
            P("engine", "seq", None),
            P("engine", "seq", None),
        ),
        out_specs=P(("engine", "seq"), None, None),
        check_vma=False,
    )
```

```python
import functools
import math

import jax
import jax.numpy as jnp
from jax import lax
from jax.experimental import pallas as pl
from jax.experimental.pallas import tpu as pltpu
from jax.sharding import PartitionSpec as P

KVH = 4
GROUP = 8
HD = 128
CAPE = 3
SCALING = HD ** (-0.5)
LOG2E = math.log2(math.e)
LSE_ONE = float(2**20)
VMEM = pl.BlockSpec(memory_space=pltpu.VMEM)
SMEM = pl.BlockSpec(memory_space=pltpu.SMEM)


def params(mib):
    return pltpu.CompilerParams(vmem_limit_bytes=mib * 1024 * 1024)


def shape(dims, dtype):
    return jax.ShapeDtypeStruct(dims, dtype)


def prepare_kernel(prompt_ref, queries_ref, rows_ref, payload_ref):
    samples, steps, features = queries_ref.shape
    heads = features // HD
    part = heads * steps // KVH
    extra = payload_ref.shape[1] - samples * part
    lanes = lax.broadcasted_iota(jnp.int32, (extra, HD), 1)
    note = jnp.zeros((extra, HD), jnp.int32)
    for sample in range(samples):
        note = jnp.where(lanes == sample, prompt_ref[sample], note)
    note = note.astype(jnp.float32).astype(jnp.bfloat16)
    for sample in range(samples):
        for first in range(0, heads, 4):
            tile = jnp.concatenate(
                [
                    queries_ref[sample, :, (first + i) * HD : (first + i + 1) * HD].astype(jnp.float32)
                    for i in range(4)
                ],
                axis=0,
            ).astype(jnp.bfloat16)
            row = first * steps
            rows_ref[sample, row : row + 4 * steps] = tile
            group, row = row // part, row % part
            for place in range(group, payload_ref.shape[0], KVH):
                payload_ref[place, sample * part + row : sample * part + row + 4 * steps] = tile
    for place in range(payload_ref.shape[0]):
        payload_ref[place, samples * part :] = note


def split_kernel(head_ref, k_ref, v_ref, *refs):
    outs, held, sems = refs[:KVH], refs[KVH], refs[KVH + 1]
    copies = []
    for place, out in enumerate(outs):
        head = jnp.bitwise_xor(head_ref[0], place)
        cols = pl.ds(pl.multiple_of(head * HD, HD), HD)
        keys = pltpu.make_async_copy(k_ref.at[0, :, cols], out.at[0], sems.at[place, 0])
        values = pltpu.make_async_copy(v_ref.at[0, :, cols], held.at[place], sems.at[place, 1])
        copies.append((keys, values))
    for keys, values in copies:
        values.start()
    for keys, values in copies:
        keys.start()
    for place, out in enumerate(outs):
        copies[place][1].wait()
        for first in range(0, held.shape[1], HD):
            out[1, first : first + HD] = held[place, first : first + HD].T
    for keys, values in copies:
        keys.wait()


def pack_kernel(samples, _, received_ref, packed_ref, slots_ref, counts_ref):
    prompts, part = packed_ref.shape[0], packed_ref.shape[1] // CAPE
    packed_ref[...] = jnp.zeros(packed_ref.shape, packed_ref.dtype)
    for prompt in range(prompts):
        counts_ref[prompt] = 0
    for place in range(received_ref.shape[0]):
        note = received_ref[place, samples * part :].astype(jnp.float32).astype(jnp.int32)
        for sample in range(samples):
            prompt = note[0, sample]
            rank = counts_ref[prompt]
            counts_ref[prompt] = rank + 1
            slots_ref[place * samples + sample] = prompt * 4 + rank
            packed_ref[prompt, pl.ds(pl.multiple_of(rank * part, part), part)] = received_ref[
                place, sample * part : (sample + 1) * part
            ]


def block_scores(rows, keys):
    return lax.dot_general(keys, rows, (((1,), (1,)), ((), ())), preferred_element_type=jnp.float32)


def block_softmax(raw):
    top = jnp.max(raw, axis=0, keepdims=True)
    probs = jnp.exp2((raw - top) * (SCALING * LOG2E))
    total = jnp.sum(probs, axis=0, keepdims=True)
    return probs.astype(jnp.bfloat16), top * (SCALING * LOG2E), total


def block_product(probs, values):
    values = jnp.concatenate(
        [values[first : first + HD] for first in range(0, values.shape[0], HD)], axis=1
    )
    return jnp.dot(values, probs, preferred_element_type=jnp.float32)


def encode(out):
    largest = jnp.max(jnp.abs(out), axis=0, keepdims=True)
    power = jnp.floor(jnp.log2(jnp.maximum(largest, 2.0**-112) * 1.0001)) + 1.0
    code = jnp.clip(jnp.round(out * jnp.exp2(15.0 - power)), -32767.0, 32767.0)
    return code.astype(jnp.int32), power.astype(jnp.int32)


def prefix_kernel(chunk, q_ref, *refs):
    blocks, reply_ref = refs[:-1], refs[-1]
    slots, per = q_ref.shape[0], q_ref.shape[1]
    rows_of = per // 2
    wide = chunk * rows_of

    def rows_from(start):
        return jnp.concatenate(
            [
                q_ref[start : start + chunk, 0:rows_of].reshape(wide, HD),
                q_ref[start : start + chunk, rows_of:per].reshape(wide, HD),
            ],
            axis=0,
        )

    def finish(start, parts):
        top = functools.reduce(jnp.maximum, [part[1] for part in parts])
        weights = [jnp.exp2(part[1] - top) for part in parts]
        total = functools.reduce(jnp.add, [w * part[2] for w, part in zip(weights, parts)])
        share = 1.0 / total
        out = functools.reduce(jnp.add, [(w * share) * part[0] for w, part in zip(weights, parts)])
        log = jnp.round((top + jnp.log2(total)) * LSE_ONE).astype(jnp.int32)
        code, power = encode(out)
        packed = jnp.bitwise_or(
            jnp.left_shift(code[:, :wide], 16), jnp.bitwise_and(code[:, wide:], 0xFFFF)
        ).T
        rest = jnp.zeros((1, HD - 2 * per), jnp.int32)
        for slot in range(chunk):
            dest, rank = (start + slot) // CAPE, (start + slot) % CAPE
            first = slot * rows_of
            for part in range(rows_of // 4):
                reply_ref[dest, rank * (rows_of // 4) + part] = packed[
                    first + part * 4 : first + part * 4 + 4
                ]
            pieces = [
                array[:, begin : begin + rows_of]
                for array in (log, power)
                for begin in (first, wide + first)
            ]
            reply_ref[dest, CAPE * (rows_of // 4), rank : rank + 1] = jnp.concatenate(
                pieces + [rest], axis=1
            )

    starts = range(0, slots, chunk)
    stages = [(start, place) for start in starts for place in range(len(blocks))]
    rows = {start: rows_from(start) for start in starts}
    scored = lambda stage: block_scores(rows[stage[0]], blocks[stage[1]][0])
    raws, waiting, parts = [scored(stage) for stage in stages[:2]], None, []

    def product():
        (start, place), (probs, top, total) = waiting
        parts.append((block_product(probs, blocks[place][1]), top, total))
        if place + 1 == len(blocks):
            finish(start, parts)
            parts.clear()

    for number, stage in enumerate(stages):
        ready = raws.pop(0)
        if number + 2 < len(stages):
            raws.append(scored(stages[number + 2]))
        if waiting is not None:
            product()
        waiting = (stage, block_softmax(ready))
    product()


def select_kernel(samples, slots_ref, reply_ref, chosen_ref):
    body = (chosen_ref.shape[1] - 1) // samples
    for sample in range(chosen_ref.shape[0] * samples):
        slot = slots_ref[sample]
        prompt, rank = lax.shift_right_logical(slot, 2), lax.bitwise_and(slot, 3)
        place, which = sample // samples, sample % samples
        chosen_ref[place, which * body : (which + 1) * body] = reply_ref[
            prompt, pl.ds(rank * body, body)
        ]
        chosen_ref[place, samples * body, which : which + 1] = reply_ref[
            prompt, CAPE * body, pl.ds(rank, 1)
        ]


def suffix_kernel(length_ref, rows_ref, fresh_k_ref, fresh_v_ref, k_ref, v_ref, out_ref, log_ref):
    samples, positions = k_ref.shape[0], k_ref.shape[1]
    fresh = 16

    def padded(array):
        rest = jnp.zeros((fresh - array.shape[0], HD), jnp.float32)
        return jnp.concatenate([array.astype(jnp.float32), rest], axis=0).astype(jnp.bfloat16)

    per = rows_ref.shape[1] // KVH
    steps = per // GROUP
    column = lax.broadcasted_iota(jnp.int32, (per, positions), 1)
    step = lax.rem(lax.broadcasted_iota(jnp.int32, (per, fresh), 0), steps)
    causal = lax.broadcasted_iota(jnp.int32, (per, fresh), 1) <= step
    for sample in range(samples):
        live = column < length_ref[sample]
        for group in range(KVH):
            cols = slice(group * HD, (group + 1) * HD)
            rows = rows_ref[sample, group * per : (group + 1) * per]
            dims = (((1,), (1,)), ((), ()))
            cache_raw = lax.dot_general(
                rows, k_ref[sample, :, cols], dims, preferred_element_type=jnp.float32
            )
            fresh_raw = lax.dot_general(
                rows, padded(fresh_k_ref[sample, :, cols]), dims, preferred_element_type=jnp.float32
            )
            cache_raw = jnp.where(live, cache_raw, -jnp.inf)
            fresh_raw = jnp.where(causal, fresh_raw, -jnp.inf)
            top = jnp.maximum(
                jnp.max(cache_raw, axis=1, keepdims=True), jnp.max(fresh_raw, axis=1, keepdims=True)
            )
            cache_probs = jnp.exp2((cache_raw - top) * (SCALING * LOG2E))
            fresh_probs = jnp.exp2((fresh_raw - top) * (SCALING * LOG2E))
            total = jnp.sum(cache_probs, axis=1, keepdims=True) + jnp.sum(
                fresh_probs, axis=1, keepdims=True
            )
            acc = jnp.dot(
                cache_probs.astype(jnp.bfloat16),
                v_ref[sample, :, cols],
                preferred_element_type=jnp.float32,
            ) + jnp.dot(
                fresh_probs.astype(jnp.bfloat16),
                padded(fresh_v_ref[sample, :, cols]),
                preferred_element_type=jnp.float32,
            )
            here = slice(group * per, (group + 1) * per)
            out_ref[sample, here] = acc / total
            log_ref[sample, here] = jnp.broadcast_to(
                top * (SCALING * LOG2E) + jnp.log2(total), (per, HD)
            )


def combine_kernel(chosen_ref, suffix_out_ref, suffix_log_ref, out_ref):
    places, samples = chosen_ref.shape[0], suffix_out_ref.shape[0]
    steps = out_ref.shape[1]
    body = (chosen_ref.shape[1] - 1) // samples
    per = 8 * body
    row = lax.broadcasted_iota(jnp.int32, (per, HD), 0)
    lane = lax.broadcasted_iota(jnp.int32, (per, HD), 1)

    def turn(note, offset):
        spread = jnp.broadcast_to(note, (per, HD))
        return jnp.sum(jnp.where(lane == row + offset, spread, 0.0), axis=1, keepdims=True)

    for sample in range(samples):
        for group in range(KVH):
            logs, scales, codes = [], [], []
            for place in range(group, places, KVH):
                packed = jnp.concatenate(
                    [chosen_ref[place, sample * body + part] for part in range(body)], axis=0
                )
                high = jnp.right_shift(packed, 16)
                low = jnp.right_shift(jnp.left_shift(packed, 16), 16)
                codes.append(jnp.concatenate([high, low], axis=0).astype(jnp.float32))
                note = chosen_ref[place, samples * body, sample : sample + 1].astype(jnp.float32)
                logs.append(turn(note, 0) * (1.0 / LSE_ONE))
                scales.append(jnp.exp2(turn(note, per) - 15.0))
            peak = functools.reduce(jnp.maximum, logs)
            weights = [jnp.exp2(log - peak) for log in logs]
            weight_sum = functools.reduce(jnp.add, weights)
            prefix = functools.reduce(
                jnp.add, [(w * s) * c for w, s, c in zip(weights, scales, codes)]
            )
            prefix_log = peak + jnp.log2(weight_sum)
            first = group * per
            suffix_log = suffix_log_ref[sample, first : first + per][:, 0:1]
            suffix = suffix_out_ref[sample, first : first + per]
            top = jnp.maximum(prefix_log, suffix_log)
            prefix_weight = jnp.exp2(prefix_log - top)
            suffix_weight = jnp.exp2(suffix_log - top)
            whole = prefix_weight + suffix_weight
            result = (prefix_weight / (weight_sum * whole)) * prefix + (
                suffix_weight / whole
            ) * suffix
            for i in range(per // steps):
                head = first // steps + i
                out_ref[sample, :, head * HD : (head + 1) * HD] = result[
                    i * steps : (i + 1) * steps
                ].astype(jnp.bfloat16)


def local(
    queries,
    new_keys,
    new_values,
    suffix_keys,
    suffix_values,
    suffix_len,
    sample_prompt,
    prefix_keys,
    prefix_values,
):
    samples, steps, features = queries.shape
    heads = features // HD
    per = GROUP * steps
    seq_count = lax.axis_size("seq")
    engine_count = lax.axis_size("engine")
    positions = prefix_keys.shape[1]

    head_id = lax.rem(lax.axis_index("seq"), KVH).reshape(1)
    heads_of_block = pl.pallas_call(
        split_kernel,
        out_shape=[shape((2, positions, HD), jnp.bfloat16)] * KVH,
        in_specs=[SMEM] + [pl.BlockSpec(memory_space=pltpu.HBM)] * 2,
        out_specs=[VMEM] * KVH,
        scratch_shapes=[
            pltpu.VMEM((KVH, positions, HD), jnp.bfloat16),
            pltpu.SemaphoreType.DMA((KVH, 2)),
        ],
        compiler_params=params(16),
        name="split",
    )(
        head_id,
        pltpu.with_memory_space_constraint(prefix_keys, pltpu.HBM),
        pltpu.with_memory_space_constraint(prefix_values, pltpu.HBM),
    )

    def swap(array, near, swapped):
        pairs = []
        for place in range(seq_count):
            chip, core = place // 2, place % 2
            chip = (chip + near * (2 * core - 1)) % (seq_count // 2)
            pairs.append((place, 2 * chip + (1 - core if swapped else core)))
        return lax.ppermute(array, "seq", pairs)

    blocks = [
        heads_of_block[0],
        swap(heads_of_block[1], 0, True),
        swap(heads_of_block[2], 1, False),
        swap(heads_of_block[3], 1, True),
    ]

    rows, payload = pl.pallas_call(
        prepare_kernel,
        out_shape=(
            shape((samples, heads * steps, HD), jnp.bfloat16),
            shape((seq_count, samples * per + 8, HD), jnp.bfloat16),
        ),
        in_specs=[SMEM, VMEM],
        out_specs=(VMEM, VMEM),
        name="prepare",
    )(sample_prompt.reshape(samples), queries)
    received = lax.all_to_all(payload, "seq", split_axis=0, concat_axis=0, tiled=True)

    suffix_out, suffix_log = pl.pallas_call(
        suffix_kernel,
        out_shape=(
            shape((samples, heads * steps, HD), jnp.float32),
            shape((samples, heads * steps, HD), jnp.float32),
        ),
        in_specs=[SMEM] + [VMEM] * 5,
        out_specs=(VMEM, VMEM),
        compiler_params=params(16),
        name="suffix",
    )(
        suffix_len,
        rows,
        new_keys,
        new_values,
        suffix_keys,
        suffix_values,
    )

    suffix_out, suffix_log = pl.pallas_call(
        suffix_kernel,
        out_shape=(
            shape((samples, heads * steps, HD), jnp.float32),
            shape((samples, heads * steps, HD), jnp.float32),
        ),
        in_specs=[SMEM] + [VMEM] * 5,
        out_specs=(VMEM, VMEM),
        compiler_params=params(16),
        name="suffix",
    )(
        suffix_len,
        rows,
        new_keys,
        new_values,
        suffix_keys,
        suffix_values,
    )

    packed, slots = pl.pallas_call(
        functools.partial(pack_kernel, samples),
        out_shape=(
            pltpu.HBM((engine_count, CAPE * per, HD), jnp.bfloat16),
            shape((seq_count * samples,), jnp.int32),
        ),
        in_specs=[pl.BlockSpec(memory_space=pl.ANY), VMEM],
        out_specs=(VMEM, SMEM),
        scratch_shapes=[pltpu.SMEM((engine_count,), jnp.int32)],
        compiler_params=params(16),
        name="pack",
    )(suffix_log, received)
    dispatched = lax.all_to_all(packed, "engine", split_axis=0, concat_axis=0, tiled=True)

    reply = pl.pallas_call(
        functools.partial(prefix_kernel, 16),
        out_shape=shape((engine_count, CAPE * per // 8 + 1, 4, HD), jnp.int32),
        in_specs=[VMEM] * (1 + KVH),
        out_specs=VMEM,
        compiler_params=params(16),
        name="prefix",
    )(
        dispatched.reshape(engine_count * CAPE, per, HD),
        *[pltpu.with_memory_space_constraint(block, pltpu.VMEM) for block in blocks],
    )
    returned = lax.all_to_all(reply, "engine", split_axis=0, concat_axis=0, tiled=True)

    chosen = pl.pallas_call(
        functools.partial(select_kernel, samples),
        out_shape=shape((seq_count, samples * per // 8 + 1, 4, HD), jnp.int32),
        in_specs=[SMEM, VMEM],
        out_specs=VMEM,
        compiler_params=params(16),
        name="select",
    )(slots, returned)
    gathered = lax.all_to_all(chosen, "seq", split_axis=0, concat_axis=0, tiled=True)

    return pl.pallas_call(
        combine_kernel,
        out_shape=shape((samples, steps, features), jnp.bfloat16),
        in_specs=[VMEM] * 3,
        out_specs=VMEM,
        compiler_params=params(16),
        name="combine",
    )(gathered, suffix_out, suffix_log)


def solution(mesh):
    return jax.shard_map(
        local,
        mesh=mesh,
        in_specs=(
            P(("engine", "seq"), None, None),
            P(("engine", "seq"), None, None),
            P(("engine", "seq"), None, None),
            P(("engine", "seq"), None, None),
            P(("engine", "seq"), None, None),
            P(("engine", "seq")),
            P(("engine", "seq"), None),
            P("engine", "seq", None),
            P("engine", "seq", None),
        ),
        out_specs=P(("engine", "seq"), None, None),
        check_vma=False,
    )
```
